32 devices in a mesh: dp: 8 (over y, x, core), mp: 4 (over z).
Axes of the slice: x: 2, y: 2, z: 4, core: 2. Of those that a mesh axis runs over, the one named last changes fastest.
Arguments:
- inputs: bfloat16 [10240, 768], P(('dp', 'mp')), may hold values from -6 to 6
- lengths: int32 [16], P('dp'), may hold values from 50 to 577, as said below
- cotangent: bfloat16 [10240, 768], P(('dp', 'mp')), may hold values from -12 to 12
- student_gains: float32 [2, 768], replicated, may hold values from 0.1 to 1.9
- student_shifts: float32 [2, 768], replicated, may hold values from -3 to 3
- student_project_in: bfloat16 [3, 768, 768], P(None, None, 'mp'), may hold values from -0.21875 to 0.21875
- student_project_bias: float32 [2, 768], P(None, 'mp'), may hold values from -3 to 3
- student_project_out: bfloat16 [768, 768], P('mp'), may hold values from -0.875 to 0.875
- student_out_bias: float32 [2, 768], replicated, may hold values from -3 to 3
- student_scales: float32 [2, 768], replicated, may hold values from 0.1 to 1.9
- student_up_weight: bfloat16 [768, 3072], P(None, 'mp'), may hold values from -0.21875 to 0.21875
- student_up_bias: float32 [3072], P('mp'), may hold values from -3 to 3
- student_down_weight: bfloat16 [3072, 768], P('mp'), may hold values from -0.109375 to 0.109375
- teacher_gains: float32 [2, 768], replicated, may hold values from 0.1 to 1.9
- teacher_shifts: float32 [2, 768], replicated, may hold values from -3 to 3
- teacher_project_in: bfloat16 [3, 768, 768], P(None, None, 'mp'), may hold values from -0.21875 to 0.21875
- teacher_project_bias: float32 [2, 768], P(None, 'mp'), may hold values from -3 to 3
- teacher_project_out: bfloat16 [768, 768], P('mp'), may hold values from -0.875 to 0.875
- teacher_out_bias: float32 [2, 768], replicated, may hold values from -3 to 3
- teacher_scales: float32 [2, 768], replicated, may hold values from 0.1 to 1.9
- teacher_up_weight: bfloat16 [768, 3072], P(None, 'mp'), may hold values from -0.21875 to 0.21875
- teacher_up_bias: float32 [3072], P('mp'), may hold values from -3 to 3
- teacher_down_weight: bfloat16 [3072, 768], P('mp'), may hold values from -0.109375 to 0.109375
Outputs:
- output: bfloat16 [10240, 768], P(('dp', 'mp'))
- input_grad: bfloat16 [10240, 768], P(('dp', 'mp'))
- student_gains_grad: float32 [2, 768], replicated
- student_shifts_grad: float32 [2, 768], replicated
- student_project_in_grad: float32 [3, 768, 768], P(None, None, 'mp')
- student_project_bias_grad: float32 [2, 768], P(None, 'mp')
- student_project_out_grad: float32 [768, 768], P('mp')
- student_out_bias_grad: float32 [2, 768], replicated
- student_scales_grad: float32 [2, 768], replicated
- student_up_weight_grad: float32 [768, 3072], P(None, 'mp')
- student_up_bias_grad: float32 [3072], P('mp')
- student_down_weight_grad: float32 [3072, 768], P('mp')
- teacher_gains_grad: float32 [2, 768], replicated
- teacher_shifts_grad: float32 [2, 768], replicated
- teacher_project_in_grad: float32 [3, 768, 768], P(None, None, 'mp')
- teacher_project_bias_grad: float32 [2, 768], P(None, 'mp')
- teacher_project_out_grad: float32 [768, 768], P('mp')
- teacher_out_bias_grad: float32 [2, 768], replicated
- teacher_scales_grad: float32 [2, 768], replicated
- teacher_up_weight_grad: float32 [768, 3072], P(None, 'mp')
- teacher_up_bias_grad: float32 [3072], P('mp')
- teacher_down_weight_grad: float32 [3072, 768], P('mp')
The draws below stay inside these ranges and needn't reach their ends.
Inputs may be any that keep to these rules, and one draw needn't show every extreme that they name: `lengths`: in each aligned run of 2 images one image has exactly 577 rows.
All inputs are finite; a program needn't handle non-finite values.
Results may differ from the reference program's by a relative error of at most 0.03.
Values may be sent and summed in bfloat16 or wider, within the bound.
A program may use at most 128 MiB of HBM per device.

```python
import jax
import jax.numpy as jnp
from jax import lax

D = 768
HEADS = 12
FF = 3072
HEAD_DIM = 64
SLOT = 640
MAXLEN = 577
MINLEN = 50
IMG_GROUP = 2
IMAGES = 16
TOKENS = 10240


def draw_lengths(key, part):
    key = jax.random.fold_in(key, 3)
    key_steps, key_pick = jax.random.split(key)
    step_draw = jax.random.randint(key_steps, (IMAGES,), 0, 24)
    lengths = MINLEN + (MAXLEN - MINLEN) * step_draw * (step_draw + 92) // 2645
    chosen_slot = jax.random.randint(key_pick, (IMAGES // IMG_GROUP, 1), 0, IMG_GROUP)
    longest = (jnp.arange(IMG_GROUP)[None, :] == chosen_slot).reshape(IMAGES)
    return jnp.where(longest, MAXLEN, lengths).astype(jnp.int32)


def draw_cotangent(key, part):
    key = jax.random.fold_in(key, 7)
    rising = 1.0 + 2.0 * jnp.arange(TOKENS, dtype=jnp.float32)[:, None] / TOKENS
    noise = jnp.clip(jax.random.normal(key, (TOKENS, D), jnp.float32), -4.0, 4.0)
    return (rising * noise).astype(jnp.bfloat16)


def shard_levels(rng, shape, cuts, least, high):
    def one(position, parts):
        draws = jax.random.uniform(jax.random.fold_in(jax.random.fold_in(rng, 6), position), (parts,), jnp.float32, least / len(cuts), high / len(cuts))
        return jnp.repeat(jnp.exp(draws), shape[position] // parts).reshape((-1,) + (1,) * (len(shape) - position - 1))

    loudness = one(*cuts[0])
    for cut in cuts[1:]:
        loudness = loudness * one(*cut)
    return loudness


def gaussian(key, extent, width, limit, cuts=(), kind=jnp.bfloat16):
    level = shard_levels(key, extent, cuts, -0.22, 0.18) if cuts else 1.0
    drawn = jax.random.normal(key, extent, jnp.float32) * width * level
    return jnp.minimum(jnp.maximum(drawn, -limit), limit).astype(kind)


def setup_inputs(seed: int = 0) -> dict:
    key_of = jax.random.split(jax.random.key(seed), 24)
    return {
        "inputs": gaussian(key_of[0], (TOKENS, D), 1.0, 6.0, ((0, 32),)),
        "lengths": draw_lengths(jax.random.fold_in(key_of[23], 71), 0),
        "cotangent": draw_cotangent(jax.random.fold_in(key_of[23], 71), 0),
        "student_gains": jnp.clip(1.0 + 0.18 * jax.random.normal(key_of[3], (2, D), jnp.float32), 0.1, 1.9),
        "student_shifts": gaussian(key_of[4], (2, D), 0.5, 3.0, (), jnp.float32),
        "student_project_in": gaussian(key_of[5], (3, D, D), D ** -0.5, 0.21875, ((2, 4),)),
        "student_project_bias": gaussian(key_of[6], (2, D), 0.5, 3.0, ((1, 4),), jnp.float32),
        "student_project_out": gaussian(key_of[7], (D, D), (D // 16) ** -0.5, 0.875, ((0, 4),)),
        "student_out_bias": gaussian(key_of[8], (2, D), 0.5, 3.0, (), jnp.float32),
        "student_scales": jnp.clip(1.0 + 0.18 * jax.random.normal(key_of[9], (2, D), jnp.float32), 0.1, 1.9),
        "student_up_weight": gaussian(key_of[10], (D, FF), D ** -0.5, 0.21875, ((1, 4),)),
        "student_up_bias": gaussian(key_of[11], (FF,), 0.5, 3.0, ((0, 4),), jnp.float32),
        "student_down_weight": gaussian(key_of[12], (FF, D), FF ** -0.5, 0.109375, ((0, 4),)),
        "teacher_gains": jnp.clip(1.0 + 0.18 * jax.random.normal(key_of[13], (2, D), jnp.float32), 0.1, 1.9),
        "teacher_shifts": gaussian(key_of[14], (2, D), 0.5, 3.0, (), jnp.float32),
        "teacher_project_in": gaussian(key_of[15], (3, D, D), D ** -0.5, 0.21875, ((2, 4),)),
        "teacher_project_bias": gaussian(key_of[16], (2, D), 0.5, 3.0, ((1, 4),), jnp.float32),
        "teacher_project_out": gaussian(key_of[17], (D, D), (D // 16) ** -0.5, 0.875, ((0, 4),)),
        "teacher_out_bias": gaussian(key_of[18], (2, D), 0.5, 3.0, (), jnp.float32),
        "teacher_scales": jnp.clip(1.0 + 0.18 * jax.random.normal(key_of[19], (2, D), jnp.float32), 0.1, 1.9),
        "teacher_up_weight": gaussian(key_of[20], (D, FF), D ** -0.5, 0.21875, ((1, 4),)),
        "teacher_up_bias": gaussian(key_of[21], (FF,), 0.5, 3.0, ((0, 4),), jnp.float32),
        "teacher_down_weight": gaussian(key_of[22], (FF, D), FF ** -0.5, 0.109375, ((0, 4),)),
    }


epsilon = 1e-06

@jax.custom_vjp
def low(v):
    return lax.optimization_barrier(v.astype(jnp.bfloat16)).astype(jnp.float32)

@jax.custom_vjp
def low_back(v):
    return v

def low_keep(v):
    return (low(v), None)

def low_pass(kept, grad):
    return (grad,)

def back_keep(v):
    return (v, None)

def back_low(kept, grad):
    return (low(grad),)
low.defvjp(low_keep, low_pass)
low_back.defvjp(back_keep, back_low)

def layer_norm(values, norm_gain, norm_shift):
    center = values - lax.optimization_barrier(jnp.mean(values, axis=-1, keepdims=True))
    spread = lax.optimization_barrier(jnp.mean(center * center, axis=-1, keepdims=True))
    return center * lax.rsqrt(spread + epsilon) * norm_gain + norm_shift

def matmul(left_side, right_side):
    return jnp.dot(left_side, right_side, precision=lax.Precision.HIGHEST)

def attend_image(image_items):
    query_img, key_img, value_img, mask_row = image_items
    query_heads = query_img.reshape(SLOT, HEADS, HEAD_DIM)
    key_heads = key_img.reshape(SLOT, HEADS, HEAD_DIM)
    value_heads = value_img.reshape(SLOT, HEADS, HEAD_DIM)
    scores = jnp.einsum('qhd,khd->hqk', query_heads, key_heads, precision=lax.Precision.HIGHEST) * HEAD_DIM ** (-0.5)
    scores = low_back(scores)
    scores = jnp.where(mask_row[None, None, :], scores, -1e+30)
    row_peak = lax.optimization_barrier(jnp.max(scores, axis=-1, keepdims=True))
    exponent = jnp.exp(scores - row_peak)
    attn_probs = low(exponent / lax.optimization_barrier(jnp.sum(exponent, axis=-1, keepdims=True)))
    head_mixed = jnp.einsum('hqk,khd->qhd', attn_probs, value_heads, precision=lax.Precision.HIGHEST)
    return head_mixed.reshape(SLOT, D)

def block(resid, key_valid, norm_gains, shifts, project_in, project_bias, project_out, out_bias, scales, up_weight, up_bias, down_weight):
    image_count = key_valid.shape[0]
    normed = low(layer_norm(resid, norm_gains[0], shifts[0]))
    query_rows = low(low_back(matmul(normed, project_in[0]) + project_bias[0]))
    key_rows = low(low_back(matmul(normed, project_in[1])))
    value_rows = low(low_back(matmul(normed, project_in[2]) + project_bias[1]))
    head_mixed = lax.map(jax.checkpoint(attend_image), (query_rows.reshape(image_count, SLOT, D), key_rows.reshape(image_count, SLOT, D), value_rows.reshape(image_count, SLOT, D), key_valid))
    head_mixed = low(low_back(head_mixed.reshape(image_count * SLOT, D)))
    attn_out = low_back(matmul(head_mixed, project_out) + out_bias[0])
    middle = resid + scales[0] * attn_out
    normed_mlp = low(layer_norm(middle, norm_gains[1], shifts[1]))
    pre_act = low_back(matmul(normed_mlp, up_weight) + up_bias)
    hidden = low(jax.nn.gelu(pre_act, approximate=False))
    mlp_out = low_back(matmul(hidden, down_weight) + out_bias[1])
    return middle + scales[1] * mlp_out

def reference(inputs, lengths, cotangent, student_gains, student_shifts, student_project_in, student_project_bias, student_project_out, student_out_bias, student_scales, student_up_weight, student_up_bias, student_down_weight, teacher_gains, teacher_shifts, teacher_project_in, teacher_project_bias, teacher_project_out, teacher_out_bias, teacher_scales, teacher_up_weight, teacher_up_bias, teacher_down_weight):
    student = (student_gains.astype(jnp.float32), student_shifts.astype(jnp.float32), student_project_in.astype(jnp.float32), student_project_bias.astype(jnp.float32), student_project_out.astype(jnp.float32), student_out_bias.astype(jnp.float32), student_scales.astype(jnp.float32), student_up_weight.astype(jnp.float32), student_up_bias.astype(jnp.float32), student_down_weight.astype(jnp.float32))
    teacher = (teacher_gains.astype(jnp.float32), teacher_shifts.astype(jnp.float32), teacher_project_in.astype(jnp.float32), teacher_project_bias.astype(jnp.float32), teacher_project_out.astype(jnp.float32), teacher_out_bias.astype(jnp.float32), teacher_scales.astype(jnp.float32), teacher_up_weight.astype(jnp.float32), teacher_up_bias.astype(jnp.float32), teacher_down_weight.astype(jnp.float32))
    group_count = lengths.shape[0] // IMG_GROUP
    group_size = IMG_GROUP * SLOT

    def group_step(running, group_items):
        group_rows, group_lengths, group_grads = group_items
        key_valid = jnp.arange(SLOT)[None, :] < group_lengths[:, None]

        def network(rows_in, first_block, second_block):
            middle_rows = block(rows_in, key_valid, *first_block)
            return block(middle_rows, key_valid, *second_block)
        result, pullback = jax.vjp(network, group_rows, student, teacher)
        grad_rows, grad_student, grad_teacher = pullback(group_grads)
        running = jax.tree.map(jnp.add, running, (grad_student, grad_teacher))
        return (running, (result, grad_rows))
    initial = jax.tree.map(jnp.zeros_like, (student, teacher))
    sweep_items = (inputs.astype(jnp.float32).reshape(group_count, group_size, D), lengths.reshape(group_count, IMG_GROUP), cotangent.astype(jnp.float32).reshape(group_count, group_size, D))
    (grad_student, grad_teacher), (outputs, grad_inputs) = lax.scan(group_step, initial, sweep_items)
    return (outputs.reshape(-1, D).astype(jnp.bfloat16), grad_inputs.reshape(-1, D).astype(jnp.bfloat16), grad_student[0], grad_student[1], grad_student[2], grad_student[3], grad_student[4], grad_student[5], grad_student[6], grad_student[7], grad_student[8], grad_student[9], grad_teacher[0], grad_teacher[1], grad_teacher[2], grad_teacher[3], grad_teacher[4], grad_teacher[5], grad_teacher[6], grad_teacher[7], grad_teacher[8], grad_teacher[9])
```

```python
import functools

import jax
import jax.numpy as jnp
from jax import lax
from jax.experimental import pallas as pl
from jax.experimental.pallas import tpu as pltpu
from jax.sharding import PartitionSpec as P

HEAD_DIM = 64
SLOT = 640
PARTS = 8
BF = jnp.bfloat16
F32 = jnp.float32

epsilon = 1e-06


def layer_norm(values, norm_gain, norm_shift):
    center = values - jnp.mean(values, axis=-1, keepdims=True)
    spread = jnp.mean(center * center, axis=-1, keepdims=True)
    inverse = lax.rsqrt(spread + epsilon)
    unit = center * inverse
    return unit * norm_gain + norm_shift, unit, inverse


def layer_norm_back(grad, unit, inverse, norm_gain):
    scaled = grad * norm_gain
    return (
        inverse
        * (
            scaled
            - jnp.mean(scaled, axis=-1, keepdims=True)
            - unit * jnp.mean(scaled * unit, axis=-1, keepdims=True)
        ),
        jnp.sum(grad * unit, axis=0),
        jnp.sum(grad, axis=0),
    )


def gelu_exact(values):
    return jax.nn.gelu(values, approximate=False)


def matmul(left_side, right_side):
    return jnp.dot(left_side, right_side, preferred_element_type=F32)


def matmul_tn(left_side, right_side):
    return lax.dot_general(
        left_side, right_side, (((0,), (0,)), ((), ())), preferred_element_type=F32
    )


def matmul_nt(left_side, right_side):
    return lax.dot_general(
        left_side, right_side, (((1,), (1,)), ((), ())), preferred_element_type=F32
    )


def swap(source, axis, bit):
    count = lax.axis_size(axis)
    return lax.ppermute(source, axis, [(i, i ^ bit) for i in range(count)])


def low_index():
    return lax.rem(lax.axis_index("dp"), PARTS)


MESH = pl.DeviceIdType.MESH
ORDERS = ((2, 4), (4, 2), (2, 4), (4, 2), (2, 4), (4, 2))
COUNT = len(ORDERS)
AHEAD = 2


def flip(index, bits):
    bit = 1
    while bit <= bits:
        if bits & bit:
            index = index + bit - 2 * bit * lax.rem(lax.div(index, bit), 2)
        bit *= 2
    return index


def partners(dp_size):
    bits = []
    bit = 1
    while bit < dp_size:
        bits.append({"dp": bit})
        bit *= 2
    return bits + [{"mp": r} for r in (1, 2, 3)]


def device_at(bits):
    return {axis: flip(lax.axis_index(axis), bit) for axis, bit in bits.items()}


def enter(dp_size):
    barrier = pltpu.get_barrier_semaphore()
    for bits in partners(dp_size):
        pl.semaphore_signal(barrier, inc=1, device_id=device_at(bits), device_id_type=MESH)
    pl.semaphore_wait(barrier, len(partners(dp_size)))


def remote(source, target, send, recv, bits):
    return pltpu.make_async_remote_copy(
        src_ref=source,
        dst_ref=target,
        send_sem=send,
        recv_sem=recv,
        device_id=device_at(bits),
        device_id_type=MESH,
    )


def piece_rows(index, size):
    return pl.ds(pl.multiple_of(index * size, size), size)


def gather_kernel(dp_size, *refs):
    local = refs[:COUNT]
    full = refs[COUNT : 2 * COUNT]
    send, recv = refs[2 * COUNT :]
    size = local[0].shape[0] // PARTS
    me = lax.rem(lax.axis_index("dp"), PARTS)
    enter(dp_size)

    def rows(mask):
        return piece_rows(flip(me, mask), size)

    def slab(i, mask):
        return full[i].at[:, rows(mask)]

    def along_z(i):
        return [
            remote(
                local[i].at[rows(0)],
                full[i].at[r - 1, rows(0)],
                send.at[i, r - 1],
                recv.at[i, r - 1],
                {"mp": r},
            )
            for r in (1, 2, 3)
        ]

    def along_dp(i, slot, mask, bit):
        return remote(
            slab(i, mask), slab(i, mask), send.at[i, slot], recv.at[i, slot], {"dp": bit}
        )

    flying = []

    def launch(copies):
        for copy in copies:
            copy.start()
        flying.extend(copies)
        return copies

    def landed(copies):
        for copy in copies:
            copy.wait_recv()

    state = [None] * COUNT

    def stage(i, s):
        first, second = ORDERS[i]
        if s == 0:
            landed(state[i])
            if i + AHEAD < COUNT:
                state[i + AHEAD] = launch(along_z(i + AHEAD))
            state[i] = launch([along_dp(i, 3, 0, first), along_dp(i, 4, 0, second)])
        elif s == 1:
            landed(state[i][:1])
            state[i] = [state[i][1]] + launch([along_dp(i, 5, first, second)])
            launch([along_dp(i, 6, 0, 1), along_dp(i, 7, first, 1)])
        elif s == 2:
            landed(state[i])
            launch([along_dp(i, 8, second, 1), along_dp(i, 9, first | second, 1)])

    for i in range(AHEAD):
        state[i] = launch(along_z(i))
    for t in range(COUNT + 2):
        for s in (0, 1, 2):
            if 0 <= t - s < COUNT:
                stage(t - s, s)
    for i in range(COUNT):
        for slot, mask in ((6, 0), (7, ORDERS[i][0]), (8, ORDERS[i][1]), (9, 6)):
            along_dp(i, slot, mask, 1).wait_recv()
    for copy in flying:
        copy.wait_send()


def gather_all(locals_):
    dp_size = lax.axis_size("dp")
    anywhere = pl.BlockSpec(memory_space=pl.ANY)
    got = pl.pallas_call(
        functools.partial(gather_kernel, dp_size),
        out_shape=[jax.ShapeDtypeStruct((3,) + local.shape, BF) for local in locals_],
        in_specs=[anywhere] * COUNT,
        out_specs=[anywhere] * COUNT,
        scratch_shapes=[
            pltpu.SemaphoreType.DMA((COUNT, 10)),
            pltpu.SemaphoreType.DMA((COUNT, 10)),
        ],
        compiler_params=pltpu.CompilerParams(collective_id=0, has_side_effects=True),
    )(*locals_)
    return [jnp.concatenate([local[None], rest]) for local, rest in zip(locals_, got)]


def reduce_kernel(dp_size, *refs):
    grad = refs[:COUNT]
    out = refs[COUNT : 2 * COUNT]
    (core_in, own, first_in, second_in, more_in, z_in, whole, wide, send, recv, load, store) = (
        refs[2 * COUNT :]
    )
    size = out[0].shape[0] // PARTS
    me = lax.rem(lax.axis_index("dp"), PARTS)
    more = []
    bit = PARTS
    while bit < dp_size:
        more.append(bit)
        bit *= 2

    def rows(mask):
        return piece_rows(flip(me, mask), size)

    def masks(i):
        first, second = ORDERS[i]
        return (0, second, first, first | second)

    flying = []

    def launch(copies):
        for copy in copies:
            copy.start()
        flying.extend(copies)
        return copies

    def landed(copies):
        for copy in copies:
            copy.wait_recv()

    def loads(i):
        return [
            pltpu.make_async_copy(grad[i].at[:, rows(mask)], own.at[i % 2, k], load.at[i % 2, k])
            for k, mask in enumerate(masks(i))
        ]

    def added(left, right):
        left[...] = (left[...].astype(F32) + right[...].astype(F32)).astype(BF)

    def add_slabs(target, source):
        @pl.loop(0, 4)
        def _(r):
            added(target.at[r], source.at[r])

    def across(i):
        return [
            remote(
                grad[i].at[:, rows(1 | mask)],
                core_in.at[i, k],
                send.at[i, k],
                recv.at[i, k],
                {"dp": 1},
            )
            for k, mask in enumerate(masks(i))
        ]

    state = [None] * COUNT

    def stage(i, s):
        first, second = ORDERS[i]
        if s == 0:
            landed(state[i])
            if i + AHEAD < COUNT:
                state[i + AHEAD] = launch(across(i + AHEAD))
            for copy in loads(i):
                copy.wait()
            for k in (2, 3):
                add_slabs(core_in.at[i, k], own.at[i % 2, k])
            state[i] = launch(
                [
                    remote(
                        core_in.at[i, pl.ds(2, 2)],
                        first_in.at[i],
                        send.at[i, 4],
                        recv.at[i, 4],
                        {"dp": first},
                    )
                ]
            )
            for k in (0, 1):
                add_slabs(core_in.at[i, k], own.at[i % 2, k])
            if i + 2 < COUNT:
                for copy in loads(i + 2):
                    copy.start()
        elif s == 1:
            landed(state[i])
            add_slabs(core_in.at[i, 1], first_in.at[i, 1])
            state[i] = launch(
                [
                    remote(
                        core_in.at[i, 1],
                        second_in.at[i],
                        send.at[i, 5],
                        recv.at[i, 5],
                        {"dp": second},
                    )
                ]
            )
            add_slabs(core_in.at[i, 0], first_in.at[i, 0])
        elif s == 2:
            landed(state[i])
            add_slabs(core_in.at[i, 0], second_in.at[i])
            for e, bit in enumerate(more):
                copy = remote(
                    core_in.at[i, 0],
                    more_in.at[i, e],
                    send.at[i, 16 + e],
                    recv.at[i, 16 + e],
                    {"dp": bit},
                )
                copy.start()
                copy.wait()
                add_slabs(core_in.at[i, 0], more_in.at[i, e])
            state[i] = launch(
                [
                    remote(
                        core_in.at[i, 0, r],
                        z_in.at[i, r - 1],
                        send.at[i, 5 + r],
                        recv.at[i, 5 + r],
                        {"mp": r},
                    )
                    for r in (1, 2, 3)
                ]
            )
        elif s == 3:
            landed(state[i])
            total = core_in[i, 0, 0].astype(F32)
            for r in range(3):
                total = total + z_in[i, r].astype(F32)
            whole[i, rows(0), :] = total.astype(BF)
            state[i] = launch([spread(i, 9, 0, first), spread(i, 10, 0, second)])
        elif s == 4:
            landed(state[i][:1])
            state[i] = [state[i][1]] + launch([spread(i, 11, first, second)])
            launch([spread(i, 12, 0, 1), spread(i, 13, first, 1)])
        elif s == 5:
            landed(state[i])
            launch([spread(i, 14, second, 1), spread(i, 15, first | second, 1)])
            state[i] = [
                spread(i, 12, 0, 1),
                spread(i, 13, first, 1),
                spread(i, 14, second, 1),
                spread(i, 15, first | second, 1),
            ]
        elif s == 6:
            landed(state[i])
            if i >= 2:
                pltpu.make_async_copy(wide.at[i % 2], out[i - 2], store.at[i % 2]).wait()
            wide_i = wide.at[i % 2]

            @pl.loop(0, PARTS)
            def _(p):
                part = piece_rows(p, size)
                wide_i[part, :] = whole[i, part, :].astype(F32)

            pltpu.make_async_copy(wide.at[i % 2], out[i], store.at[i % 2]).start()

    def spread(i, slot, mask, bit):
        place = whole.at[i, rows(mask)]
        return remote(place, place, send.at[i, slot], recv.at[i, slot], {"dp": bit})

    for i in (0, 1):
        for copy in loads(i):
            copy.start()
    enter(dp_size)
    for i in range(AHEAD):
        state[i] = launch(across(i))
    for t in range(COUNT + 6):
        for s in range(7):
            if 0 <= t - s < COUNT:
                stage(t - s, s)
    for i in (COUNT - 2, COUNT - 1):
        pltpu.make_async_copy(wide.at[i % 2], out[i], store.at[i % 2]).wait()
    for copy in flying:
        copy.wait_send()


def reduce_all(grads):
    dp_size = lax.axis_size("dp")
    anywhere = pl.BlockSpec(memory_space=pl.ANY)
    rows, columns = grads[0].shape[1:]
    size = rows // PARTS
    more = max(1, (dp_size // PARTS).bit_length() - 1)
    return pl.pallas_call(
        functools.partial(reduce_kernel, dp_size),
        out_shape=[jax.ShapeDtypeStruct((rows, columns), F32)] * COUNT,
        in_specs=[anywhere] * COUNT,
        out_specs=[anywhere] * COUNT,
        scratch_shapes=[
            pltpu.VMEM((COUNT, 4, 4, size, columns), BF),
            pltpu.VMEM((2, 4, 4, size, columns), BF),
            pltpu.VMEM((COUNT, 2, 4, size, columns), BF),
            pltpu.VMEM((COUNT, 4, size, columns), BF),
            pltpu.VMEM((COUNT, more, 4, size, columns) if dp_size > PARTS else (1, 1, 4, 16, 128), BF),
            pltpu.VMEM((COUNT, 3, size, columns), BF),
            pltpu.VMEM((COUNT, rows, columns), BF),
            pltpu.VMEM((2, rows, columns), F32),
            pltpu.SemaphoreType.DMA((COUNT, 16 + more)),
            pltpu.SemaphoreType.DMA((COUNT, 16 + more)),
            pltpu.SemaphoreType.DMA((2, 4)),
            pltpu.SemaphoreType.DMA((2,)),
        ],
        compiler_params=pltpu.CompilerParams(
            collective_id=1, has_side_effects=True, vmem_limit_bytes=60 * 1024 * 1024
        ),
    )(*grads)


def reduce_rows(rows):
    for axis in ("mp", "dp"):
        bit = 1
        while bit < lax.axis_size(axis):
            rows = rows + swap(rows, axis, bit)
            bit *= 2
    return rows


def relative(chunks):
    return jnp.take(chunks, jnp.arange(4) ^ lax.axis_index("mp"), axis=0)


def heads_of(values):
    return values.reshape(values.shape[0], -1, HEAD_DIM)


def forward_block(resid, key_valid, small, full):
    gains, shifts, in_bias, out_bias, scales, up_bias = small
    attn_w, up_w, down_w = full
    normed, unit0, inverse0 = layer_norm(resid, gains[0], shifts[0])
    normed = normed.astype(BF)
    normed_all = jnp.concatenate([normed, swap(normed, "mp", 1)])
    wq = attn_w[:, 0:192].reshape(768, 768)
    wk = attn_w[:, 192:384].reshape(768, 768)
    wv = attn_w[:, 384:576].reshape(768, 768)
    wo = attn_w[:, 576:768].reshape(768, 768)
    query = (matmul_nt(normed, wq) + in_bias[0]).astype(BF)
    key = matmul_nt(normed_all, wk).astype(BF)
    value = (matmul_nt(normed_all, wv) + in_bias[1]).astype(BF)
    scores = jnp.einsum(
        "qhd,khd->hqk", heads_of(query), heads_of(key), preferred_element_type=F32
    ) * HEAD_DIM ** (-0.5)
    scores = jnp.where(key_valid[None, None, :], scores, -1e30)
    peak = jnp.max(scores, axis=-1, keepdims=True)
    exponent = jnp.exp(scores - peak)
    total = jnp.sum(exponent, axis=-1, keepdims=True)
    probs = (exponent / total).astype(BF)
    mixed = jnp.einsum("hqk,khd->qhd", probs, heads_of(value), preferred_element_type=F32)
    mixed = mixed.reshape(query.shape).astype(BF)
    log_total = peak + jnp.log(total)
    attn = matmul(mixed, wo) + out_bias[0]
    middle = resid + scales[0] * attn
    normed2, unit1, inverse1 = layer_norm(middle, gains[1], shifts[1])
    normed2 = normed2.astype(BF)
    pre = jnp.stack([matmul(normed2, up_w[r]) + up_bias[r] for r in range(4)], axis=1)
    hidden = gelu_exact(pre).astype(BF)
    mlp = (
        matmul(hidden.reshape(hidden.shape[0], -1), down_w.reshape(-1, 768)) + out_bias[1]
    )
    result = middle + scales[1] * mlp
    kept = (
        unit0,
        inverse0,
        normed_all,
        query,
        key,
        value,
        log_total,
        mixed,
        attn,
        unit1,
        inverse1,
        normed2,
        pre,
        hidden,
        mlp,
    )
    return result, kept


def backward_block(grad, key_valid, small, full, kept):
    gains, shifts, in_bias, out_bias, scales, up_bias = small
    attn_w, up_w, down_w = full
    (
        unit0,
        inverse0,
        normed_all,
        query,
        key,
        value,
        log_total,
        mixed,
        attn,
        unit1,
        inverse1,
        normed2,
        pre,
        hidden,
        mlp,
    ) = kept
    rows = grad.shape[0]
    scale_mlp = jnp.sum(grad * mlp, axis=0)
    grad_branch = (scales[1] * grad).astype(BF)
    bias_mlp = jnp.sum(grad_branch.astype(F32), axis=0)
    grad_down = jnp.stack([matmul_tn(hidden[:, r], grad_branch).astype(BF) for r in range(4)])
    grad_hidden = matmul_nt(grad_branch, down_w.reshape(-1, 768)).reshape(pre.shape)
    value_, gelu_back = jax.vjp(gelu_exact, pre)
    grad_pre = gelu_back(grad_hidden)[0].astype(BF)
    grad_up_bias = jnp.sum(grad_pre.astype(F32), axis=0)
    grad_up = jnp.stack([matmul_tn(normed2, grad_pre[:, r]).astype(BF) for r in range(4)])
    grad_normed2 = sum(matmul_nt(grad_pre[:, r], up_w[r]) for r in range(4))
    grad_middle, gain_mlp, shift_mlp = layer_norm_back(grad_normed2, unit1, inverse1, gains[1])
    grad_middle = grad + grad_middle
    scale_attn = jnp.sum(grad_middle * attn, axis=0)
    grad_attn = (scales[0] * grad_middle).astype(BF)
    bias_attn = jnp.sum(grad_attn.astype(F32), axis=0)
    wq = attn_w[:, 0:192].reshape(768, 768)
    wk = attn_w[:, 192:384].reshape(768, 768)
    wv = attn_w[:, 384:576].reshape(768, 768)
    wo = attn_w[:, 576:768].reshape(768, 768)
    grad_wo = matmul_tn(mixed, grad_attn).astype(BF)
    grad_mixed = matmul_nt(grad_attn, wo).astype(BF)
    scores = jnp.einsum(
        "qhd,khd->hqk", heads_of(query), heads_of(key), preferred_element_type=F32
    ) * HEAD_DIM ** (-0.5)
    scores = jnp.where(key_valid[None, None, :], scores, -1e30)
    probs = jnp.exp(scores - log_total)
    grad_probs = jnp.einsum(
        "qhd,khd->hqk", heads_of(grad_mixed), heads_of(value), preferred_element_type=F32
    )
    grad_value = jnp.einsum(
        "hqk,qhd->khd", probs.astype(BF), heads_of(grad_mixed), preferred_element_type=F32
    )
    inner = jnp.sum(probs * grad_probs, axis=-1, keepdims=True)
    grad_scores = (probs * (grad_probs - inner)).astype(BF)
    grad_query = jnp.einsum(
        "hqk,khd->qhd", grad_scores, heads_of(key), preferred_element_type=F32
    )
    grad_key = jnp.einsum(
        "hqk,qhd->khd", grad_scores, heads_of(query), preferred_element_type=F32
    )
    scale = HEAD_DIM ** (-0.5)
    grad_query = (grad_query * scale).astype(BF).reshape(query.shape)
    grad_key = (grad_key * scale).astype(BF).reshape(key.shape)
    grad_value = grad_value.astype(BF).reshape(key.shape)
    grad_in = [
        matmul_tn(grad_query, normed_all[:rows]).astype(BF).reshape(4, 192, 768),
        matmul_tn(grad_key, normed_all).astype(BF).reshape(4, 192, 768),
        matmul_tn(grad_value, normed_all).astype(BF).reshape(4, 192, 768),
        grad_wo.reshape(4, 192, 768),
    ]
    grad_attn_w = jnp.concatenate(grad_in, axis=1)
    grad_in_bias = jnp.stack(
        [
            jnp.sum(grad_query.astype(F32), axis=0),
            jnp.sum(grad_value.astype(F32), axis=0),
        ]
    )
    away = matmul(grad_key[rows:], wk) + matmul(grad_value[rows:], wv)
    grad_normed = (
        matmul(grad_query, wq)
        + matmul(grad_key[:rows], wk)
        + matmul(grad_value[:rows], wv)
        + swap(away.astype(BF), "mp", 1).astype(F32)
    )
    grad_resid, gain_attn, shift_attn = layer_norm_back(grad_normed, unit0, inverse0, gains[0])
    grad_resid = grad_middle + grad_resid
    packed = jnp.stack(
        [
            gain_attn,
            gain_mlp,
            shift_attn,
            shift_mlp,
            bias_attn,
            bias_mlp,
            scale_attn,
            scale_mlp,
        ]
    )
    in_bias_abs = relative(grad_in_bias.reshape(2, 4, 192).swapaxes(0, 1))
    packed = jnp.concatenate(
        [packed, in_bias_abs.reshape(2, 768), relative(grad_up_bias).reshape(4, 768)]
    )
    packed = reduce_rows(packed)
    in_bias_abs = packed[8:10].reshape(4, 2, 192)
    mine = lax.axis_index("mp")
    in_bias_out = lax.dynamic_index_in_dim(in_bias_abs, mine, 0, keepdims=False)
    up_bias_out = lax.dynamic_index_in_dim(packed[10:14], mine, 0, keepdims=False)
    rest = (packed, in_bias_out, up_bias_out)
    return grad_resid, (grad_down, grad_up, grad_attn_w), rest


def arrange(reduced, rest):
    grad_down, grad_up, grad_attn_w = reduced
    packed, in_bias_out, up_bias_out = rest
    return (
        packed[0:2],
        packed[2:4],
        grad_attn_w[:576].reshape(3, 192, 768).swapaxes(1, 2),
        in_bias_out,
        grad_attn_w[576:],
        packed[4:6],
        packed[6:8],
        grad_up,
        up_bias_out,
        grad_down,
    )


def local_block(weights):
    gains, shifts, p_in, p_bias, p_out, out_bias, scales, up, up_bias, down = weights
    attn_local = jnp.concatenate([p_in.swapaxes(1, 2).reshape(-1, p_in.shape[1]), p_out])
    return [attn_local, up, down]


def gather_small(project_bias, up_bias):
    bias = lax.all_gather(
        jnp.concatenate([project_bias.reshape(-1), up_bias]), "mp", axis=0, tiled=False
    )
    bias = relative(bias)
    in_bias = bias[:, :384].reshape(4, 2, 192).swapaxes(0, 1).reshape(2, 768)
    return in_bias, bias[:, 384:]


def body(inputs, lengths, cotangent, *params):
    student, teacher = params[:10], params[10:]
    z = lax.axis_index("mp")
    length = lax.dynamic_index_in_dim(lengths, z // 2, 0, keepdims=False)
    rows = inputs.shape[0]
    half = lax.rem(z, 2)
    position = jnp.concatenate(
        [half * rows + jnp.arange(rows), (1 - half) * rows + jnp.arange(rows)]
    )
    key_valid = position < length

    def prepare(weights):
        gains, shifts, p_in, p_bias, p_out, out_bias, scales, up, up_bias, down = weights
        in_bias, up_bias_all = gather_small(p_bias, up_bias)
        return (gains, shifts, in_bias, out_bias, scales, up_bias_all)

    full = gather_all(local_block(student) + local_block(teacher))
    student_full, teacher_full = full[:3], full[3:]
    student_small = prepare(student)
    teacher_small = prepare(teacher)
    start_rows = inputs.astype(F32)
    student_out, student_kept = forward_block(start_rows, key_valid, student_small, student_full)
    teacher_out, teacher_kept = forward_block(student_out, key_valid, teacher_small, teacher_full)
    grad_mid, teacher_large, teacher_rest = backward_block(
        cotangent.astype(F32), key_valid, teacher_small, teacher_full, teacher_kept
    )
    grad_input, student_large, student_rest = backward_block(
        grad_mid, key_valid, student_small, student_full, student_kept
    )
    reduced = reduce_all(teacher_large + student_large)
    return (
        (teacher_out.astype(BF), grad_input.astype(BF))
        + arrange(reduced[3:], student_rest)
        + arrange(reduced[:3], teacher_rest)
    )


def solution(mesh):
    rows = P(("dp", "mp"), None)
    weights = (
        P(),
        P(),
        P(None, None, "mp"),
        P(None, "mp"),
        P("mp", None),
        P(),
        P(),
        P(None, "mp"),
        P("mp"),
        P("mp", None),
    )
    in_specs = (rows, P("dp"), rows) + weights + weights
    out_specs = (rows, rows) + weights + weights
    return jax.shard_map(body, mesh=mesh, in_specs=in_specs, out_specs=out_specs, check_vma=False)
```

```python
import functools

import jax
import jax.numpy as jnp
from jax import lax
from jax.experimental import pallas as pl
from jax.experimental.pallas import tpu as pltpu
from jax.sharding import PartitionSpec as P

HEAD_DIM = 64
SLOT = 640
PARTS = 8
BF = jnp.bfloat16
F32 = jnp.float32

epsilon = 1e-06


def layer_norm(values, norm_gain, norm_shift):
    center = values - jnp.mean(values, axis=-1, keepdims=True)
    spread = jnp.mean(center * center, axis=-1, keepdims=True)
    inverse = lax.rsqrt(spread + epsilon)
    unit = center * inverse
    return unit * norm_gain + norm_shift, unit, inverse


def layer_norm_back(grad, unit, inverse, norm_gain):
    scaled = grad * norm_gain
    return (
        inverse
        * (
            scaled
            - jnp.mean(scaled, axis=-1, keepdims=True)
            - unit * jnp.mean(scaled * unit, axis=-1, keepdims=True)
        ),
        jnp.sum(grad * unit, axis=0),
        jnp.sum(grad, axis=0),
    )


def gelu_exact(values):
    return jax.nn.gelu(values, approximate=False)


def matmul(left_side, right_side):
    return jnp.dot(left_side, right_side, preferred_element_type=F32)


def matmul_tn(left_side, right_side):
    return lax.dot_general(
        left_side, right_side, (((0,), (0,)), ((), ())), preferred_element_type=F32
    )


def matmul_nt(left_side, right_side):
    return lax.dot_general(
        left_side, right_side, (((1,), (1,)), ((), ())), preferred_element_type=F32
    )


def swap(source, axis, bit):
    count = lax.axis_size(axis)
    return lax.ppermute(source, axis, [(i, i ^ bit) for i in range(count)])


def low_index():
    return lax.rem(lax.axis_index("dp"), PARTS)


MESH = pl.DeviceIdType.MESH
ORDERS = ((2, 4), (4, 2), (2, 4), (4, 2), (2, 4), (4, 2))
COUNT = len(ORDERS)
AHEAD = 2


def flip(index, bits):
    bit = 1
    while bit <= bits:
        if bits & bit:
            index = index + bit - 2 * bit * lax.rem(lax.div(index, bit), 2)
        bit *= 2
    return index


def partners(dp_size):
    bits = []
    bit = 1
    while bit < dp_size:
        bits.append({"dp": bit})
        bit *= 2
    return bits + [{"mp": r} for r in (1, 2, 3)]


def device_at(bits):
    return {axis: flip(lax.axis_index(axis), bit) for axis, bit in bits.items()}


def enter(dp_size):
    barrier = pltpu.get_barrier_semaphore()
    for bits in partners(dp_size):
        pl.semaphore_signal(barrier, inc=1, device_id=device_at(bits), device_id_type=MESH)
    pl.semaphore_wait(barrier, len(partners(dp_size)))


def remote(source, target, send, recv, bits):
    return pltpu.make_async_remote_copy(
        src_ref=source,
        dst_ref=target,
        send_sem=send,
        recv_sem=recv,
        device_id=device_at(bits),
        device_id_type=MESH,
    )


def piece_rows(index, size):
    return pl.ds(pl.multiple_of(index * size, size), size)


def dot(left_side, right_side, contract=(1, 0)):
    return lax.dot_general(
        left_side,
        right_side,
        (((contract[0],), (contract[1],)), ((), ())),
        preferred_element_type=F32,
    )


def blocks(count, size, body):
    @pl.loop(0, count)
    def _(i):
        body(pl.ds(pl.multiple_of(i * size, size), size))


def norm_parts(values):
    center = values - jnp.mean(values, axis=-1, keepdims=True)
    spread = jnp.mean(center * center, axis=-1, keepdims=True)
    inverse = lax.rsqrt(spread + epsilon)
    return center * inverse, inverse


def norm_rows(source, gain, shift, target):
    def body(rows):
        unit, _ = norm_parts(source[rows, :])
        target[rows, :] = (unit * gain + shift).astype(BF)

    blocks(source.shape[0] // 32, 32, body)


def project_rows(source, weight, bias, target):
    def body(columns):
        value = dot(source[...], weight[columns, :], (1, 1))
        if bias is not None:
            value = value + bias[:, columns]
        target[:, columns] = value.astype(BF)

    blocks(weight.shape[0] // 256, 256, body)


def low_lanes(shape):
    return lax.broadcasted_iota(jnp.int32, shape, 1) < HEAD_DIM


def attend_pairs(first, last, query, key, value, key_bias, mixed, log_total):
    rows = query.shape[0]

    @pl.loop(first, last)
    def _(p):
        lanes = pl.ds(pl.multiple_of(p * 128, 128), 128)
        query_pair = query[:, lanes]
        key_pair = key[:, lanes]
        value_pair = value[:, lanes]
        low = low_lanes((rows, 128))
        parts = []
        for side in range(2):
            chosen = low if side == 0 else ~low
            one = jnp.where(chosen, query_pair, jnp.zeros_like(query_pair))
            scores = dot(one, key_pair, (1, 1)) * HEAD_DIM ** (-0.5) + key_bias[...]
            peak = jnp.max(scores, axis=1, keepdims=True)
            exponent = jnp.exp(scores - peak)
            total = jnp.sum(exponent, axis=1, keepdims=True)
            probs = (exponent * (1.0 / total)).astype(BF)
            parts.append(dot(probs, value_pair))
            logs = jnp.broadcast_to(peak + jnp.log(total), (rows, 128))
            log_total[p, side, :, :] = logs.T[0:8, :]
        mixed[:, lanes] = jnp.where(low, parts[0], parts[1]).astype(BF)


def attend_out(mixed, weight, bias, scale, resid, attn, middle):
    def body(columns):
        value = dot(mixed[...], weight[:, columns]) + bias[:, columns]
        attn[:, columns] = value
        middle[:, columns] = resid[:, columns] + scale[:, columns] * value

    blocks(3, 256, body)


def gelu_exact(values):
    return 0.5 * values * (1.0 + lax.erf(values * (0.5**0.5)))


def mlp_chunk(r, normed, up, up_bias, down, pre, hidden, mlp):
    def body(columns):
        value = dot(normed[...], up[r, :, columns]) + up_bias[r : r + 1, columns]
        pre[r, :, columns] = value
        unit = gelu_exact(value).astype(BF)
        hidden[r, :, columns] = unit
        mlp[...] += dot(unit, down[r, columns, :])

    blocks(3, 256, body)

KEPT = (
    ("resid", (320, 768), F32),
    ("normed", (640, 768), BF),
    ("query", (320, 768), BF),
    ("key", (640, 768), BF),
    ("value", (640, 768), BF),
    ("log_total", (6, 2, 8, 320), F32),
    ("mixed", (320, 768), BF),
    ("attn", (320, 768), F32),
    ("middle", (320, 768), F32),
    ("normed2", (320, 768), BF),
    ("pre", (4, 320, 768), F32),
    ("hidden", (4, 320, 768), BF),
    ("mlp", (320, 768), F32),
)
KEPT_NAMES = [name for name, _, _ in KEPT]


def forward_kernel(*refs):
    refs = list(refs)

    def take(count):
        got = refs[:count]
        del refs[:count]
        return got

    local = take(COUNT)
    inputs, key_bias, small = take(3)
    params = [take(4), take(4)]
    full = take(COUNT)
    kept_out = [dict(zip(KEPT_NAMES, take(len(KEPT)))) for _ in range(2)]
    (output,) = take(1)
    kept = [{name: ref.at[b] for name, ref in zip(KEPT_NAMES, refs)} for b in range(2)]
    take(len(KEPT))
    attn_w, up_w, down_w, small_in, in_bias, up_bias = take(6)
    send, recv, other, load, store = take(5)
    size = local[0].shape[0] // PARTS
    rows = inputs.shape[0]
    me = lax.rem(lax.axis_index("dp"), PARTS)
    flying = []
    waiting = []

    def part(mask):
        return piece_rows(flip(me, mask), size)

    def slab(i, mask):
        return full[i].at[:, part(mask)]

    def along_z(i):
        return [
            remote(
                local[i].at[part(0)],
                full[i].at[r - 1, part(0)],
                send.at[i, r - 1],
                recv.at[i, r - 1],
                {"mp": r},
            )
            for r in (1, 2, 3)
        ]

    def along_dp(i, slot, mask, bit):
        return remote(
            slab(i, mask), slab(i, mask), send.at[i, slot], recv.at[i, slot], {"dp": bit}
        )

    def launch(copies):
        for copy in copies:
            copy.start()
        flying.extend(copies)
        return copies

    def landed(copies):
        for copy in copies:
            copy.wait_recv()

    state = [None] * COUNT

    def stage(i, s):
        first, second = ORDERS[i]
        if s == 0:
            landed(state[i])
            if i + AHEAD < COUNT:
                state[i + AHEAD] = launch(along_z(i + AHEAD))
            state[i] = launch([along_dp(i, 3, 0, first), along_dp(i, 4, 0, second)])
        elif s == 1:
            landed(state[i][:1])
            state[i] = [state[i][1]] + launch([along_dp(i, 5, first, second)])
            launch([along_dp(i, 6, 0, 1), along_dp(i, 7, first, 1)])
        elif s == 2:
            landed(state[i])
            launch([along_dp(i, 8, second, 1), along_dp(i, 9, first | second, 1)])

    def step(t):
        for s in (0, 1, 2):
            if 0 <= t - s < COUNT:
                stage(t - s, s)

    def complete(i):
        for slot, mask in ((6, 0), (7, ORDERS[i][0]), (8, ORDERS[i][1]), (9, 6)):
            along_dp(i, slot, mask, 1).wait_recv()

    def chunk(i, r):
        return local[i] if r == 0 else full[i].at[r - 1]

    def load_attn(i):
        copies = []
        for kind in range(4):
            for r in range(4):
                copies.append(
                    pltpu.make_async_copy(
                        chunk(i, r).at[pl.ds(kind * 192, 192)],
                        attn_w.at[kind, pl.ds(r * 192, 192)],
                        load.at[0, kind * 4 + r],
                    )
                )
        for copy in copies:
            copy.start()
        return copies

    def load_mlp(i, target, slot):
        copies = [
            pltpu.make_async_copy(chunk(i, r), target.at[r], load.at[slot, r]) for r in range(4)
        ]
        for copy in copies:
            copy.start()
        return copies

    def finish(copies):
        for copy in copies:
            copy.wait()

    def save(b, *names):
        for name in names:
            copy = pltpu.make_async_copy(
                kept[b][name], kept_out[b][name], store.at[b, KEPT_NAMES.index(name)]
            )
            copy.start()
            waiting.append(copy)

    def exchange(b):
        copy = remote(
            kept[b]["normed"].at[pl.ds(0, rows)],
            kept[b]["normed"].at[pl.ds(rows, rows)],
            other.at[0, 3 + b],
            other.at[1, 3 + b],
            {"mp": 1},
        )
        return launch([copy])

    enter(lax.axis_size("dp"))
    bias_in = launch(
        [
            remote(small.at[r], small_in.at[r - 1], other.at[0, r - 1], other.at[1, r - 1], {"mp": r})
            for r in (1, 2, 3)
        ]
    )
    for i in range(AHEAD):
        state[i] = launch(along_z(i))

    def widen(part_rows):
        kept[0]["resid"][part_rows, :] = inputs[part_rows, :].astype(F32)

    blocks(10, 32, widen)

    for b in range(2):
        k = kept[b]
        gains, shifts, out_bias, scales = params[b]
        base = 3 * b
        norm_rows(k["resid"], gains[0:1, :], shifts[0:1, :], k["normed"].at[pl.ds(0, rows)])
        save(b, "resid")
        swapped = exchange(b)
        if b == 0:
            step(0)
            step(1)
            step(2)
            landed(bias_in)
            for c in range(2):
                in_bias[c] = small[0, c, 0:8] + small_in[0, c] + small_in[1, c] + small_in[2, c]
                up_bias[c, 0:1] = small[0, c, 0:1]
                for r in (1, 2, 3):
                    up_bias[c, r : r + 1] = small_in[r - 1, c, 0:1]
        complete(base)
        pending = load_attn(base)
        project_bias = in_bias.at[b]
        landed(swapped)
        finish(pending)
        project_rows(k["normed"].at[pl.ds(0, rows)], attn_w.at[0], project_bias.at[pl.ds(1, 1)], k["query"])
        project_rows(k["normed"], attn_w.at[1], None, k["key"])
        project_rows(k["normed"], attn_w.at[2], project_bias.at[pl.ds(2, 1)], k["value"])
        save(b, "normed", "query", "key", "value")
        pair_args = (k["query"], k["key"], k["value"], key_bias, k["mixed"], k["log_total"])
        attend_pairs(0, 3, *pair_args)
        step(3 * b + 3)
        attend_pairs(3, 6, *pair_args)
        save(b, "log_total", "mixed")
        attend_out(
            k["mixed"],
            attn_w.at[3],
            out_bias.at[pl.ds(0, 1)],
            scales.at[pl.ds(0, 1)],
            k["resid"],
            k["attn"],
            k["middle"],
        )
        norm_rows(k["middle"], gains[1:2, :], shifts[1:2, :], k["normed2"])
        save(b, "attn", "middle", "normed2")
        complete(base + 1)
        pending = load_mlp(base + 1, up_w, 1)
        step(3 * b + 4)
        complete(base + 2)
        pending = pending + load_mlp(base + 2, down_w, 2)
        k["mlp"][...] = jnp.broadcast_to(out_bias[1:2, :], k["mlp"].shape)
        finish(pending)
        for r in range(4):
            mlp_chunk(
                r, k["normed2"], up_w, up_bias.at[b], down_w, k["pre"], k["hidden"], k["mlp"]
            )
            if r == 1:
                step(3 * b + 5)
        save(b, "pre", "hidden", "mlp")

        def result(part_rows):
            value = k["middle"][part_rows, :] + scales[1:2, :] * k["mlp"][part_rows, :]
            if b == 0:
                kept[1]["resid"][part_rows, :] = value
            else:
                output[part_rows, :] = value.astype(BF)

        blocks(10, 32, result)
    for copy in flying:
        copy.wait_send()
    finish(waiting)


def forward_all(locals_, inputs, key_bias, small, params):
    anywhere = pl.BlockSpec(memory_space=pl.ANY)
    vmem = pl.BlockSpec(memory_space=pltpu.VMEM)
    matrix = locals_[0].shape
    kept_shapes = [jax.ShapeDtypeStruct(shape, kind) for _, shape, kind in KEPT]
    got = pl.pallas_call(
        forward_kernel,
        out_shape=[jax.ShapeDtypeStruct((3,) + matrix, BF)] * COUNT
        + kept_shapes * 2
        + [jax.ShapeDtypeStruct(inputs.shape, BF)],
        in_specs=[anywhere] * COUNT + [vmem] * 11,
        out_specs=[anywhere] * (COUNT + 2 * len(KEPT)) + [vmem],
        scratch_shapes=[pltpu.VMEM((2,) + shape, kind) for _, shape, kind in KEPT]
        + [
            pltpu.VMEM((4,) + matrix, BF),
            pltpu.VMEM((4,) + matrix, BF),
            pltpu.VMEM((4,) + matrix, BF),
            pltpu.VMEM((3, 2, 8, 768), F32),
            pltpu.VMEM((2, 8, 768), F32),
            pltpu.VMEM((2, 8, 768), F32),
            pltpu.SemaphoreType.DMA((COUNT, 10)),
            pltpu.SemaphoreType.DMA((COUNT, 10)),
            pltpu.SemaphoreType.DMA((2, 5)),
            pltpu.SemaphoreType.DMA((3, 16)),
            pltpu.SemaphoreType.DMA((2, len(KEPT))),
        ],
        compiler_params=pltpu.CompilerParams(
            collective_id=0, has_side_effects=True, vmem_limit_bytes=60 * 1024 * 1024
        ),
    )(*locals_, inputs, key_bias, small, *params)
    full = got[:COUNT]
    kept = [
        dict(zip(KEPT_NAMES, got[COUNT + b * len(KEPT) : COUNT + (b + 1) * len(KEPT)]))
        for b in range(2)
    ]
    return full, kept, got[-1]


def reduce_kernel(dp_size, *refs):
    grad = refs[:COUNT]
    out = refs[COUNT : 2 * COUNT]
    (core_in, own, first_in, second_in, more_in, z_in, whole, wide, send, recv, load, store) = (
        refs[2 * COUNT :]
    )
    size = out[0].shape[0] // PARTS
    me = lax.rem(lax.axis_index("dp"), PARTS)
    more = []
    bit = PARTS
    while bit < dp_size:
        more.append(bit)
        bit *= 2

    def rows(mask):
        return piece_rows(flip(me, mask), size)

    def masks(i):
        first, second = ORDERS[i]
        return (0, second, first, first | second)

    flying = []

    def launch(copies):
        for copy in copies:
            copy.start()
        flying.extend(copies)
        return copies

    def landed(copies):
        for copy in copies:
            copy.wait_recv()

    def loads(i):
        return [
            pltpu.make_async_copy(grad[i].at[:, rows(mask)], own.at[i % 2, k], load.at[i % 2, k])
            for k, mask in enumerate(masks(i))
        ]

    def added(left, right):
        left[...] = (left[...].astype(F32) + right[...].astype(F32)).astype(BF)

    def add_slabs(target, source):
        @pl.loop(0, 4)
        def _(r):
            added(target.at[r], source.at[r])

    def across(i):
        return [
            remote(
                grad[i].at[:, rows(1 | mask)],
                core_in.at[i, k],
                send.at[i, k],
                recv.at[i, k],
                {"dp": 1},
            )
            for k, mask in enumerate(masks(i))
        ]

    state = [None] * COUNT

    def stage(i, s):
        first, second = ORDERS[i]
        if s == 0:
            landed(state[i])
            if i + AHEAD < COUNT:
                state[i + AHEAD] = launch(across(i + AHEAD))
            for copy in loads(i):
                copy.wait()
            for k in (2, 3):
                add_slabs(core_in.at[i, k], own.at[i % 2, k])
            state[i] = launch(
                [
                    remote(
                        core_in.at[i, pl.ds(2, 2)],
                        first_in.at[i],
                        send.at[i, 4],
                        recv.at[i, 4],
                        {"dp": first},
                    )
                ]
            )
            for k in (0, 1):
                add_slabs(core_in.at[i, k], own.at[i % 2, k])
            if i + 2 < COUNT:
                for copy in loads(i + 2):
                    copy.start()
        elif s == 1:
            landed(state[i])
            add_slabs(core_in.at[i, 1], first_in.at[i, 1])
            state[i] = launch(
                [
                    remote(
                        core_in.at[i, 1],
                        second_in.at[i],
                        send.at[i, 5],
                        recv.at[i, 5],
                        {"dp": second},
                    )
                ]
            )
            add_slabs(core_in.at[i, 0], first_in.at[i, 0])
        elif s == 2:
            landed(state[i])
            add_slabs(core_in.at[i, 0], second_in.at[i])
            for e, bit in enumerate(more):
                copy = remote(
                    core_in.at[i, 0],
                    more_in.at[i, e],
                    send.at[i, 16 + e],
                    recv.at[i, 16 + e],
                    {"dp": bit},
                )
                copy.start()
                copy.wait()
                add_slabs(core_in.at[i, 0], more_in.at[i, e])
            state[i] = launch(
                [
                    remote(
                        core_in.at[i, 0, r],
                        z_in.at[i, r - 1],
                        send.at[i, 5 + r],
                        recv.at[i, 5 + r],
                        {"mp": r},
                    )
                    for r in (1, 2, 3)
                ]
            )
        elif s == 3:
            landed(state[i])
            total = core_in[i, 0, 0].astype(F32)
            for r in range(3):
                total = total + z_in[i, r].astype(F32)
            whole[i, rows(0), :] = total.astype(BF)
            state[i] = launch([spread(i, 9, 0, first), spread(i, 10, 0, second)])
        elif s == 4:
            landed(state[i][:1])
            state[i] = [state[i][1]] + launch([spread(i, 11, first, second)])
            launch([spread(i, 12, 0, 1), spread(i, 13, first, 1)])
        elif s == 5:
            landed(state[i])
            launch([spread(i, 14, second, 1), spread(i, 15, first | second, 1)])
            state[i] = [
                spread(i, 12, 0, 1),
                spread(i, 13, first, 1),
                spread(i, 14, second, 1),
                spread(i, 15, first | second, 1),
            ]
        elif s == 6:
            landed(state[i])
            if i >= 2:
                pltpu.make_async_copy(wide.at[i % 2], out[i - 2], store.at[i % 2]).wait()
            wide_i = wide.at[i % 2]

            @pl.loop(0, PARTS)
            def _(p):
                part = piece_rows(p, size)
                wide_i[part, :] = whole[i, part, :].astype(F32)

            pltpu.make_async_copy(wide.at[i % 2], out[i], store.at[i % 2]).start()

    def spread(i, slot, mask, bit):
        place = whole.at[i, rows(mask)]
        return remote(place, place, send.at[i, slot], recv.at[i, slot], {"dp": bit})

    for i in (0, 1):
        for copy in loads(i):
            copy.start()
    enter(dp_size)
    for i in range(AHEAD):
        state[i] = launch(across(i))
    for t in range(COUNT + 6):
        for s in range(7):
            if 0 <= t - s < COUNT:
                stage(t - s, s)
    for i in (COUNT - 2, COUNT - 1):
        pltpu.make_async_copy(wide.at[i % 2], out[i], store.at[i % 2]).wait()
    for copy in flying:
        copy.wait_send()


def reduce_all(grads):
    dp_size = lax.axis_size("dp")
    anywhere = pl.BlockSpec(memory_space=pl.ANY)
    rows, columns = grads[0].shape[1:]
    size = rows // PARTS
    more = max(1, (dp_size // PARTS).bit_length() - 1)
    return pl.pallas_call(
        functools.partial(reduce_kernel, dp_size),
        out_shape=[jax.ShapeDtypeStruct((rows, columns), F32)] * COUNT,
        in_specs=[anywhere] * COUNT,
        out_specs=[anywhere] * COUNT,
        scratch_shapes=[
            pltpu.VMEM((COUNT, 4, 4, size, columns), BF),
            pltpu.VMEM((2, 4, 4, size, columns), BF),
            pltpu.VMEM((COUNT, 2, 4, size, columns), BF),
            pltpu.VMEM((COUNT, 4, size, columns), BF),
            pltpu.VMEM((COUNT, more, 4, size, columns) if dp_size > PARTS else (1, 1, 4, 16, 128), BF),
            pltpu.VMEM((COUNT, 3, size, columns), BF),
            pltpu.VMEM((COUNT, rows, columns), BF),
            pltpu.VMEM((2, rows, columns), F32),
            pltpu.SemaphoreType.DMA((COUNT, 16 + more)),
            pltpu.SemaphoreType.DMA((COUNT, 16 + more)),
            pltpu.SemaphoreType.DMA((2, 4)),
            pltpu.SemaphoreType.DMA((2,)),
        ],
        compiler_params=pltpu.CompilerParams(
            collective_id=1, has_side_effects=True, vmem_limit_bytes=60 * 1024 * 1024
        ),
    )(*grads)


def reduce_rows(rows):
    for axis in ("mp", "dp"):
        bit = 1
        while bit < lax.axis_size(axis):
            rows = rows + swap(rows, axis, bit)
            bit *= 2
    return rows


def relative(chunks):
    return jnp.take(chunks, jnp.arange(4) ^ lax.axis_index("mp"), axis=0)


def heads_of(values):
    return values.reshape(values.shape[0], -1, HEAD_DIM)


def backward_block(grad, key_valid, small, full, kept):
    gains, shifts, in_bias, out_bias, scales, up_bias = small
    attn_w, up_w, down_w = full
    (
        unit0,
        inverse0,
        normed_all,
        query,
        key,
        value,
        log_total,
        mixed,
        attn,
        unit1,
        inverse1,
        normed2,
        pre,
        hidden,
        mlp,
    ) = kept
    rows = grad.shape[0]
    scale_mlp = jnp.sum(grad * mlp, axis=0)
    grad_branch = (scales[1] * grad).astype(BF)
    bias_mlp = jnp.sum(grad_branch.astype(F32), axis=0)
    grad_down = jnp.stack([matmul_tn(hidden[:, r], grad_branch).astype(BF) for r in range(4)])
    grad_hidden = matmul_nt(grad_branch, down_w.reshape(-1, 768)).reshape(pre.shape)
    value_, gelu_back = jax.vjp(gelu_exact, pre)
    grad_pre = gelu_back(grad_hidden)[0].astype(BF)
    grad_up_bias = jnp.sum(grad_pre.astype(F32), axis=0)
    grad_up = jnp.stack([matmul_tn(normed2, grad_pre[:, r]).astype(BF) for r in range(4)])
    grad_normed2 = sum(matmul_nt(grad_pre[:, r], up_w[r]) for r in range(4))
    grad_middle, gain_mlp, shift_mlp = layer_norm_back(grad_normed2, unit1, inverse1, gains[1])
    grad_middle = grad + grad_middle
    scale_attn = jnp.sum(grad_middle * attn, axis=0)
    grad_attn = (scales[0] * grad_middle).astype(BF)
    bias_attn = jnp.sum(grad_attn.astype(F32), axis=0)
    wq = attn_w[:, 0:192].reshape(768, 768)
    wk = attn_w[:, 192:384].reshape(768, 768)
    wv = attn_w[:, 384:576].reshape(768, 768)
    wo = attn_w[:, 576:768].reshape(768, 768)
    grad_wo = matmul_tn(mixed, grad_attn).astype(BF)
    grad_mixed = matmul_nt(grad_attn, wo).astype(BF)
    scores = jnp.einsum(
        "qhd,khd->hqk", heads_of(query), heads_of(key), preferred_element_type=F32
    ) * HEAD_DIM ** (-0.5)
    scores = jnp.where(key_valid[None, None, :], scores, -1e30)
    probs = jnp.exp(scores - log_total)
    grad_probs = jnp.einsum(
        "qhd,khd->hqk", heads_of(grad_mixed), heads_of(value), preferred_element_type=F32
    )
    grad_value = jnp.einsum(
        "hqk,qhd->khd", probs.astype(BF), heads_of(grad_mixed), preferred_element_type=F32
    )
    inner = jnp.sum(probs * grad_probs, axis=-1, keepdims=True)
    grad_scores = (probs * (grad_probs - inner)).astype(BF)
    grad_query = jnp.einsum(
        "hqk,khd->qhd", grad_scores, heads_of(key), preferred_element_type=F32
    )
    grad_key = jnp.einsum(
        "hqk,qhd->khd", grad_scores, heads_of(query), preferred_element_type=F32
    )
    scale = HEAD_DIM ** (-0.5)
    grad_query = (grad_query * scale).astype(BF).reshape(query.shape)
    grad_key = (grad_key * scale).astype(BF).reshape(key.shape)
    grad_value = grad_value.astype(BF).reshape(key.shape)
    grad_in = [
        matmul_tn(grad_query, normed_all[:rows]).astype(BF).reshape(4, 192, 768),
        matmul_tn(grad_key, normed_all).astype(BF).reshape(4, 192, 768),
        matmul_tn(grad_value, normed_all).astype(BF).reshape(4, 192, 768),
        grad_wo.reshape(4, 192, 768),
    ]
    grad_attn_w = jnp.concatenate(grad_in, axis=1)
    grad_in_bias = jnp.stack(
        [
            jnp.sum(grad_query.astype(F32), axis=0),
            jnp.sum(grad_value.astype(F32), axis=0),
        ]
    )
    away = matmul(grad_key[rows:], wk) + matmul(grad_value[rows:], wv)
    grad_normed = (
        matmul(grad_query, wq)
        + matmul(grad_key[:rows], wk)
        + matmul(grad_value[:rows], wv)
        + swap(away.astype(BF), "mp", 1).astype(F32)
    )
    grad_resid, gain_attn, shift_attn = layer_norm_back(grad_normed, unit0, inverse0, gains[0])
    grad_resid = grad_middle + grad_resid
    packed = jnp.stack(
        [
            gain_attn,
            gain_mlp,
            shift_attn,
            shift_mlp,
            bias_attn,
            bias_mlp,
            scale_attn,
            scale_mlp,
        ]
    )
    in_bias_abs = relative(grad_in_bias.reshape(2, 4, 192).swapaxes(0, 1))
    packed = jnp.concatenate(
        [packed, in_bias_abs.reshape(2, 768), relative(grad_up_bias).reshape(4, 768)]
    )
    packed = reduce_rows(packed)
    in_bias_abs = packed[8:10].reshape(4, 2, 192)
    mine = lax.axis_index("mp")
    in_bias_out = lax.dynamic_index_in_dim(in_bias_abs, mine, 0, keepdims=False)
    up_bias_out = lax.dynamic_index_in_dim(packed[10:14], mine, 0, keepdims=False)
    rest = (packed, in_bias_out, up_bias_out)
    return grad_resid, (grad_down, grad_up, grad_attn_w), rest


def arrange(reduced, rest):
    grad_down, grad_up, grad_attn_w = reduced
    packed, in_bias_out, up_bias_out = rest
    return (
        packed[0:2],
        packed[2:4],
        grad_attn_w[:576].reshape(3, 192, 768).swapaxes(1, 2),
        in_bias_out,
        grad_attn_w[576:],
        packed[4:6],
        packed[6:8],
        grad_up,
        up_bias_out,
        grad_down,
    )


def local_block(weights):
    gains, shifts, p_in, p_bias, p_out, out_bias, scales, up, up_bias, down = weights
    attn_local = jnp.concatenate([p_in.swapaxes(1, 2).reshape(-1, p_in.shape[1]), p_out])
    return [attn_local, up, down]


def small_rows(weights):
    p_bias, up_bias = weights[3], weights[8]
    width = p_bias.shape[1]
    rows = [
        jnp.concatenate(
            [
                up_bias[None],
                jnp.pad(p_bias, ((0, 0), (r * width, (3 - r) * width))),
                jnp.zeros((5, 4 * width), F32),
            ]
        )
        for r in range(4)
    ]
    return jnp.stack(rows)


def unpack_kept(k, gains):
    unit0, inverse0 = norm_parts(k["resid"])
    unit1, inverse1 = norm_parts(k["middle"])
    log_total = k["log_total"][:, :, 0].reshape(12, -1, 1)
    return (
        unit0,
        inverse0,
        k["normed"],
        k["query"],
        k["key"],
        k["value"],
        log_total,
        k["mixed"],
        k["attn"],
        unit1,
        inverse1,
        k["normed2"],
        k["pre"].swapaxes(0, 1),
        k["hidden"].swapaxes(0, 1),
        k["mlp"],
    )


def body(inputs, lengths, cotangent, *params):
    student, teacher = params[:10], params[10:]
    z = lax.axis_index("mp")
    length = lax.dynamic_index_in_dim(lengths, z // 2, 0, keepdims=False)
    rows = inputs.shape[0]
    half = lax.rem(z, 2)
    position = jnp.concatenate(
        [half * rows + jnp.arange(rows), (1 - half) * rows + jnp.arange(rows)]
    )
    key_valid = position < length
    key_bias = jnp.where(key_valid, 0.0, -1e30).astype(F32)[None]
    locals_ = local_block(student) + local_block(teacher)
    small = jnp.stack([small_rows(student), small_rows(teacher)], axis=1)
    replicated = [
        weights[position_] for weights in (student, teacher) for position_ in (0, 1, 5, 6)
    ]
    got, kept, output = forward_all(locals_, inputs, key_bias, small, replicated)
    full = [jnp.concatenate([local[None], rest]) for local, rest in zip(locals_, got)]
    student_full, teacher_full = full[:3], full[3:]

    def trimmed(weights):
        return (weights[0], weights[1], None, weights[5], weights[6], None)

    grad_mid, teacher_large, teacher_rest = backward_block(
        cotangent.astype(F32),
        key_valid,
        trimmed(teacher),
        teacher_full,
        unpack_kept(kept[1], teacher[0]),
    )
    grad_input, student_large, student_rest = backward_block(
        grad_mid, key_valid, trimmed(student), student_full, unpack_kept(kept[0], student[0])
    )
    reduced = reduce_all(teacher_large + student_large)
    return (
        (output, grad_input.astype(BF))
        + arrange(reduced[3:], student_rest)
        + arrange(reduced[:3], teacher_rest)
    )


def solution(mesh):
    rows = P(("dp", "mp"), None)
    weights = (
        P(),
        P(),
        P(None, None, "mp"),
        P(None, "mp"),
        P("mp", None),
        P(),
        P(),
        P(None, "mp"),
        P("mp"),
        P("mp", None),
    )
    in_specs = (rows, P("dp"), rows) + weights + weights
    out_specs = (rows, rows) + weights + weights
    return jax.shard_map(body, mesh=mesh, in_specs=in_specs, out_specs=out_specs, check_vma=False)
```

```python
import functools

import jax
import jax.numpy as jnp
from jax import lax
from jax.experimental import pallas as pl
from jax.experimental.pallas import tpu as pltpu
from jax.sharding import PartitionSpec as P

HEAD_DIM = 64
SLOT = 640
PARTS = 8
BF = jnp.bfloat16
F32 = jnp.float32

epsilon = 1e-06

MESH = pl.DeviceIdType.MESH
COUNT = 6
AHEAD = 2


def flip(index, bits):
    bit = 1
    while bit <= bits:
        if bits & bit:
            index = index + bit - 2 * bit * lax.rem(lax.div(index, bit), 2)
        bit *= 2
    return index


def partners(dp_size):
    bits = []
    bit = 1
    while bit < dp_size:
        bits.append({"dp": bit})
        bit *= 2
    return bits + [{"mp": r} for r in (1, 2, 3)]


def device_at(bits):
    return {axis: flip(lax.axis_index(axis), bit) for axis, bit in bits.items()}


def enter(dp_size):
    barrier = pltpu.get_barrier_semaphore()
    for bits in partners(dp_size):
        pl.semaphore_signal(barrier, inc=1, device_id=device_at(bits), device_id_type=MESH)
    pl.semaphore_wait(barrier, len(partners(dp_size)))


def remote(source, target, send, recv, bits):
    return pltpu.make_async_remote_copy(
        src_ref=source,
        dst_ref=target,
        send_sem=send,
        recv_sem=recv,
        device_id=device_at(bits),
        device_id_type=MESH,
    )


def piece_rows(index, size):
    return pl.ds(pl.multiple_of(index * size, size), size)


def dot(left_side, right_side, contract=(1, 0)):
    return lax.dot_general(
        left_side,
        right_side,
        (((contract[0],), (contract[1],)), ((), ())),
        preferred_element_type=F32,
    )


def blocks(count, size, body):
    @pl.loop(0, count)
    def _(i):
        body(pl.ds(pl.multiple_of(i * size, size), size))


def norm_parts(values):
    center = values - jnp.mean(values, axis=-1, keepdims=True)
    spread = jnp.mean(center * center, axis=-1, keepdims=True)
    inverse = lax.rsqrt(spread + epsilon)
    return center * inverse, inverse


def norm_rows(source, gain, shift, target):
    def body(rows):
        unit, _ = norm_parts(source[rows, :])
        target[rows, :] = (unit * gain + shift).astype(BF)

    blocks(source.shape[0] // 32, 32, body)


def project_rows(source, weight, bias, target):
    def body(columns):
        value = dot(source[...], weight[columns, :], (1, 1))
        if bias is not None:
            value = value + bias[:, columns]
        target[:, columns] = value.astype(BF)

    blocks(weight.shape[0] // 256, 256, body)


def low_lanes(shape):
    return lax.broadcasted_iota(jnp.int32, shape, 1) < HEAD_DIM


def two_heads(pair, low):
    nothing = jnp.zeros_like(pair)
    return jnp.concatenate([jnp.where(low, pair, nothing), jnp.where(low, nothing, pair)])


def attend_pairs(first, last, query, key, value, key_bias, mixed, log_total):
    rows = query.shape[0]

    @pl.loop(first, last)
    def _(p):
        lanes = pl.ds(pl.multiple_of(p * 128, 128), 128)
        low = low_lanes((rows, 128))
        both = two_heads(query[:, lanes], low)
        scores = dot(both, key[:, lanes], (1, 1)) * HEAD_DIM ** (-0.5) + key_bias[...]
        peak = jnp.max(scores, axis=1, keepdims=True)
        exponent = jnp.exp(scores - peak)
        total = jnp.sum(exponent, axis=1, keepdims=True)
        probs = (exponent * (1.0 / total)).astype(BF)
        result = dot(probs, value[:, lanes])
        logs = jnp.broadcast_to(peak + jnp.log(total), (2 * rows, 128))
        log_total[p, :, :] = logs.T[0:8, :]
        mixed[:, lanes] = jnp.where(low, result[0:rows], result[rows:]).astype(BF)


def attend_out(mixed, weight, bias, scale, resid, attn, middle):
    def body(columns):
        value = dot(mixed[...], weight[:, columns]) + bias[:, columns]
        attn[:, columns] = value
        middle[:, columns] = resid[:, columns] + scale[:, columns] * value

    blocks(3, 256, body)


def gelu_exact(values):
    return 0.5 * values * (1.0 + lax.erf(values * (0.5**0.5)))


def mlp_chunk(r, normed, up, up_bias, down, pre, hidden, mlp):
    def body(columns):
        value = dot(normed[...], up[r, :, columns]) + up_bias[r : r + 1, columns]
        pre[r, :, columns] = value
        unit = gelu_exact(value).astype(BF)
        hidden[r, :, columns] = unit
        mlp[...] += dot(unit, down[r, columns, :])

    blocks(3, 256, body)


def attend_pairs_back(
    first, last, query, key, value, key_bias, log_total, grad, grad_query, grad_key, grad_value
):
    rows = query.shape[0]
    scale = HEAD_DIM ** (-0.5)

    @pl.loop(first, last)
    def _(p):
        lanes = pl.ds(pl.multiple_of(p * 128, 128), 128)
        low = low_lanes((rows, 128))
        both = two_heads(query[:, lanes], low)
        both_grad = two_heads(grad[:, lanes], low)
        key_pair = key[:, lanes]
        scores = dot(key_pair, both, (1, 1)) * scale + key_bias[...]
        probs = jnp.exp(scores - log_total[p, 0:1, :])
        grad_value[:, lanes] = dot(probs.astype(BF), both_grad).astype(BF)
        grad_probs = dot(value[:, lanes], both_grad, (1, 1))
        inner = jnp.sum(probs * grad_probs, axis=0, keepdims=True)
        grad_scores = (probs * (grad_probs - inner)).astype(BF)
        grad_key[:, lanes] = (dot(grad_scores, both) * scale).astype(BF)
        result = dot(grad_scores, key_pair, (0, 0)) * scale
        grad_query[:, lanes] = jnp.where(low, result[0:rows], result[rows:]).astype(BF)


def gelu_slope(values):
    bell = jnp.exp(-0.5 * values * values) * 0.3989422804014327
    return 0.5 * (1.0 + lax.erf(values * (0.5**0.5))) + values * bell


def column_sum(values):
    return jnp.sum(values, axis=0, keepdims=True)


def branch_grad(grad, mlp, scale, branch, scale_sum, bias_sum):
    scale_sum[...] = jnp.zeros_like(scale_sum)
    bias_sum[...] = jnp.zeros_like(bias_sum)

    def body(rows):
        value = grad[rows, :]
        scale_sum[...] += column_sum(value * mlp[rows, :])
        low = (scale * value).astype(BF)
        branch[rows, :] = low
        bias_sum[...] += column_sum(low.astype(F32))

    blocks(grad.shape[0] // 32, 32, body)


def norm_back(source, slope, gain, grad, gain_sum, shift_sum, after=None):
    gain_sum[...] = jnp.zeros_like(gain_sum)
    shift_sum[...] = jnp.zeros_like(shift_sum)

    def body(rows):
        unit, inverse = norm_parts(source[rows, :])
        value = slope[rows, :]
        gain_sum[...] += column_sum(value * unit)
        shift_sum[...] += column_sum(value)
        scaled = value * gain
        value = (
            scaled
            - jnp.mean(scaled, axis=-1, keepdims=True)
            - unit * jnp.mean(scaled * unit, axis=-1, keepdims=True)
        )
        value = grad[rows, :] + inverse * value
        grad[rows, :] = value
        if after is not None:
            after(rows, value)

    blocks(source.shape[0] // 32, 32, body)


def outer(left_side, right_side, target, target_rows=None):
    def body(columns):
        target[columns, :] = dot(left_side[:, columns], right_side[...], (0, 0)).astype(BF)

    blocks(left_side.shape[1] // 256, 256, body)


def hidden_grad(branch, down, pre, grad_pre, bias_sum):
    def body(columns):
        value = dot(branch[...], down[columns, :], (1, 1)) * gelu_slope(pre[:, columns])
        low = value.astype(BF)
        grad_pre[:, columns] = low
        bias_sum[:, columns] = column_sum(low.astype(F32))

    blocks(3, 256, body)


KEPT = (
    ("resid", (320, 768), F32),
    ("normed", (640, 768), BF),
    ("query", (320, 768), BF),
    ("key", (640, 768), BF),
    ("value", (640, 768), BF),
    ("log_total", (6, 8, 640), F32),
    ("mixed", (320, 768), BF),
    ("attn", (320, 768), F32),
    ("middle", (320, 768), F32),
    ("normed2", (320, 768), BF),
    ("pre", (4, 320, 768), F32),
    ("hidden", (4, 320, 768), BF),
    ("mlp", (320, 768), F32),
)
KEPT_NAMES = [name for name, _, _ in KEPT]


def forward_kernel(*refs):
    refs = list(refs)

    def take(count):
        got = refs[:count]
        del refs[:count]
        return got

    local = take(COUNT)
    inputs, key_bias, small = take(3)
    params = [take(4), take(4)]
    full = take(COUNT)
    kept_out = [dict(zip(KEPT_NAMES, take(len(KEPT)))) for _ in range(2)]
    (output,) = take(1)
    kept = [{name: ref.at[b] for name, ref in zip(KEPT_NAMES, refs)} for b in range(2)]
    take(len(KEPT))
    attn_w, up_w, down_w, small_in, in_bias, up_bias = take(6)
    send, recv, other, load, store = take(5)
    size = local[0].shape[0] // PARTS
    rows = inputs.shape[0]
    me = lax.rem(lax.axis_index("dp"), PARTS)
    flying = []
    waiting = []

    def part(mask):
        return piece_rows(flip(me, mask), size)

    def slab(i, mask, half=None):
        if half is None:
            return full[i].at[:, part(mask)]
        start = flip(me, mask) * size + half * (size // 2)
        return full[i].at[:, pl.ds(pl.multiple_of(start, size // 2), size // 2)]

    def along_z(i):
        return [
            remote(
                local[i].at[part(0)],
                full[i].at[r - 1, part(0)],
                send.at[i, r - 1],
                recv.at[i, r - 1],
                {"mp": r},
            )
            for r in (1, 2, 3)
        ]

    def along_dp(i, slot, mask, bit, half=None):
        place = slab(i, mask, half)
        return remote(place, place, send.at[i, slot], recv.at[i, slot], {"dp": bit})

    def launch(copies):
        for copy in copies:
            copy.start()
        flying.extend(copies)
        return copies

    def landed(copies):
        for copy in copies:
            copy.wait_recv()

    state = [None] * COUNT

    def stage(i, s):
        if s == 0:
            landed(state[i])
            if i + AHEAD < COUNT:
                state[i + AHEAD] = launch(along_z(i + AHEAD))
            state[i] = launch([along_dp(i, 3, 0, 2), along_dp(i, 4, 0, 4)])
            launch([along_dp(i, 7, 0, 1)])
        elif s == 1:
            landed(state[i])
            state[i] = launch([along_dp(i, 5, 2, 4, 0), along_dp(i, 6, 4, 2, 1)])
            launch([along_dp(i, 8, 2, 1), along_dp(i, 9, 4, 1)])
        elif s == 2:
            landed(state[i])
            launch([along_dp(i, 10, 6, 1)])

    def step(t):
        for s in (0, 1, 2):
            if 0 <= t - s < COUNT:
                stage(t - s, s)

    def complete(i):
        for slot, mask in ((7, 0), (8, 2), (9, 4), (10, 6)):
            along_dp(i, slot, mask, 1).wait_recv()

    def chunk(i, r):
        return local[i] if r == 0 else full[i].at[r - 1]

    def load_attn(i):
        copies = []
        for kind in range(4):
            for r in range(4):
                copies.append(
                    pltpu.make_async_copy(
                        chunk(i, r).at[pl.ds(kind * 192, 192)],
                        attn_w.at[kind, pl.ds(r * 192, 192)],
                        load.at[0, kind * 4 + r],
                    )
                )
        for copy in copies:
            copy.start()
        return copies

    def load_mlp(i, target, slot):
        copies = [
            pltpu.make_async_copy(chunk(i, r), target.at[r], load.at[slot, r]) for r in range(4)
        ]
        for copy in copies:
            copy.start()
        return copies

    def finish(copies):
        for copy in copies:
            copy.wait()

    def save(b, *names):
        for name in names:
            copy = pltpu.make_async_copy(
                kept[b][name], kept_out[b][name], store.at[b, KEPT_NAMES.index(name)]
            )
            copy.start()
            waiting.append(copy)

    def exchange(b):
        copy = remote(
            kept[b]["normed"].at[pl.ds(0, rows)],
            kept[b]["normed"].at[pl.ds(rows, rows)],
            other.at[0, 3 + b],
            other.at[1, 3 + b],
            {"mp": 1},
        )
        return launch([copy])

    enter(lax.axis_size("dp"))
    bias_in = launch(
        [
            remote(small.at[r], small_in.at[r - 1], other.at[0, r - 1], other.at[1, r - 1], {"mp": r})
            for r in (1, 2, 3)
        ]
    )
    for i in range(AHEAD):
        state[i] = launch(along_z(i))

    def widen(part_rows):
        kept[0]["resid"][part_rows, :] = inputs[part_rows, :].astype(F32)

    blocks(10, 32, widen)

    for b in range(2):
        k = kept[b]
        gains, shifts, out_bias, scales = params[b]
        base = 3 * b
        norm_rows(k["resid"], gains[0:1, :], shifts[0:1, :], k["normed"].at[pl.ds(0, rows)])
        save(b, "resid")
        swapped = exchange(b)
        if b == 0:
            step(0)
            step(1)
            step(2)
            landed(bias_in)
            for c in range(2):
                in_bias[c] = small[0, c, 0:8] + small_in[0, c] + small_in[1, c] + small_in[2, c]
                up_bias[c, 0:1] = small[0, c, 0:1]
                for r in (1, 2, 3):
                    up_bias[c, r : r + 1] = small_in[r - 1, c, 0:1]
        complete(base)
        pending = load_attn(base)
        project_bias = in_bias.at[b]
        landed(swapped)
        finish(pending)
        project_rows(k["normed"].at[pl.ds(0, rows)], attn_w.at[0], project_bias.at[pl.ds(1, 1)], k["query"])
        project_rows(k["normed"], attn_w.at[1], None, k["key"])
        project_rows(k["normed"], attn_w.at[2], project_bias.at[pl.ds(2, 1)], k["value"])
        save(b, "normed", "query", "key", "value")
        pair_args = (k["query"], k["key"], k["value"], key_bias, k["mixed"], k["log_total"])
        attend_pairs(0, 3, *pair_args)
        step(3 * b + 3)
        attend_pairs(3, 6, *pair_args)
        save(b, "log_total", "mixed")
        attend_out(
            k["mixed"],
            attn_w.at[3],
            out_bias.at[pl.ds(0, 1)],
            scales.at[pl.ds(0, 1)],
            k["resid"],
            k["attn"],
            k["middle"],
        )
        norm_rows(k["middle"], gains[1:2, :], shifts[1:2, :], k["normed2"])
        save(b, "attn", "middle", "normed2")
        complete(base + 1)
        pending = load_mlp(base + 1, up_w, 1)
        step(3 * b + 4)
        complete(base + 2)
        pending = pending + load_mlp(base + 2, down_w, 2)
        k["mlp"][...] = jnp.broadcast_to(out_bias[1:2, :], k["mlp"].shape)
        finish(pending)
        for r in range(4):
            mlp_chunk(
                r, k["normed2"], up_w, up_bias.at[b], down_w, k["pre"], k["hidden"], k["mlp"]
            )
            if r == 1:
                step(3 * b + 5)
        save(b, "pre", "hidden", "mlp")

        def result(part_rows):
            value = k["middle"][part_rows, :] + scales[1:2, :] * k["mlp"][part_rows, :]
            if b == 0:
                kept[1]["resid"][part_rows, :] = value
            else:
                output[part_rows, :] = value.astype(BF)

        blocks(10, 32, result)
    for copy in flying:
        copy.wait_send()
    finish(waiting)


def forward_all(locals_, inputs, key_bias, small, params):
    anywhere = pl.BlockSpec(memory_space=pl.ANY)
    vmem = pl.BlockSpec(memory_space=pltpu.VMEM)
    matrix = locals_[0].shape
    kept_shapes = [jax.ShapeDtypeStruct(shape, kind) for _, shape, kind in KEPT]
    got = pl.pallas_call(
        forward_kernel,
        out_shape=[jax.ShapeDtypeStruct((3,) + matrix, BF)] * COUNT
        + kept_shapes * 2
        + [jax.ShapeDtypeStruct(inputs.shape, BF)],
        in_specs=[anywhere] * COUNT + [vmem] * 11,
        out_specs=[anywhere] * (COUNT + 2 * len(KEPT)) + [vmem],
        scratch_shapes=[pltpu.VMEM((2,) + shape, kind) for _, shape, kind in KEPT]
        + [
            pltpu.VMEM((4,) + matrix, BF),
            pltpu.VMEM((4,) + matrix, BF),
            pltpu.VMEM((4,) + matrix, BF),
            pltpu.VMEM((3, 2, 8, 768), F32),
            pltpu.VMEM((2, 8, 768), F32),
            pltpu.VMEM((2, 8, 768), F32),
            pltpu.SemaphoreType.DMA((COUNT, 11)),
            pltpu.SemaphoreType.DMA((COUNT, 11)),
            pltpu.SemaphoreType.DMA((2, 5)),
            pltpu.SemaphoreType.DMA((3, 16)),
            pltpu.SemaphoreType.DMA((2, len(KEPT))),
        ],
        compiler_params=pltpu.CompilerParams(
            collective_id=0, has_side_effects=True, vmem_limit_bytes=60 * 1024 * 1024
        ),
    )(*locals_, inputs, key_bias, small, *params)
    full = got[:COUNT]
    kept = [
        dict(zip(KEPT_NAMES, got[COUNT + b * len(KEPT) : COUNT + (b + 1) * len(KEPT)]))
        for b in range(2)
    ]
    return full, kept, got[-1]


RING = 3


def backward_kernel(dp_size, *refs):
    refs = list(refs)

    def take(count):
        got = refs[:count]
        del refs[:count]
        return got

    local = take(COUNT)
    full = take(COUNT)
    kept = [dict(zip(KEPT_NAMES, take(len(KEPT)))) for _ in range(2)]
    cotangent, key_bias = take(2)
    params = [take(2), take(2)]
    (whole, more_in, sums_out, grad_out) = take(4)
    (grad_w, core_in, first_in, second_in, more_stage, z_in, piece) = take(7)
    (up_w, down_w, attn_w) = take(3)
    (grad, buf_p, buf_q, branch, normed2, hidden, pre) = take(7)
    (grad_pre, slope, query, key, value, normed, mixed) = take(7)
    (grad_mixed, grad_query, grad_key, grad_value, log_total) = take(5)
    (away, away_in, sums, sums_in, hidden_sum) = take(5)
    (send, recv, load, store, free, other) = take(6)
    rows = grad.shape[0]
    size = piece.shape[1]
    me = lax.rem(lax.axis_index("dp"), PARTS)
    z = lax.axis_index("mp")
    more = [PARTS << e for e in range((dp_size // PARTS).bit_length() - 1)]

    def part(mask):
        return piece_rows(flip(me, mask), size)

    slots = {}
    pending = {}

    def fetch(name, source, target):
        slot = slots.setdefault(name, len(slots))
        copy = pltpu.make_async_copy(source, target, load.at[slot])
        copy.start()
        pending[name] = copy

    def need(*names):
        for name in names:
            pending.pop(name).wait()

    def fetch_kept(b, name, target):
        fetch(name, kept[b][name], target)

    def chunk(i, r):
        return local[i] if r == 0 else full[i].at[r - 1]

    def fetch_mlp(b, r):
        fetch(("pre", r % 2), kept[b]["pre"].at[r], pre.at[r % 2])
        fetch(("up", r % 2), chunk(3 * b + 1, r), up_w.at[r % 2])
        fetch(("down", r % 2), chunk(3 * b + 2, r), down_w.at[r % 2])

    def fetch_attn(b):
        for kind in range(4):
            for r in range(4):
                fetch(
                    ("attn", kind, r),
                    chunk(3 * b, r).at[pl.ds(kind * 192, 192)],
                    attn_w.at[kind, pl.ds(r * 192, 192)],
                )

    def need_attn(*kinds):
        for kind in kinds:
            need(*[("attn", kind, r) for r in range(4)])

    flying = []
    state = [None] * COUNT
    sent = [[] for _ in range(COUNT)]
    at = [0] * COUNT

    def launch(copies):
        for copy in copies:
            copy.start()
        return copies

    def landed(copies):
        for copy in copies:
            copy.wait_recv()

    def added(left, right):
        left[...] = (left[...].astype(F32) + right[...].astype(F32)).astype(BF)

    def add_slabs(target, source):
        @pl.loop(0, 4)
        def _(r):
            added(target.at[r], source.at[r])

    def add_own(j, high, low):
        own = part(4 * high + 2 * low)

        @pl.loop(0, 4)
        def _(r):
            added(core_in.at[j % RING, high, low, r], grad_w.at[j % 2, r, own])

    owns = []

    def credit(stage, j, bits):
        if j < COUNT:
            pl.semaphore_signal(
                free.at[stage, j], inc=1, device_id=device_at(bits), device_id_type=MESH
            )

    def spend(stage, j):
        if j >= RING:
            pl.semaphore_wait(free.at[stage, j], 1)

    def across(j):
        spend(0, j)
        state[j] = launch(
            [
                remote(
                    grad_w.at[j % 2, :, part(1 | 4 * high | 2 * low)],
                    core_in.at[j % RING, high, low],
                    send.at[j, 2 * high + low],
                    recv.at[j, 2 * high + low],
                    {"dp": 1},
                )
                for high in range(2)
                for low in range(2)
            ]
        )
        sent[j] = list(state[j])

    def reuse(j):
        if j >= 2:
            for copy in sent[j - 2]:
                copy.wait_send()

    def spread(j, slot, mask, bit, half=None):
        if half is None:
            place = whole.at[j, part(mask)]
        else:
            start = flip(me, mask) * size + half * (size // 2)
            place = whole.at[j, pl.ds(pl.multiple_of(start, size // 2), size // 2)]
        source = piece.at[j] if mask == 0 else place
        return remote(source, place, send.at[j, slot], recv.at[j, slot], {"dp": bit})

    def advance(*matrices):
        for j in matrices:
            stage(j, at[j])
            at[j] += 1

    def stage(j, s):
        ring = j % RING
        core = core_in.at[ring]
        half = (pl.ds(0, size // 2), pl.ds(size // 2, size // 2))
        if s == 0:
            landed(state[j])
            spend(1, j)
            spend(3, j)
            add_own(j, 1, 1)
            add_own(j, 0, 1)
            out = [(core.at[:, 1, :, half[0]], 2), (core.at[1, :, :, half[1]], 4)]
            state[j] = []
            for h, (source, bit) in enumerate(out):
                if h == 1:
                    add_own(j, 1, 0)
                state[j] += launch(
                    [
                        remote(
                            source,
                            first_in.at[ring, h],
                            send.at[j, 4 + h],
                            recv.at[j, 4 + h],
                            {"dp": bit},
                        )
                    ]
                )
            flying.extend((j, copy) for copy in state[j])
            add_own(j, 0, 0)
        elif s == 1:
            spend(2, j)
            spend(4, j)
            got = state[j]
            state[j] = []
            for h, bit in enumerate((4, 2)):
                landed(got[h : h + 1])
                away_part = core.at[1, 0, :, half[0]] if h == 0 else core.at[0, 1, :, half[1]]
                add_slabs(away_part, first_in.at[ring, h, 1])
                state[j] += launch(
                    [
                        remote(
                            away_part,
                            second_in.at[ring, h],
                            send.at[j, 6 + h],
                            recv.at[j, 6 + h],
                            {"dp": bit},
                        )
                    ]
                )
            flying.extend((j, copy) for copy in state[j])
            for h in range(2):
                add_slabs(core.at[0, 0, :, half[h]], first_in.at[ring, h, 0])
            for h, bit in enumerate((2, 4)):
                credit(1 + 2 * h, j + RING, {"dp": bit})
        elif s == 2:
            landed(state[j])
            for h in range(2):
                add_slabs(core.at[0, 0, :, half[h]], second_in.at[ring, h])
            for h, bit in enumerate((4, 2)):
                credit(2 + 2 * h, j + RING, {"dp": bit})
            mine = core.at[0, 0]
            for e, bit in enumerate(more):
                copy = remote(
                    mine, more_in.at[j, e], send.at[j, 19 + e], recv.at[j, 19 + e], {"dp": bit}
                )
                copy.start()
                copy.wait()
                back = pltpu.make_async_copy(more_in.at[j, e], more_stage, load.at[LOADS - 1])
                back.start()
                back.wait()
                add_slabs(mine, more_stage)
            state[j] = launch(
                [
                    remote(
                        mine.at[r],
                        z_in.at[j, r - 1],
                        send.at[j, 7 + r],
                        recv.at[j, 7 + r],
                        {"mp": r},
                    )
                    for r in (1, 2, 3)
                ]
            )
            flying.extend((j, copy) for copy in state[j])
        elif s == 3:
            landed(state[j])
            total = core[0, 0, 0].astype(F32)
            for r in range(3):
                total = total + z_in[j, r].astype(F32)
            piece[j] = total.astype(BF)
            state[j] = launch([spread(j, 11, 0, 2), spread(j, 12, 0, 4)])
            core_copy = launch([spread(j, 15, 0, 1)])
            own = pltpu.make_async_copy(piece.at[j], whole.at[j, part(0)], store.at[j])
            own.start()
            owns.append(own)
            if j + RING < COUNT:
                for owner, copy in flying:
                    if owner == j:
                        copy.wait_send()
                flying[:] = [(owner, copy) for owner, copy in flying if owner != j]
                credit(0, j + RING, {"dp": 1})
            flying.extend((j, copy) for copy in state[j] + core_copy)
        elif s == 4:
            landed(state[j])
            state[j] = launch([spread(j, 13, 2, 4, 0), spread(j, 14, 4, 2, 1)])
            core_copies = launch([spread(j, 16, 2, 1), spread(j, 17, 4, 1)])
            flying.extend((j, copy) for copy in state[j] + core_copies)
        elif s == 5:
            landed(state[j])
            core_copies = launch([spread(j, 18, 6, 1)])
            flying.extend((j, copy) for copy in core_copies)
            state[j] = [spread(j, 15 + n, mask, 1) for n, mask in enumerate((0, 2, 4, 6))]
        elif s == 6:
            landed(state[j])

    def start_block(b):
        fetch_kept(b, "mlp", buf_p)
        fetch_kept(b, "hidden", hidden)
        fetch_mlp(b, 0)
        fetch_mlp(b, 1)
        fetch_kept(b, "normed2", normed2)

    def start_attn(b):
        fetch_kept(b, "mixed", mixed)
        fetch_kept(b, "query", query)
        fetch_kept(b, "key", key)
        fetch_kept(b, "value", value)
        fetch_kept(b, "log_total", log_total)

    def sum_of(b, row):
        return sums.at[pl.ds(16 * b + row, 1)]

    def head_sums(b, lane, source, count):
        hidden_sum[...] = jnp.zeros_like(hidden_sum)

        def body(chunk_rows):
            hidden_sum[...] += column_sum(source[chunk_rows, :].astype(F32))

        blocks(count // 32, 32, body)
        for r in range(4):
            row = pl.ds(16 * b + 12 + flip(z, r), 1)
            sums[row, lane : lane + 192] = hidden_sum[:, r * 192 : (r + 1) * 192]

    start_block(1)
    fetch_kept(1, "middle", buf_q)
    start_attn(1)
    fetch_kept(1, "normed", normed)
    fetch_attn(1)
    enter(dp_size)
    sums[...] = jnp.zeros_like(sums)

    def widen(chunk_rows):
        grad[chunk_rows, :] = cotangent[chunk_rows, :].astype(F32)

    blocks(rows // 32, 32, widen)

    for b in (1, 0):
        gains, scales = params[b]
        base = 3 if b == 0 else 0
        plan = PLANS[b]
        need("mlp")
        branch_grad(grad, buf_p, scales[1:2, :], branch, sum_of(b, 7), sum_of(b, 5))
        fetch_kept(b, "attn", buf_p)
        need("hidden")
        reuse(base)
        for r in range(4):
            outer(hidden.at[r], branch, grad_w.at[base % 2, r])
        across(base)
        if b == 1:
            fetch_kept(0, "hidden", hidden)
        advance(*plan[0])
        need("normed2")
        reuse(base + 1)
        for r in range(4):
            need(("pre", r % 2), ("down", r % 2), ("up", r % 2))
            hidden_grad(branch, down_w.at[r % 2], pre.at[r % 2], grad_pre, hidden_sum)
            sums[pl.ds(16 * b + 8 + flip(z, r), 1), :] = hidden_sum[...]
            outer(normed2, grad_pre, grad_w.at[(base + 1) % 2, r])

            def back(columns, r=r):
                part_sum = dot(grad_pre[...], up_w[r % 2, columns, :], (1, 1))
                if r == 0:
                    slope[:, columns] = part_sum
                else:
                    slope[:, columns] += part_sum

            blocks(3, 256, back)
            if r < 2:
                fetch_mlp(b, r + 2)
            elif b == 1:
                fetch_mlp(0, r - 2)
            if r == 1:
                advance(*plan[1])
        across(base + 1)
        if b == 1:
            fetch_kept(0, "normed2", normed2)
        advance(*plan[2])
        need("middle", "attn")
        sum_of(b, 6)[...] = jnp.zeros((1, 768), F32)
        sum_of(b, 4)[...] = jnp.zeros((1, 768), F32)

        def after(chunk_rows, value_rows, b=b, scales=scales):
            sums[16 * b + 6 : 16 * b + 7, :] += column_sum(value_rows * buf_p[chunk_rows, :])
            low = (scales[0:1, :] * value_rows).astype(BF)
            branch[chunk_rows, :] = low
            sums[16 * b + 4 : 16 * b + 5, :] += column_sum(low.astype(F32))

        norm_back(buf_q, slope, gains[1:2, :], grad, sum_of(b, 1), sum_of(b, 3), after)
        fetch_kept(b, "resid", buf_q)
        if b == 1:
            fetch_kept(0, "mlp", buf_p)
        need("mixed")
        need_attn(0, 1, 2, 3)
        project_rows(branch, attn_w.at[3], None, grad_mixed)
        advance(*plan[3])
        need("query", "key", "value", "log_total")
        attn_args = (
            query,
            key,
            value,
            key_bias,
            log_total,
            grad_mixed,
            grad_query,
            grad_key,
            grad_value,
        )
        attend_pairs_back(0, 3, *attn_args)
        advance(*plan[4])
        attend_pairs_back(3, 6, *attn_args)
        advance(*plan[5])
        reuse(base + 2)
        target = grad_w.at[(base + 2) % 2]
        need("normed")

        for kind, left, right in (
            (0, grad_query, normed.at[pl.ds(0, rows)]),
            (1, grad_key, normed),
            (2, grad_value, normed),
            (3, mixed, branch),
        ):
            for h in range(2):
                value_h = dot(left[:, h * 384 : (h + 1) * 384], right[...], (0, 0)).astype(BF)
                for r in range(2):
                    target[2 * h + r, kind * 192 : (kind + 1) * 192, :] = value_h[
                        r * 192 : (r + 1) * 192
                    ]
        across(base + 2)
        head_sums(b, 0, grad_query, rows)
        head_sums(b, 256, grad_value, 2 * rows)

        def give(columns):
            away[b, :, columns] = (
                dot(grad_key[rows:, :], attn_w[1, :, columns])
                + dot(grad_value[rows:, :], attn_w[2, :, columns])
            ).astype(BF)

        blocks(3, 256, give)
        given = launch(
            [remote(away.at[b], away_in.at[b], other.at[0, b], other.at[1, b], {"mp": 1})]
        )
        flying.append((-1, given[0]))

        def keep(columns):
            slope[:, columns] = (
                dot(grad_query[...], attn_w[0, :, columns])
                + dot(grad_key[0:rows, :], attn_w[1, :, columns])
                + dot(grad_value[0:rows, :], attn_w[2, :, columns])
            )

        blocks(3, 256, keep)
        if b == 1:
            start_attn(0)
            fetch_kept(0, "normed", normed)
            fetch_attn(0)
        advance(*plan[6])
        landed(given)

        def join(chunk_rows):
            slope[chunk_rows, :] += away_in[b, chunk_rows, :].astype(F32)

        blocks(rows // 32, 32, join)
        need("resid")
        if b == 1:
            norm_back(buf_q, slope, gains[0:1, :], grad, sum_of(b, 0), sum_of(b, 2))
            fetch_kept(0, "middle", buf_q)
        else:

            def final(chunk_rows, value_rows):
                grad_out[chunk_rows, :] = value_rows.astype(BF)

            norm_back(buf_q, slope, gains[0:1, :], grad, sum_of(b, 0), sum_of(b, 2), final)

    hops = [bits for bits in partners(dp_size) if bits.get("mp") != 3]
    for h, bits in enumerate(hops):
        copy = remote(sums, sums_in.at[h], other.at[0, 2 + h], other.at[1, 2 + h], bits)
        copy.start()
        if h < len(TAIL):
            advance(*TAIL[h])
        copy.wait()
        sums[...] += sums_in[h]
    for tail in TAIL[len(hops) :]:
        advance(*tail)
    sums_out[...] = sums[...]
    for own in owns:
        own.wait()
    for _, copy in flying:
        copy.wait_send()
    for j in (COUNT - 2, COUNT - 1):
        for copy in sent[j]:
            copy.wait_send()


LOADS = 40
PLANS = {
    1: ((), (0,), (), (1, 0), (1, 0), (1, 0), (2,)),
    0: ((2, 1, 0), (3, 2, 1), (2, 0, 3, 1), (4, 2, 0, 3), (4, 3, 2, 1), (4, 3, 2), (5, 4)),
}


def complete_tail():
    at = [0] * COUNT
    for plan in (PLANS[1], PLANS[0]):
        for group in plan:
            for j in group:
                at[j] += 1
    rounds = []
    while min(at) < 7:
        group = [j for j in range(COUNT) if at[j] < 7]
        for j in group:
            at[j] += 1
        rounds.append(tuple(group))
    return tuple(rounds)


TAIL = complete_tail()


def backward_all(locals_, full, kept, cotangent, key_bias, params):
    dp_size = lax.axis_size("dp")
    anywhere = pl.BlockSpec(memory_space=pl.ANY)
    vmem = pl.BlockSpec(memory_space=pltpu.VMEM)
    matrix = locals_[0].shape
    size = matrix[0] // PARTS
    rows = cotangent.shape[0]
    more = (dp_size // PARTS).bit_length() - 1
    more_shape = (COUNT, more, 4, size, 768) if more else (16, 128)
    stage_shape = (4, size, 768) if more else (16, 128)
    shape = jax.ShapeDtypeStruct
    hops = 2 + dp_size.bit_length() - 1
    flat_kept = [kept[b][name] for b in range(2) for name in KEPT_NAMES]
    scratch = [
        ((2, 4) + matrix, BF),
        ((RING, 2, 2, 4, size, 768), BF),
        ((RING, 2, 2, 4, size // 2, 768), BF),
        ((RING, 2, 4, size // 2, 768), BF),
        (stage_shape, BF),
        ((COUNT, 3, size, 768), BF),
        ((COUNT, size, 768), BF),
        ((2,) + matrix, BF),
        ((2,) + matrix, BF),
        ((4,) + matrix, BF),
        ((rows, 768), F32),
        ((rows, 768), F32),
        ((rows, 768), F32),
        ((rows, 768), BF),
        ((rows, 768), BF),
        ((4, rows, 768), BF),
        ((2, rows, 768), F32),
        ((rows, 768), BF),
        ((rows, 768), F32),
        ((rows, 768), BF),
        ((2 * rows, 768), BF),
        ((2 * rows, 768), BF),
        ((2 * rows, 768), BF),
        ((rows, 768), BF),
        ((rows, 768), BF),
        ((rows, 768), BF),
        ((2 * rows, 768), BF),
        ((2 * rows, 768), BF),
        ((6, 8, 2 * rows), F32),
        ((2, rows, 768), BF),
        ((2, rows, 768), BF),
        ((32, 768), F32),
        ((hops, 32, 768), F32),
        ((1, 768), F32),
    ]
    got = pl.pallas_call(
        functools.partial(backward_kernel, dp_size),
        out_shape=[
            shape((COUNT,) + matrix, BF),
            shape(more_shape, BF),
            shape((32, 768), F32),
            shape((rows, 768), BF),
        ],
        in_specs=[anywhere] * (2 * COUNT + 2 * len(KEPT)) + [vmem] * 6,
        out_specs=[anywhere] * 2 + [vmem] * 2,
        scratch_shapes=[pltpu.VMEM(dims, kind) for dims, kind in scratch]
        + [
            pltpu.SemaphoreType.DMA((COUNT, 19 + more)),
            pltpu.SemaphoreType.DMA((COUNT, 19 + more)),
            pltpu.SemaphoreType.DMA((LOADS,)),
            pltpu.SemaphoreType.DMA((COUNT,)),
            pltpu.SemaphoreType.REGULAR((5, COUNT)),
            pltpu.SemaphoreType.DMA((2, 2 + hops)),
        ],
        compiler_params=pltpu.CompilerParams(
            collective_id=1, has_side_effects=True, vmem_limit_bytes=63 * 1024 * 1024
        ),
    )(*locals_, *full, *flat_kept, cotangent, key_bias, *params)
    return got[0], got[2], got[3]


def finish_kernel(whole, sums, *refs):
    passed, outs, refs = refs[:2], refs[2:24], refs[24:]
    low, high, load, store = refs
    z = lax.axis_index("mp")
    loads = [
        pltpu.make_async_copy(whole.at[j], low.at[j], load.at[j]) for j in range(COUNT)
    ]
    for copy in loads:
        copy.start()
    for source, target in zip(passed, outs[:2]):
        target[...] = source[...]
    stores = []

    def keep(source, target):
        copy = pltpu.make_async_copy(source, target, store.at[len(stores)])
        copy.start()
        stores.append(copy)

    for b in range(2):
        project_in, project_out, up, down = outs[2 + 10 * b : 6 + 10 * b]
        gains, shifts, out_bias, scales, up_bias, project_bias = outs[6 + 10 * b : 12 + 10 * b]
        base = 16 * b
        for row, ref in zip((0, 2, 4, 6), (gains, shifts, out_bias, scales)):
            ref[...] = sums[base + row : base + row + 2, :]
        up_bias[...] = sums[pl.ds(base + 8 + z, 1), :]
        mine = sums[pl.ds(base + 12 + z, 1), :]
        project_bias[0:1, :] = mine[:, 0:192]
        project_bias[1:2, :] = mine[:, 256:448]
    for j in range(COUNT):
        b = 1 if j < 3 else 0
        project_in, project_out, up, down = outs[2 + 10 * b : 6 + 10 * b]
        loads[j].wait()

        def widen(chunk_rows):
            high[j, chunk_rows, :] = low[j, chunk_rows, :].astype(F32)

        blocks(8, 96, widen)
        if j % 3 == 0:
            keep(high.at[j], down)
        elif j % 3 == 1:
            keep(high.at[j], up)
        else:
            keep(high.at[j, pl.ds(0, 576)], project_in)
            keep(high.at[j, pl.ds(576, 192)], project_out)
    for copy in stores:
        copy.wait()


def finish_all(whole, sums, output, grad_input):
    anywhere = pl.BlockSpec(memory_space=pl.ANY)
    vmem = pl.BlockSpec(memory_space=pltpu.VMEM)
    shape = jax.ShapeDtypeStruct
    matrix = whole.shape[1:]
    big = [shape((576, 768), F32), shape((192, 768), F32), shape(matrix, F32), shape(matrix, F32)]
    little = [shape((2, 768), F32)] * 4 + [shape((1, 768), F32), shape((2, 192), F32)]
    return pl.pallas_call(
        finish_kernel,
        out_shape=[shape(output.shape, BF)] * 2 + (big + little) * 2,
        in_specs=[anywhere] + [vmem] * 3,
        out_specs=[vmem] * 2 + ([anywhere] * 4 + [vmem] * 6) * 2,
        scratch_shapes=[
            pltpu.VMEM((COUNT,) + matrix, BF),
            pltpu.VMEM((COUNT,) + matrix, F32),
            pltpu.SemaphoreType.DMA((COUNT,)),
            pltpu.SemaphoreType.DMA((COUNT + 2,)),
        ],
        compiler_params=pltpu.CompilerParams(vmem_limit_bytes=60 * 1024 * 1024),
    )(whole, sums, output, grad_input)


def local_block(weights):
    p_in, p_out, up, down = weights[2], weights[4], weights[7], weights[9]
    attn_local = jnp.concatenate([p_in.swapaxes(1, 2).reshape(-1, p_in.shape[1]), p_out])
    return [attn_local, up, down]


def small_rows(weights):
    p_bias, up_bias = weights[3], weights[8]
    width = p_bias.shape[1]
    rows = [
        jnp.concatenate(
            [
                up_bias[None],
                jnp.pad(p_bias, ((0, 0), (r * width, (3 - r) * width))),
                jnp.zeros((5, 4 * width), F32),
            ]
        )
        for r in range(4)
    ]
    return jnp.stack(rows)


def arrange(grads):
    project_in, project_out, up, down = grads[:4]
    gains, shifts, out_bias, scales, up_bias, project_bias = grads[4:]
    return (
        gains,
        shifts,
        project_in.reshape(3, 192, 768).swapaxes(1, 2),
        project_bias,
        project_out,
        out_bias,
        scales,
        up,
        up_bias[0],
        down,
    )


def body(inputs, lengths, cotangent, *params):
    student, teacher = params[:10], params[10:]
    z = lax.axis_index("mp")
    length = lax.dynamic_index_in_dim(lengths, z // 2, 0, keepdims=False)
    rows = inputs.shape[0]
    half = lax.rem(z, 2)
    position = jnp.concatenate(
        [half * rows + jnp.arange(rows), (1 - half) * rows + jnp.arange(rows)]
    )
    key_bias = jnp.where(position < length, 0.0, -1e30).astype(F32)
    locals_ = local_block(student) + local_block(teacher)
    small = jnp.stack([small_rows(student), small_rows(teacher)], axis=1)
    replicated = [weights[p] for weights in (student, teacher) for p in (0, 1, 5, 6)]
    full, kept, output = forward_all(locals_, inputs, key_bias[None], small, replicated)
    needed = [weights[p] for weights in (student, teacher) for p in (0, 6)]
    whole, sums, grad_input = backward_all(
        locals_, full, kept, cotangent, key_bias[:, None], needed
    )
    outs = finish_all(whole, sums, output, grad_input)
    return tuple(outs[:2]) + arrange(outs[2:12]) + arrange(outs[12:22])


def solution(mesh):
    rows = P(("dp", "mp"), None)
    weights = (
        P(),
        P(),
        P(None, None, "mp"),
        P(None, "mp"),
        P("mp", None),
        P(),
        P(),
        P(None, "mp"),
        P("mp"),
        P("mp", None),
    )
    in_specs = (rows, P("dp"), rows) + weights + weights
    out_specs = (rows, rows) + weights + weights
    return jax.shard_map(body, mesh=mesh, in_specs=in_specs, out_specs=out_specs, check_vma=False)
```

```python
import functools

import jax
import jax.numpy as jnp
from jax import lax
from jax.experimental import pallas as pl
from jax.experimental.pallas import tpu as pltpu
from jax.sharding import PartitionSpec as P

HEAD_DIM = 64
SLOT = 640
PARTS = 8
BF = jnp.bfloat16
F32 = jnp.float32

epsilon = 1e-06

MESH = pl.DeviceIdType.MESH
COUNT = 6


def flip(index, bits):
    bit = 1
    while bit <= bits:
        if bits & bit:
            index = index + bit - 2 * bit * lax.rem(lax.div(index, bit), 2)
        bit *= 2
    return index


def partners(dp_size):
    bits = [{"dp": 6}]
    bit = 1
    while bit < dp_size:
        bits.append({"dp": bit})
        bit *= 2
    return bits + [{"mp": r} for r in (1, 2, 3)]


def device_at(bits):
    return {axis: flip(lax.axis_index(axis), bit) for axis, bit in bits.items()}


def enter(dp_size):
    barrier = pltpu.get_barrier_semaphore()
    for bits in partners(dp_size):
        pl.semaphore_signal(barrier, inc=1, device_id=device_at(bits), device_id_type=MESH)
    pl.semaphore_wait(barrier, len(partners(dp_size)))


def remote(source, target, send, recv, bits):
    return pltpu.make_async_remote_copy(
        src_ref=source,
        dst_ref=target,
        send_sem=send,
        recv_sem=recv,
        device_id=device_at(bits),
        device_id_type=MESH,
    )


def piece_rows(index, size):
    return pl.ds(pl.multiple_of(index * size, size), size)


def dot(left_side, right_side, contract=(1, 0)):
    return lax.dot_general(
        left_side,
        right_side,
        (((contract[0],), (contract[1],)), ((), ())),
        preferred_element_type=F32,
    )


def blocks(count, size, body):
    @pl.loop(0, count)
    def _(i):
        body(pl.ds(pl.multiple_of(i * size, size), size))


def norm_parts(values):
    center = values - jnp.mean(values, axis=-1, keepdims=True)
    spread = jnp.mean(center * center, axis=-1, keepdims=True)
    inverse = lax.rsqrt(spread + epsilon)
    return center * inverse, inverse


def norm_rows(source, gain, shift, target):
    def body(rows):
        unit, _ = norm_parts(source[rows, :])
        target[rows, :] = (unit * gain + shift).astype(BF)

    blocks(source.shape[0] // 32, 32, body)


def project_rows(source, weight, bias, target):
    for columns in (slice(0, 384), slice(384, 768)):
        if len(weight.shape) == 2:
            value = weight[columns, :]
        else:
            value = weight[columns.start // 192 : columns.stop // 192].reshape(384, 768)
        value = dot(source[...], value, (1, 1))
        if bias is not None:
            value = value + bias[:, columns]
        target[:, columns] = value.astype(BF)


def low_lanes(shape):
    return lax.broadcasted_iota(jnp.int32, shape, 1) < HEAD_DIM


def two_heads(pair, low):
    nothing = jnp.zeros_like(pair)
    return jnp.concatenate([jnp.where(low, pair, nothing), jnp.where(low, nothing, pair)])


def attend_pairs(first, last, query, key, value, key_bias, mixed, log_total):
    rows = query.shape[0]

    @pl.loop(first, last)
    def _(p):
        lanes = pl.ds(pl.multiple_of(p * 128, 128), 128)
        low = low_lanes((rows, 128))
        both = two_heads(query[:, lanes], low)
        scores = dot(both, key[:, lanes], (1, 1)) * HEAD_DIM ** (-0.5) + key_bias[...]
        peak = jnp.max(scores, axis=1, keepdims=True)
        exponent = jnp.exp(scores - peak)
        total = jnp.sum(exponent, axis=1, keepdims=True)
        probs = (exponent * (1.0 / total)).astype(BF)
        result = dot(probs, value[:, lanes])
        logs = jnp.broadcast_to(peak + jnp.log(total), (2 * rows, 128))
        log_total[p, :, :] = logs.T[0:8, :]
        mixed[:, lanes] = jnp.where(low, result[0:rows], result[rows:]).astype(BF)


def attend_out(mixed, weight, bias, scale, resid, attn, middle):
    def body(columns):
        value = dot(mixed[...], weight[:, :, columns].reshape(768, 256)) + bias[:, columns]
        attn[:, columns] = value
        middle[:, columns] = resid[:, columns] + scale[:, columns] * value

    blocks(3, 256, body)


def gelu_exact(values):
    return 0.5 * values * (1.0 + lax.erf(values * (0.5**0.5)))


def mlp_up(r, normed, up, up_bias, pre, hidden):
    def body(columns):
        value = dot(normed[...], up[r, :, columns]) + up_bias[r : r + 1, columns]
        pre[r, :, columns] = value
        hidden[r, :, columns] = gelu_exact(value).astype(BF)

    blocks(3, 256, body)


def mlp_down(hidden, down, bias, mlp):
    def body(columns):
        value = dot(hidden[0], down[0, :, columns])
        for r in (1, 2, 3):
            value = value + dot(hidden[r], down[r, :, columns])
        mlp[:, columns] = value + bias[:, columns]

    blocks(3, 256, body)


def attend_pairs_back(
    first, last, query, key, value, key_bias, log_total, grad, grad_query, grad_key, grad_value
):
    rows = query.shape[0]
    scale = HEAD_DIM ** (-0.5)

    @pl.loop(first, last)
    def _(p):
        lanes = pl.ds(pl.multiple_of(p * 128, 128), 128)
        low = low_lanes((rows, 128))
        both = two_heads(query[:, lanes], low)
        both_grad = two_heads(grad[:, lanes], low)
        key_pair = key[:, lanes]
        scores = dot(key_pair, both, (1, 1)) * scale + key_bias[...]
        probs = jnp.exp(scores - log_total[p, 0:1, :])
        grad_value[:, lanes] = dot(probs.astype(BF), both_grad).astype(BF)
        grad_probs = dot(value[:, lanes], both_grad, (1, 1))
        inner = jnp.sum(probs * grad_probs, axis=0, keepdims=True)
        grad_scores = (probs * (grad_probs - inner)).astype(BF)
        grad_key[:, lanes] = (dot(grad_scores, both) * scale).astype(BF)
        result = dot(grad_scores, key_pair, (0, 0)) * scale
        grad_query[:, lanes] = jnp.where(low, result[0:rows], result[rows:]).astype(BF)


def gelu_slope(values):
    bell = jnp.exp(-0.5 * values * values) * 0.3989422804014327
    return 0.5 * (1.0 + lax.erf(values * (0.5**0.5))) + values * bell


def column_sum(values):
    return jnp.sum(values, axis=0, keepdims=True)


def branch_grad(grad, mlp, scale, branch, scale_sum, bias_sum):
    scale_sum[...] = jnp.zeros_like(scale_sum)
    bias_sum[...] = jnp.zeros_like(bias_sum)

    def body(rows):
        value = grad[rows, :]
        scale_sum[...] += column_sum(value * mlp[rows, :])
        low = (scale * value).astype(BF)
        branch[rows, :] = low
        bias_sum[...] += column_sum(low.astype(F32))

    blocks(grad.shape[0] // 32, 32, body)


def norm_back(source, slope, gain, grad, gain_sum, shift_sum, after=None):
    gain_sum[...] = jnp.zeros_like(gain_sum)
    shift_sum[...] = jnp.zeros_like(shift_sum)

    def body(rows):
        unit, inverse = norm_parts(source[rows, :])
        value = slope[rows, :]
        gain_sum[...] += column_sum(value * unit)
        shift_sum[...] += column_sum(value)
        scaled = value * gain
        value = (
            scaled
            - jnp.mean(scaled, axis=-1, keepdims=True)
            - unit * jnp.mean(scaled * unit, axis=-1, keepdims=True)
        )
        value = grad[rows, :] + inverse * value
        grad[rows, :] = value
        if after is not None:
            after(rows, value)

    blocks(source.shape[0] // 32, 32, body)


def outer(left_side, right_side, target, target_rows=None):
    def body(columns):
        target[columns, :] = dot(left_side[:, columns], right_side[...], (0, 0)).astype(BF)

    blocks(left_side.shape[1] // 256, 256, body)


def hidden_grad(branch, down, pre, grad_pre, bias_sum):
    def body(columns):
        value = dot(branch[...], down[columns, :], (1, 1)) * gelu_slope(pre[:, columns])
        low = value.astype(BF)
        grad_pre[:, columns] = low
        bias_sum[:, columns] = column_sum(low.astype(F32))

    blocks(3, 256, body)


KEPT = (
    ("resid", (320, 768), F32),
    ("normed", (640, 768), BF),
    ("query", (320, 768), BF),
    ("key", (640, 768), BF),
    ("value", (640, 768), BF),
    ("log_total", (6, 8, 640), F32),
    ("mixed", (320, 768), BF),
    ("attn", (320, 768), F32),
    ("middle", (320, 768), F32),
    ("normed2", (320, 768), BF),
    ("pre", (4, 320, 768), F32),
    ("hidden", (4, 320, 768), BF),
    ("mlp", (320, 768), F32),
)
KEPT_NAMES = [name for name, _, _ in KEPT]


FORWARD_PLAN = (
    (),
    (0,),
    (),
    (),
    (0, 1, 0, 2, 1, 0, 3),
    (),
    (),
    (1, 2),
    (4,),
    (),
    (),
    (3, 2),
    (5, 1),
    (),
    (),
    (),
    (),
    (4, 2),
    (),
    (),
    (3,),
    (),
    (),
    (),
    (5, 3),
    (4,),
    (),
    (),
    (5,),
    (),
    (),
    (),
    (5, 4),
    (),
    (),
    (),
    (),
    (),
    (),
    (),
    (),
    (),
    (),
)


def attn_chunk(local, full, i, r, kind):
    if r:
        return full[i].at[r - 1, pl.ds(kind * 192, 192)]
    project_in, project_out = local[i // 3][:2]
    return project_in.at[pl.ds(kind * 192, 192)] if kind < 3 else project_out


def forward_kernel(*refs):
    refs = list(refs)

    def take(count):
        got = refs[:count]
        del refs[:count]
        return got

    local = [take(4), take(4)]
    inputs, lengths = take(2)
    params = [take(6), take(6)]
    full = take(COUNT)
    kept_out = [dict(zip(KEPT_NAMES, take(len(KEPT)))) for _ in range(2)]
    (output,) = take(1)
    kept = [{name: ref.at[b] for name, ref in zip(KEPT_NAMES, refs)} for b in range(2)]
    take(len(KEPT))
    attn_w, up_w, down_w, small, small_in, key_bias, in_bias, up_bias = take(8)
    send, recv, other, load, store = take(5)
    size = full[0].shape[1] // PARTS
    rows = inputs.shape[0]
    me = lax.rem(lax.axis_index("dp"), PARTS)
    z = lax.axis_index("mp")
    flying = []
    waiting = []

    def part(mask):
        return piece_rows(flip(me, mask), size)

    def place(i, chunks, mask, half=None):
        b, kind = divmod(i, 3)
        index = flip(me, mask)
        start, count = index * size, size
        if kind == 0:
            start = lax.rem(index, 2) * size
        if half is not None:
            start, count = start + half * (size // 2), size // 2
        where = pl.ds(pl.multiple_of(start, count), count)
        if kind == 0:
            return attn_w.at[b, lax.div(index, 2), chunks, where]
        return (up_w if kind == 1 else down_w).at[b, chunks, where]

    def slab(i, mask, half=None):
        return place(i, pl.ds(1, 3), mask, half)

    def along_z(i):
        b, kind = divmod(i, 3)

        def copies(source, rows_of):
            return [
                remote(
                    source.at[rows_of],
                    place(i, r, 0),
                    send.at[i, r - 1],
                    recv.at[i, r - 1],
                    {"mp": r},
                )
                for r in (1, 2, 3)
            ]

        if kind:
            return launch(copies(local[b][1 + kind], part(0)))
        project_in, project_out = local[b][:2]
        inner = project_in.shape[0] // size

        @pl.when(me < inner)
        def _():
            for copy in copies(project_in, part(0)):
                copy.start()

        @pl.when(me >= inner)
        def _():
            for copy in copies(project_out, piece_rows(lax.max(me - inner, 0), size)):
                copy.start()

        started = copies(project_out, pl.ds(0, size))
        flying.extend(started)
        return started

    def along_dp(i, slot, mask, bit, half=None):
        there = slab(i, mask, half)
        return remote(there, there, send.at[i, slot], recv.at[i, slot], {"dp": bit})

    def launch(copies):
        for copy in copies:
            copy.start()
        flying.extend(copies)
        return copies

    def landed(copies):
        for copy in copies:
            copy.wait_recv()

    state = [None] * COUNT

    at = [0] * COUNT
    plan = iter(FORWARD_PLAN)

    def slot():
        for i in next(plan):
            stage(i, at[i])
            at[i] += 1

    def stage(i, s):
        if s == 0:
            state[i] = along_z(i)
        elif s == 1:
            landed(state[i])
            state[i] = launch([along_dp(i, 3, 0, 2), along_dp(i, 4, 0, 4)])
            launch([along_dp(i, 7, 0, 1)])
        elif s == 2:
            landed(state[i])
            state[i] = launch([along_dp(i, 5, 2, 4, 0), along_dp(i, 6, 4, 2, 1)])
            launch([along_dp(i, 8, 2, 1), along_dp(i, 9, 4, 1)])
        elif s == 3:
            landed(state[i])
            launch([along_dp(i, 10, 6, 1)])

    def complete(i):
        for slot, mask in ((7, 0), (8, 2), (9, 4), (10, 6)):
            along_dp(i, slot, mask, 1).wait_recv()
        b, kind = divmod(i, 3)
        finish(owned[b][:4] if kind == 0 else owned[b][3 + kind : 4 + kind])
        save_full(i)

    def load_own():
        for b in range(2):
            project_in, project_out, up, down = local[b]
            copies = [
                pltpu.make_async_copy(
                    project_in.at[pl.ds(kind * 192, 192)], attn_w.at[b, kind, 0], load.at[b, kind]
                )
                for kind in range(3)
            ]
            copies += [
                pltpu.make_async_copy(project_out, attn_w.at[b, 3, 0], load.at[b, 3]),
                pltpu.make_async_copy(up, up_w.at[b, 0], load.at[b, 4]),
                pltpu.make_async_copy(down, down_w.at[b, 0], load.at[b, 5]),
            ]
            for copy in copies:
                copy.start()
            owned.append(copies)

    def save_full(i):
        b, kind = divmod(i, 3)
        if kind == 0:
            copies = [
                pltpu.make_async_copy(
                    attn_w.at[b, n, pl.ds(1, 3)],
                    full[i].at[:, pl.ds(n * 192, 192)],
                    load.at[b, 6 + n],
                )
                for n in range(4)
            ]
        else:
            source = up_w if kind == 1 else down_w
            copies = [
                pltpu.make_async_copy(source.at[b, pl.ds(1, 3)], full[i], load.at[b, 9 + kind])
            ]
        for copy in copies:
            copy.start()
        waiting.extend(copies)

    owned = []

    def finish(copies):
        for copy in copies:
            copy.wait()

    def save(b, *names):
        for name in names:
            copy = pltpu.make_async_copy(
                kept[b][name], kept_out[b][name], store.at[b, KEPT_NAMES.index(name)]
            )
            copy.start()
            waiting.append(copy)

    def exchange(b):
        copy = remote(
            kept[b]["normed"].at[pl.ds(0, rows)],
            kept[b]["normed"].at[pl.ds(rows, rows)],
            other.at[0, 3 + b],
            other.at[1, 3 + b],
            {"mp": 1},
        )
        return launch([copy])

    load_own()
    enter(lax.axis_size("dp"))
    slot()
    slot()
    for b in range(2):
        small[:, b] = jnp.zeros((4, 8, 768), F32)
        project_bias, hidden_bias = params[b][4:]
        for r in range(4):
            small[r, b, 0:1, :] = hidden_bias[...].reshape(1, 768)
            small[r, b, 1:3, r * 192 : (r + 1) * 192] = project_bias[...]
    bias_in = launch(
        [
            remote(small.at[r], small_in.at[r - 1], other.at[0, r - 1], other.at[1, r - 1], {"mp": r})
            for r in (1, 2, 3)
        ]
    )

    def widen(part_rows):
        kept[0]["resid"][part_rows, :] = inputs[part_rows, :].astype(F32)

    blocks(10, 32, widen)
    position = lax.broadcasted_iota(jnp.int32, (1, 2 * rows), 1)
    shifted = position + lax.rem(z, 2) * jnp.where(position < rows, rows, -rows)
    key_bias[...] = jnp.where(shifted < lengths[lax.div(z, 2)], 0.0, -1e30).astype(F32)

    def first_norm(b):
        gains, shifts = params[b][:2]
        k = kept[b]
        slot()
        norm_rows(k["resid"], gains[0:1, :], shifts[0:1, :], k["normed"].at[pl.ds(0, rows)])
        save(b, "resid")

    first_norm(0)
    for b in range(2):
        k = kept[b]
        gains, shifts, out_bias, scales = params[b][:4]
        base = 3 * b
        slot()
        swapped = exchange(b)
        slot()
        complete(base)
        if b == 0:
            landed(bias_in)
            for c in range(2):
                in_bias[c] = small[0, c] + small_in[0, c] + small_in[1, c] + small_in[2, c]
                up_bias[c, 0:1] = small[0, c, 0:1]
                for r in (1, 2, 3):
                    up_bias[c, r : r + 1] = small_in[r - 1, c, 0:1]
        project_bias = in_bias.at[b]
        slot()
        landed(swapped)
        slot()
        project_rows(
            k["normed"].at[pl.ds(0, rows)],
            attn_w.at[b, 0],
            project_bias.at[pl.ds(1, 1)],
            k["query"],
        )
        slot()
        project_rows(k["normed"], attn_w.at[b, 1], None, k["key"])
        slot()
        project_rows(k["normed"], attn_w.at[b, 2], project_bias.at[pl.ds(2, 1)], k["value"])
        save(b, "normed", "query", "key", "value")
        pair_args = (k["query"], k["key"], k["value"], key_bias, k["mixed"], k["log_total"])
        for pair in (0, 2, 4):
            slot()
            attend_pairs(pair, pair + 2, *pair_args)
        save(b, "log_total", "mixed")
        slot()
        attend_out(
            k["mixed"],
            attn_w.at[b, 3],
            out_bias.at[pl.ds(0, 1)],
            scales.at[pl.ds(0, 1)],
            k["resid"],
            k["attn"],
            k["middle"],
        )
        slot()
        norm_rows(k["middle"], gains[1:2, :], shifts[1:2, :], k["normed2"])
        save(b, "attn", "middle", "normed2")
        slot()
        complete(base + 1)
        for r in range(4):
            slot()
            mlp_up(r, k["normed2"], up_w.at[b], up_bias.at[b], k["pre"], k["hidden"])
        save(b, "pre", "hidden")
        slot()
        complete(base + 2)
        slot()
        mlp_down(k["hidden"], down_w.at[b], out_bias.at[pl.ds(1, 1)], k["mlp"])
        save(b, "mlp")
        slot()

        def result(part_rows):
            value = k["middle"][part_rows, :] + scales[1:2, :] * k["mlp"][part_rows, :]
            if b == 0:
                kept[1]["resid"][part_rows, :] = value
            else:
                output[part_rows, :] = value.astype(BF)

        blocks(10, 32, result)
        if b == 0:
            first_norm(1)
    slot()
    for copy in flying:
        copy.wait_send()
    finish(waiting)


def forward_all(locals_, inputs, lengths, params):
    anywhere = pl.BlockSpec(memory_space=pl.ANY)
    vmem = pl.BlockSpec(memory_space=pltpu.VMEM)
    smem = pl.BlockSpec(memory_space=pltpu.SMEM)
    matrix = locals_[2].shape
    kept_shapes = [jax.ShapeDtypeStruct(shape, kind) for _, shape, kind in KEPT]
    got = pl.pallas_call(
        forward_kernel,
        out_shape=[jax.ShapeDtypeStruct((3,) + matrix, BF)] * COUNT
        + kept_shapes * 2
        + [jax.ShapeDtypeStruct(inputs.shape, BF)],
        in_specs=[anywhere] * 8 + [vmem, smem] + [vmem] * 12,
        out_specs=[anywhere] * (COUNT + 2 * len(KEPT)) + [vmem],
        scratch_shapes=[pltpu.VMEM((2,) + shape, kind) for _, shape, kind in KEPT]
        + [
            pltpu.VMEM((2, 4, 4, 192, 768), BF),
            pltpu.VMEM((2, 4) + matrix, BF),
            pltpu.VMEM((2, 4) + matrix, BF),
            pltpu.VMEM((4, 2, 8, 768), F32),
            pltpu.VMEM((3, 2, 8, 768), F32),
            pltpu.VMEM((1, 2 * inputs.shape[0]), F32),
            pltpu.VMEM((2, 8, 768), F32),
            pltpu.VMEM((2, 8, 768), F32),
            pltpu.SemaphoreType.DMA((COUNT, 11)),
            pltpu.SemaphoreType.DMA((COUNT, 11)),
            pltpu.SemaphoreType.DMA((2, 5)),
            pltpu.SemaphoreType.DMA((2, 12)),
            pltpu.SemaphoreType.DMA((2, len(KEPT))),
        ],
        compiler_params=pltpu.CompilerParams(
            collective_id=0, has_side_effects=True, vmem_limit_bytes=63 * 1024 * 1024
        ),
    )(*locals_, inputs, lengths, *params)
    full = got[:COUNT]
    kept = [
        dict(zip(KEPT_NAMES, got[COUNT + b * len(KEPT) : COUNT + (b + 1) * len(KEPT)]))
        for b in range(2)
    ]
    return full, kept, got[-1]


RING = 3


def backward_kernel(dp_size, *refs):
    refs = list(refs)

    def take(count):
        got = refs[:count]
        del refs[:count]
        return got

    local = [take(4), take(4)]
    full = take(COUNT)
    kept = [dict(zip(KEPT_NAMES, take(len(KEPT)))) for _ in range(2)]
    cotangent, lengths = take(2)
    params = [take(2), take(2)]
    (whole, more_in, sums_out, grad_out) = take(4)
    (grad_w, core_in, first_in, second_in, more_stage, z_in, piece) = take(7)
    (up_w, down_w, attn_w) = take(3)
    (grad, buf_p, buf_q, branch, normed2, hidden, pre) = take(7)
    (grad_pre, slope, query, key, value, normed, mixed) = take(7)
    (grad_mixed, grad_query, grad_key, grad_value, log_total) = take(5)
    (away, away_in, sums, sums_in, hidden_sum, key_bias) = take(6)
    (send, recv, load, store, free, other) = take(6)
    rows = grad.shape[0]
    size = piece.shape[1]
    me = lax.rem(lax.axis_index("dp"), PARTS)
    z = lax.axis_index("mp")
    more = [PARTS << e for e in range((dp_size // PARTS).bit_length() - 1)]

    def part(mask):
        return piece_rows(flip(me, mask), size)

    slots = {}
    pending = {}

    def fetch(name, source, target):
        slot = slots.setdefault(name, len(slots))
        copy = pltpu.make_async_copy(source, target, load.at[slot])
        copy.start()
        pending[name] = copy

    def need(*names):
        for name in names:
            pending.pop(name).wait()

    def fetch_kept(b, name, target):
        fetch(name, kept[b][name], target)

    def chunk(i, r):
        return local[i // 3][1 + i % 3] if r == 0 else full[i].at[r - 1]

    def fetch_mlp(b, r):
        fetch(("pre", r % 2), kept[b]["pre"].at[r], pre.at[r % 2])
        fetch(("up", r % 2), chunk(3 * b + 1, r), up_w.at[r % 2])
        fetch(("down", r % 2), chunk(3 * b + 2, r), down_w.at[r % 2])

    def fetch_attn(b):
        for kind in range(4):
            for r in range(4):
                fetch(
                    ("attn", kind, r),
                    attn_chunk(local, full, 3 * b, r, kind),
                    attn_w.at[kind, pl.ds(r * 192, 192)],
                )

    def need_attn(*kinds):
        for kind in kinds:
            need(*[("attn", kind, r) for r in range(4)])

    flying = []
    state = [None] * (COUNT + 2)
    sent = [[] for _ in range(COUNT)]
    at = [0] * (COUNT + 2)

    def launch(copies):
        for copy in copies:
            copy.start()
        return copies

    def landed(copies):
        for copy in copies:
            copy.wait_recv()

    def added(left, right):
        left[...] = (left[...].astype(F32) + right[...].astype(F32)).astype(BF)

    def add_slabs(target, source):
        @pl.loop(0, 4)
        def _(r):
            added(target.at[r], source.at[r])

    half = [pl.ds(0, size // 2), pl.ds(size // 2, size // 2)]

    def add_own(j, high, low):
        own = part(4 * high + 2 * low)

        @pl.loop(0, 4)
        def _(r):
            added(core_in.at[j % RING, high, low, r], grad_w.at[j % 2, r, own])

    owns = []

    def credit(stage, j, bits):
        if j < COUNT:
            pl.semaphore_signal(
                free.at[stage, j], inc=1, device_id=device_at(bits), device_id_type=MESH
            )

    def spend(stage, j):
        if j >= RING:
            pl.semaphore_wait(free.at[stage, j], 1)

    def across(j):
        spend(0, j)
        state[j] = launch(
            [
                remote(
                    grad_w.at[j % 2, :, part(1 | 4 * high | 2 * low)],
                    core_in.at[j % RING, high, low],
                    send.at[j, 2 * high + low],
                    recv.at[j, 2 * high + low],
                    {"dp": 1},
                )
                for high in range(2)
                for low in range(2)
            ]
        )
        sent[j] = list(state[j])

    def reuse(j):
        if j >= 2:
            for copy in sent[j - 2]:
                copy.wait_send()

    def spread(j, slot, mask, bit, half=None):
        if half is None:
            place = whole.at[j, part(mask)]
        else:
            start = flip(me, mask) * size + half * (size // 2)
            place = whole.at[j, pl.ds(pl.multiple_of(start, size // 2), size // 2)]
        source = piece.at[j] if mask == 0 else place
        return remote(source, place, send.at[j, slot], recv.at[j, slot], {"dp": bit})

    def advance(*matrices):
        for j in matrices:
            (stage if j < COUNT else sum_stage)(j, at[j])
            at[j] += 1

    def send_out(j, slot, source, target, bits):
        copies = launch([remote(source, target, send.at[j, slot], recv.at[j, slot], bits)])
        flying.extend((j, copy) for copy in copies)
        return copies[0]

    def stage(j, s):
        core = core_in.at[j % RING]
        if s == 0:
            landed(state[j])
            add_own(j, 1, 1)
            add_own(j, 0, 1)
            state[j] = [
                send_out(j, 4, core.at[:, 1, :, half[0]], first_in.at[j, 0], {"dp": 2})
            ]
            add_own(j, 1, 0)
            state[j].append(
                send_out(j, 5, core.at[1, :, :, half[1]], first_in.at[j, 1], {"dp": 4})
            )
            add_own(j, 0, 0)
        elif s == 1:
            got = state[j]
            state[j] = []
            for h, bit in enumerate((4, 2)):
                landed(got[h : h + 1])
                away_part = core.at[1, 0, :, half[0]] if h == 0 else core.at[0, 1, :, half[1]]
                add_slabs(away_part, first_in.at[j, h, 1])
                state[j].append(
                    send_out(j, 6 + h, away_part, second_in.at[j, h], {"dp": bit})
                )
            for h in range(2):
                add_slabs(core.at[0, 0, :, half[h]], first_in.at[j, h, 0])
        elif s == 2:
            landed(state[j])
            for h in range(2):
                add_slabs(core.at[0, 0, :, half[h]], second_in.at[j, h])
            mine = core.at[0, 0]
            for e, bit in enumerate(more):
                copy = remote(
                    mine, more_in.at[j, e], send.at[j, 19 + e], recv.at[j, 19 + e], {"dp": bit}
                )
                copy.start()
                copy.wait()
                back = pltpu.make_async_copy(more_in.at[j, e], more_stage, load.at[LOADS - 1])
                back.start()
                back.wait()
                add_slabs(mine, more_stage)
            state[j] = [
                send_out(j, 7 + r, mine.at[r], z_in.at[j, r - 1], {"mp": r}) for r in (1, 2, 3)
            ]
        elif s == 3:
            landed(state[j])
            total = core[0, 0, 0].astype(F32)
            for r in range(3):
                total = total + z_in[j, r].astype(F32)
            piece[j] = total.astype(BF)
            state[j] = launch([spread(j, 11, 0, 2), spread(j, 12, 0, 4)])
            core_copy = launch([spread(j, 15, 0, 1)])
            own = pltpu.make_async_copy(piece.at[j], whole.at[j, part(0)], store.at[j])
            own.start()
            owns.append(own)
            if j + RING < COUNT:
                for owner, copy in flying:
                    if owner == j:
                        copy.wait_send()
                flying[:] = [(owner, copy) for owner, copy in flying if owner != j]
                credit(0, j + RING, {"dp": 1})
            flying.extend((j, copy) for copy in state[j] + core_copy)
        elif s == 5:
            landed(state[j])
            state[j] = launch([spread(j, 13, 2, 4, 0), spread(j, 14, 4, 2, 1)])
            core_copies = launch([spread(j, 16, 2, 1), spread(j, 17, 4, 1)])
            flying.extend((j, copy) for copy in state[j] + core_copies)
        elif s == 6:
            landed(state[j])
            core_copies = launch([spread(j, 18, 6, 1)])
            flying.extend((j, copy) for copy in core_copies)
            state[j] = [spread(j, 15 + n, mask, 1) for n, mask in enumerate((0, 2, 4, 6))]
        elif s == 7:
            landed(state[j])

    def sum_send(b, step, bits):
        place = 2 * EXCHANGE + (SUM_STEPS + len(more)) * b + step
        copy = remote(
            sums.at[pl.ds(16 * b, 16)],
            sums_in.at[b, step],
            other.at[0, place],
            other.at[1, place],
            bits,
        )
        copy.start()
        return copy

    def sum_stage(j, s):
        b = 7 - j
        mine = sums.at[pl.ds(16 * b, 16)]
        if s:
            for copy in state[j]:
                copy.wait()
        if s == 0:
            state[j] = [sum_send(b, r - 1, {"mp": r}) for r in (1, 2, 3)]
        elif s == 1:
            mine[...] = (mine[...] + sums_in[b, 0]) + (sums_in[b, 1] + sums_in[b, 2])
            state[j] = [sum_send(b, 3, {"dp": 1})]
        elif s == 2:
            mine[...] += sums_in[b, 3]
            for e, bit in enumerate(more):
                sum_send(b, SUM_STEPS + e, {"dp": bit}).wait()
                mine[...] += sums_in[b, SUM_STEPS + e]
            state[j] = [sum_send(b, 3 + n, {"dp": 2 * n}) for n in (1, 2, 3)]
        elif s == 3:
            mine[...] = (mine[...] + sums_in[b, 4]) + (sums_in[b, 5] + sums_in[b, 6])

    def start_block(b):
        fetch_kept(b, "mlp", buf_p)
        fetch_kept(b, "hidden", hidden)
        fetch_mlp(b, 0)
        fetch_mlp(b, 1)
        fetch_kept(b, "normed2", normed2)

    def start_attn(b):
        fetch_kept(b, "mixed", mixed)
        fetch_kept(b, "query", query)
        fetch_kept(b, "key", key)
        fetch_kept(b, "value", value)
        fetch_kept(b, "log_total", log_total)

    def sum_of(b, row):
        return sums.at[pl.ds(16 * b + row, 1)]

    def head_sums(b, lane, source, count):
        hidden_sum[...] = jnp.zeros_like(hidden_sum)

        def body(chunk_rows):
            hidden_sum[...] += column_sum(source[chunk_rows, :].astype(F32))

        blocks(count // 32, 32, body)
        for r in range(4):
            row = pl.ds(16 * b + 12 + flip(z, r), 1)
            sums[row, lane : lane + 192] = hidden_sum[:, r * 192 : (r + 1) * 192]

    start_block(1)
    fetch_kept(1, "middle", buf_q)
    start_attn(1)
    fetch_kept(1, "normed", normed)
    fetch_attn(1)
    enter(dp_size)
    sums[...] = jnp.zeros_like(sums)
    position = lax.broadcasted_iota(jnp.int32, (2 * rows, 1), 0)
    shifted = position + lax.rem(z, 2) * jnp.where(position < rows, rows, -rows)
    key_bias[...] = jnp.where(shifted < lengths[lax.div(z, 2)], 0.0, -1e30).astype(F32)

    plan = iter(PLAN)

    def slot():
        advance(*next(plan))

    slot()

    def widen(chunk_rows):
        grad[chunk_rows, :] = cotangent[chunk_rows, :].astype(F32)

    blocks(rows // 32, 32, widen)

    for b in (1, 0):
        gains, scales = params[b]
        base = 3 if b == 0 else 0
        slot()
        need("mlp")
        branch_grad(grad, buf_p, scales[1:2, :], branch, sum_of(b, 7), sum_of(b, 5))
        fetch_kept(b, "attn", buf_p)
        need("hidden")
        slot()
        reuse(base)
        for r in range(4):
            if r % 2 == 0:
                slot()
            outer(hidden.at[r], branch, grad_w.at[base % 2, r])
        slot()
        across(base)
        if b == 1:
            fetch_kept(0, "hidden", hidden)
        need("normed2")
        slot()
        reuse(base + 1)
        for r in range(4):
            slot()
            need(("pre", r % 2), ("down", r % 2), ("up", r % 2))
            hidden_grad(branch, down_w.at[r % 2], pre.at[r % 2], grad_pre, hidden_sum)
            sums[pl.ds(16 * b + 8 + flip(z, r), 1), :] = hidden_sum[...]
            outer(normed2, grad_pre, grad_w.at[(base + 1) % 2, r])

            def back(columns, r=r):
                part_sum = dot(grad_pre[...], up_w[r % 2, columns, :], (1, 1))
                if r == 0:
                    slope[:, columns] = part_sum
                else:
                    slope[:, columns] += part_sum

            blocks(3, 256, back)
            if r < 2:
                fetch_mlp(b, r + 2)
            elif b == 1:
                fetch_mlp(0, r - 2)
        slot()
        across(base + 1)
        if b == 1:
            fetch_kept(0, "normed2", normed2)
        slot()
        need("middle", "attn")
        sum_of(b, 6)[...] = jnp.zeros((1, 768), F32)
        sum_of(b, 4)[...] = jnp.zeros((1, 768), F32)

        def after(chunk_rows, value_rows, b=b, scales=scales):
            sums[16 * b + 6 : 16 * b + 7, :] += column_sum(value_rows * buf_p[chunk_rows, :])
            low = (scales[0:1, :] * value_rows).astype(BF)
            branch[chunk_rows, :] = low
            sums[16 * b + 4 : 16 * b + 5, :] += column_sum(low.astype(F32))

        norm_back(buf_q, slope, gains[1:2, :], grad, sum_of(b, 1), sum_of(b, 3), after)
        fetch_kept(b, "resid", buf_q)
        if b == 1:
            fetch_kept(0, "mlp", buf_p)
        slot()
        need("mixed")
        need_attn(0, 1, 2, 3)
        project_rows(branch, attn_w.at[3], None, grad_mixed)
        need("query", "key", "value", "log_total")
        attn_args = (
            query,
            key,
            value,
            key_bias,
            log_total,
            grad_mixed,
            grad_query,
            grad_key,
            grad_value,
        )
        for pair in (0, 2, 4):
            slot()
            attend_pairs_back(pair, pair + 2, *attn_args)
        slot()

        def give(columns):
            away[b, :, columns] = (
                dot(grad_key[rows:, :], attn_w[1, :, columns])
                + dot(grad_value[rows:, :], attn_w[2, :, columns])
            ).astype(BF)

        blocks(3, 256, give)
        slot()
        given = launch(
            [
                remote(
                    away.at[b, pl.ds(n * rows // EXCHANGE, rows // EXCHANGE)],
                    away_in.at[b, pl.ds(n * rows // EXCHANGE, rows // EXCHANGE)],
                    other.at[0, b * EXCHANGE + n],
                    other.at[1, b * EXCHANGE + n],
                    {"mp": 1},
                )
                for n in range(EXCHANGE)
            ]
        )
        flying.extend((-1, copy) for copy in given)
        slot()
        reuse(base + 2)
        target = grad_w.at[(base + 2) % 2]
        need("normed")
        for kind, left, right in (
            (0, grad_query, normed.at[pl.ds(0, rows)]),
            (1, grad_key, normed),
            (2, grad_value, normed),
            (3, mixed, branch),
        ):
            if kind % 2 == 0:
                slot()
            for h in range(2):
                value_h = dot(left[:, h * 384 : (h + 1) * 384], right[...], (0, 0)).astype(BF)
                for r in range(2):
                    target[2 * h + r, kind * 192 : (kind + 1) * 192, :] = value_h[
                        r * 192 : (r + 1) * 192
                    ]
        slot()
        across(base + 2)
        slot()
        head_sums(b, 0, grad_query, rows)
        head_sums(b, 256, grad_value, 2 * rows)
        slot()

        def keep(columns):
            slope[:, columns] = (
                dot(grad_query[...], attn_w[0, :, columns])
                + dot(grad_key[0:rows, :], attn_w[1, :, columns])
                + dot(grad_value[0:rows, :], attn_w[2, :, columns])
            )

        blocks(3, 256, keep)
        if b == 1:
            start_attn(0)
            fetch_kept(0, "normed", normed)
            fetch_attn(0)
        slot()
        landed(given)
        slot()

        def join(chunk_rows):
            slope[chunk_rows, :] += away_in[b, chunk_rows, :].astype(F32)

        blocks(rows // 32, 32, join)
        need("resid")
        if b == 1:
            norm_back(buf_q, slope, gains[0:1, :], grad, sum_of(b, 0), sum_of(b, 2))
            fetch_kept(0, "middle", buf_q)
        else:

            def final(chunk_rows, value_rows):
                grad_out[chunk_rows, :] = value_rows.astype(BF)

            norm_back(buf_q, slope, gains[0:1, :], grad, sum_of(b, 0), sum_of(b, 2), final)

        slot()
    slot()
    sums_out[...] = sums[...]
    for own in owns:
        own.wait()
    for _, copy in flying:
        copy.wait_send()
    for j in (COUNT - 2, COUNT - 1):
        for copy in sent[j]:
            copy.wait_send()


LOADS = 40
EXCHANGE = 1
SUM_STEPS = 7
PLAN = (
    (),
    (),
    (),
    (),
    (),
    (),
    (),
    (),
    (),
    (0,),
    (),
    (),
    (),
    (),
    (),
    (0, 1),
    (),
    (),
    (),
    (),
    (),
    (),
    (),
    (),
    (0, 1, 2),
    (0,),
    (0,),
    (),
    (),
    (6,),
    (),
    (),
    (),
    (0, 1),
    (),
    (2,),
    (3, 6),
    (6,),
    (1, 1, 2),
    (),
    (),
    (),
    (0, 4, 1),
    (),
    (),
    (),
    (6, 0, 3, 2),
    (2,),
    (1,),
    (),
    (),
    (),
    (1, 5),
    (),
    (),
    (7, 4, 3, 4, 2, 5, 5, 7, 2, 7, 3, 7, 4, 3, 4, 3, 2, 4, 5, 3, 5, 3, 5, 4, 5, 4, 5),
)


def backward_all(locals_, full, kept, cotangent, lengths, params):
    dp_size = lax.axis_size("dp")
    anywhere = pl.BlockSpec(memory_space=pl.ANY)
    vmem = pl.BlockSpec(memory_space=pltpu.VMEM)
    smem = pl.BlockSpec(memory_space=pltpu.SMEM)
    matrix = locals_[2].shape
    size = matrix[0] // PARTS
    rows = cotangent.shape[0]
    more = (dp_size // PARTS).bit_length() - 1
    more_shape = (COUNT, more, 4, size, 768) if more else (16, 128)
    stage_shape = (4, size, 768) if more else (16, 128)
    shape = jax.ShapeDtypeStruct
    steps = SUM_STEPS + more
    flat_kept = [kept[b][name] for b in range(2) for name in KEPT_NAMES]
    scratch = [
        ((2, 4) + matrix, BF),
        ((RING, 2, 2, 4, size, 768), BF),
        ((COUNT, 2, 2, 4, size // 2, 768), BF),
        ((COUNT, 2, 4, size // 2, 768), BF),
        (stage_shape, BF),
        ((COUNT, 3, size, 768), BF),
        ((COUNT, size, 768), BF),
        ((2,) + matrix, BF),
        ((2,) + matrix, BF),
        ((4,) + matrix, BF),
        ((rows, 768), F32),
        ((rows, 768), F32),
        ((rows, 768), F32),
        ((rows, 768), BF),
        ((rows, 768), BF),
        ((4, rows, 768), BF),
        ((2, rows, 768), F32),
        ((rows, 768), BF),
        ((rows, 768), F32),
        ((rows, 768), BF),
        ((2 * rows, 768), BF),
        ((2 * rows, 768), BF),
        ((2 * rows, 768), BF),
        ((rows, 768), BF),
        ((rows, 768), BF),
        ((rows, 768), BF),
        ((2 * rows, 768), BF),
        ((2 * rows, 768), BF),
        ((6, 8, 2 * rows), F32),
        ((2, rows, 768), BF),
        ((2, rows, 768), BF),
        ((32, 768), F32),
        ((2, steps, 16, 768), F32),
        ((1, 768), F32),
        ((2 * rows, 1), F32),
    ]
    got = pl.pallas_call(
        functools.partial(backward_kernel, dp_size),
        out_shape=[
            shape((COUNT,) + matrix, BF),
            shape(more_shape, BF),
            shape((32, 768), F32),
            shape((rows, 768), BF),
        ],
        in_specs=[anywhere] * (8 + COUNT + 2 * len(KEPT)) + [vmem, smem] + [vmem] * 4,
        out_specs=[anywhere] * 2 + [vmem] * 2,
        scratch_shapes=[pltpu.VMEM(dims, kind) for dims, kind in scratch]
        + [
            pltpu.SemaphoreType.DMA((COUNT, 19 + more)),
            pltpu.SemaphoreType.DMA((COUNT, 19 + more)),
            pltpu.SemaphoreType.DMA((LOADS,)),
            pltpu.SemaphoreType.DMA((COUNT,)),
            pltpu.SemaphoreType.REGULAR((1, COUNT)),
            pltpu.SemaphoreType.DMA((2, 2 * EXCHANGE + 2 * steps)),
        ],
        compiler_params=pltpu.CompilerParams(
            collective_id=1, has_side_effects=True, vmem_limit_bytes=63 * 1024 * 1024
        ),
    )(*locals_, *full, *flat_kept, cotangent, lengths, *params)
    return got[0], got[2], got[3]


def finish_kernel(whole, sums, *refs):
    passed, outs, refs = refs[:2], refs[2:24], refs[24:]
    low, high, load, store = refs
    z = lax.axis_index("mp")
    loads = [
        pltpu.make_async_copy(whole.at[j], low.at[j], load.at[j]) for j in range(COUNT)
    ]
    for copy in loads:
        copy.start()
    for source, target in zip(passed, outs[:2]):
        target[...] = source[...]
    stores = []

    def keep(source, target):
        copy = pltpu.make_async_copy(source, target, store.at[len(stores)])
        copy.start()
        stores.append(copy)

    for b in range(2):
        project_in, project_out, up, down = outs[2 + 10 * b : 6 + 10 * b]
        gains, shifts, out_bias, scales, up_bias, project_bias = outs[6 + 10 * b : 12 + 10 * b]
        base = 16 * b
        for row, ref in zip((0, 2, 4, 6), (gains, shifts, out_bias, scales)):
            ref[...] = sums[base + row : base + row + 2, :]
        up_bias[...] = sums[pl.ds(base + 8 + z, 1), :].reshape(768)
        mine = sums[pl.ds(base + 12 + z, 1), :]
        project_bias[0:1, :] = mine[:, 0:192]
        project_bias[1:2, :] = mine[:, 256:448]
    for j in range(COUNT):
        b = 1 if j < 3 else 0
        project_in, project_out, up, down = outs[2 + 10 * b : 6 + 10 * b]
        loads[j].wait()

        def widen(chunk_rows):
            high[j, chunk_rows, :] = low[j, chunk_rows, :].astype(F32)

        blocks(8, 96, widen)
        if j % 3 == 0:
            keep(high.at[j], down)
        elif j % 3 == 1:
            keep(high.at[j], up)
        else:
            keep(high.at[j, pl.ds(0, 576)], project_in)
            keep(high.at[j, pl.ds(576, 192)], project_out)
    for copy in stores:
        copy.wait()


def finish_all(whole, sums, output, grad_input):
    anywhere = pl.BlockSpec(memory_space=pl.ANY)
    vmem = pl.BlockSpec(memory_space=pltpu.VMEM)
    shape = jax.ShapeDtypeStruct
    matrix = whole.shape[1:]
    big = [shape((576, 768), F32), shape((192, 768), F32), shape(matrix, F32), shape(matrix, F32)]
    little = [shape((2, 768), F32)] * 4 + [shape((768,), F32), shape((2, 192), F32)]
    return pl.pallas_call(
        finish_kernel,
        out_shape=[shape(output.shape, BF)] * 2 + (big + little) * 2,
        in_specs=[anywhere] + [vmem] * 3,
        out_specs=[vmem] * 2 + ([anywhere] * 4 + [vmem] * 6) * 2,
        scratch_shapes=[
            pltpu.VMEM((COUNT,) + matrix, BF),
            pltpu.VMEM((COUNT,) + matrix, F32),
            pltpu.SemaphoreType.DMA((COUNT,)),
            pltpu.SemaphoreType.DMA((COUNT + 2,)),
        ],
        compiler_params=pltpu.CompilerParams(vmem_limit_bytes=60 * 1024 * 1024),
    )(whole, sums, output, grad_input)


def local_block(weights):
    p_in, p_out, up, down = weights[2], weights[4], weights[7], weights[9]
    return [p_in.swapaxes(1, 2).reshape(-1, p_in.shape[1]), p_out, up, down]


def arrange(grads):
    project_in, project_out, up, down = grads[:4]
    gains, shifts, out_bias, scales, up_bias, project_bias = grads[4:]
    return (
        gains,
        shifts,
        project_in.reshape(3, 192, 768).swapaxes(1, 2),
        project_bias,
        project_out,
        out_bias,
        scales,
        up,
        up_bias,
        down,
    )


def body(inputs, lengths, cotangent, *params):
    blocks_ = params[:10], params[10:]
    locals_ = local_block(blocks_[0]) + local_block(blocks_[1])
    forward_params = [weights[p] for weights in blocks_ for p in (0, 1, 5, 6, 3, 8)]
    full, kept, output = forward_all(locals_, inputs, lengths, forward_params)
    backward_params = [weights[p] for weights in blocks_ for p in (0, 6)]
    whole, sums, grad_input = backward_all(
        locals_, full, kept, cotangent, lengths, backward_params
    )
    outs = finish_all(whole, sums, output, grad_input)
    return tuple(outs[:2]) + arrange(outs[2:12]) + arrange(outs[12:22])


def solution(mesh):
    rows = P(("dp", "mp"), None)
    weights = (
        P(),
        P(),
        P(None, None, "mp"),
        P(None, "mp"),
        P("mp", None),
        P(),
        P(),
        P(None, "mp"),
        P("mp"),
        P("mp", None),
    )
    in_specs = (rows, P("dp"), rows) + weights + weights
    out_specs = (rows, rows) + weights + weights
    return jax.shard_map(body, mesh=mesh, in_specs=in_specs, out_specs=out_specs, check_vma=False)
```

```python
import functools

import jax
import jax.numpy as jnp
from jax import lax
from jax.experimental import pallas as pl
from jax.experimental.pallas import tpu as pltpu
from jax.sharding import PartitionSpec as P

HEAD_DIM = 64
SLOT = 640
PARTS = 8
BF = jnp.bfloat16
F32 = jnp.float32

epsilon = 1e-06

MESH = pl.DeviceIdType.MESH
COUNT = 6


def flip(index, bits):
    bit = 1
    while bit <= bits:
        if bits & bit:
            index = index + bit - 2 * bit * lax.rem(lax.div(index, bit), 2)
        bit *= 2
    return index


def partners(dp_size):
    bits = [{"dp": 6}]
    bit = 1
    while bit < dp_size:
        bits.append({"dp": bit})
        bit *= 2
    return bits + [{"mp": r} for r in (1, 2, 3)]


def device_at(bits):
    return {axis: flip(lax.axis_index(axis), bit) for axis, bit in bits.items()}


def enter(dp_size):
    barrier = pltpu.get_barrier_semaphore()
    for bits in partners(dp_size):
        pl.semaphore_signal(barrier, inc=1, device_id=device_at(bits), device_id_type=MESH)
    pl.semaphore_wait(barrier, len(partners(dp_size)))


def remote(source, target, send, recv, bits):
    return pltpu.make_async_remote_copy(
        src_ref=source,
        dst_ref=target,
        send_sem=send,
        recv_sem=recv,
        device_id=device_at(bits),
        device_id_type=MESH,
    )


def piece_rows(index, size):
    return pl.ds(pl.multiple_of(index * size, size), size)


def dot(left_side, right_side, contract=(1, 0)):
    return lax.dot_general(
        left_side,
        right_side,
        (((contract[0],), (contract[1],)), ((), ())),
        preferred_element_type=F32,
    )


def blocks(count, size, body):
    @pl.loop(0, count)
    def _(i):
        body(pl.ds(pl.multiple_of(i * size, size), size))


def norm_parts(values):
    center = values - jnp.mean(values, axis=-1, keepdims=True)
    spread = jnp.mean(center * center, axis=-1, keepdims=True)
    inverse = lax.rsqrt(spread + epsilon)
    return center * inverse, inverse


def norm_rows(source, gain, shift, target):
    unit, _ = norm_parts(source[...])
    target[...] = (unit * gain + shift).astype(BF)


def project_rows(source, weight, bias, target):
    value = dot(source[...], weight[...].reshape(768, 768), (1, 1))
    if bias is not None:
        value = value + bias[...]
    target[...] = value.astype(BF)


def low_lanes(shape):
    return lax.broadcasted_iota(jnp.int32, shape, 1) < HEAD_DIM


def two_heads(pair, low):
    nothing = jnp.zeros_like(pair)
    return jnp.concatenate([jnp.where(low, pair, nothing), jnp.where(low, nothing, pair)])


def attend_pairs(first, last, query, key, value, key_bias, mixed, log_total):
    rows = query.shape[0]

    @pl.loop(first, last)
    def _(p):
        lanes = pl.ds(pl.multiple_of(p * 128, 128), 128)
        low = low_lanes((rows, 128))
        both = two_heads(query[:, lanes], low)
        scores = dot(both, key[:, lanes], (1, 1)) * HEAD_DIM ** (-0.5) + key_bias[...]
        peak = jnp.max(scores, axis=1, keepdims=True)
        exponent = jnp.exp(scores - peak)
        total = jnp.sum(exponent, axis=1, keepdims=True)
        probs = (exponent * (1.0 / total)).astype(BF)
        result = dot(probs, value[:, lanes])
        logs = jnp.broadcast_to(peak + jnp.log(total), (2 * rows, 128))
        log_total[p, :, :] = logs.T[0:8, :]
        mixed[:, lanes] = jnp.where(low, result[0:rows], result[rows:]).astype(BF)


def attend_out(mixed, weight, bias, scale, resid, attn, middle):
    value = dot(mixed[...], weight[...].reshape(768, 768)) + bias[...]
    attn[...] = value
    middle[...] = resid[...] + scale[...] * value


def gelu_exact(values):
    return 0.5 * values * (1.0 + lax.erf(values * (0.5**0.5)))


def mlp_up(r, normed, up, up_bias, pre, hidden):
    value = dot(normed[...], up[r]) + up_bias[r : r + 1, :]
    pre[r] = value
    hidden[r] = gelu_exact(value).astype(BF)


def mlp_down(hidden, down, bias, mlp):
    value = dot(hidden[0], down[0])
    for r in (1, 2, 3):
        value = value + dot(hidden[r], down[r])
    mlp[...] = value + bias[...]


def attend_pairs_back(
    first, last, query, key, value, key_bias, log_total, grad, grad_query, grad_key, grad_value
):
    rows = query.shape[0]
    scale = HEAD_DIM ** (-0.5)

    @pl.loop(first, last)
    def _(p):
        lanes = pl.ds(pl.multiple_of(p * 128, 128), 128)
        low = low_lanes((rows, 128))
        both = two_heads(query[:, lanes], low)
        both_grad = two_heads(grad[:, lanes], low)
        key_pair = key[:, lanes]
        scores = dot(key_pair, both, (1, 1)) * scale + key_bias[...]
        probs = jnp.exp(scores - log_total[p, 0:1, :])
        grad_value[:, lanes] = dot(probs.astype(BF), both_grad).astype(BF)
        grad_probs = dot(value[:, lanes], both_grad, (1, 1))
        inner = jnp.sum(probs * grad_probs, axis=0, keepdims=True)
        grad_scores = (probs * (grad_probs - inner)).astype(BF)
        grad_key[:, lanes] = (dot(grad_scores, both) * scale).astype(BF)
        result = dot(grad_scores, key_pair, (0, 0)) * scale
        grad_query[:, lanes] = jnp.where(low, result[0:rows], result[rows:]).astype(BF)


def gelu_slope(values):
    bell = jnp.exp(-0.5 * values * values) * 0.3989422804014327
    return 0.5 * (1.0 + lax.erf(values * (0.5**0.5))) + values * bell


def column_sum(values):
    return jnp.sum(values, axis=0, keepdims=True)


def branch_grad(grad, mlp, scale, branch, scale_sum, bias_sum):
    scale_sum[...] = jnp.zeros_like(scale_sum)
    bias_sum[...] = jnp.zeros_like(bias_sum)

    def body(rows):
        value = grad[rows, :]
        scale_sum[...] += column_sum(value * mlp[rows, :])
        low = (scale * value).astype(BF)
        branch[rows, :] = low
        bias_sum[...] += column_sum(low.astype(F32))

    blocks(grad.shape[0] // 32, 32, body)


def norm_back(source, slope, gain, grad, gain_sum, shift_sum, after=None):
    gain_sum[...] = jnp.zeros_like(gain_sum)
    shift_sum[...] = jnp.zeros_like(shift_sum)

    def body(rows):
        unit, inverse = norm_parts(source[rows, :])
        value = slope[rows, :]
        gain_sum[...] += column_sum(value * unit)
        shift_sum[...] += column_sum(value)
        scaled = value * gain
        value = (
            scaled
            - jnp.mean(scaled, axis=-1, keepdims=True)
            - unit * jnp.mean(scaled * unit, axis=-1, keepdims=True)
        )
        value = grad[rows, :] + inverse * value
        grad[rows, :] = value
        if after is not None:
            after(rows, value)

    blocks(source.shape[0] // 160, 160, body)


def outer(left_side, right_side, target):
    target[...] = dot(left_side[...], right_side[...], (0, 0)).astype(BF)


def hidden_grad(branch, down, pre, grad_pre, bias_sum):
    value = dot(branch[...], down[...], (1, 1)) * gelu_slope(pre[...])
    low = value.astype(BF)
    grad_pre[...] = low
    bias_sum[...] = column_sum(low.astype(F32))


KEPT = (
    ("resid", (320, 768), F32),
    ("normed", (640, 768), BF),
    ("query", (320, 768), BF),
    ("key", (640, 768), BF),
    ("value", (640, 768), BF),
    ("log_total", (6, 8, 640), F32),
    ("mixed", (320, 768), BF),
    ("attn", (320, 768), F32),
    ("middle", (320, 768), F32),
    ("normed2", (320, 768), BF),
    ("pre", (4, 320, 768), F32),
    ("hidden", (4, 320, 768), BF),
    ("mlp", (320, 768), F32),
)
KEPT_NAMES = [name for name, _, _ in KEPT]


FORWARD_PLAN = (
    (),
    (0,),
    (),
    (),
    (0, 1, 0, 2, 0, 1),
    (),
    (3, 2),
    (),
    (4,),
    (),
    (1, 2),
    (3,),
    (),
    (1,),
    (),
    (5,),
    (),
    (),
    (2,),
    (4,),
    (),
    (),
    (),
    (),
    (3, 5, 3),
    (),
    (),
    (),
    (),
    (4,),
    (5,),
    (),
    (4,),
    (),
    (),
    (),
    (),
    (5,),
    (),
    (),
    (),
    (),
    (),
)


def attn_chunk(local, full, i, r, kind):
    if r:
        return full[i].at[r - 1, pl.ds(kind * 192, 192)]
    project_in, project_out = local[i // 3][:2]
    return project_in.at[pl.ds(kind * 192, 192)] if kind < 3 else project_out


def forward_kernel(*refs):
    refs = list(refs)

    def take(count):
        got = refs[:count]
        del refs[:count]
        return got

    local = [take(4), take(4)]
    inputs, lengths = take(2)
    params = [take(6), take(6)]
    full = take(COUNT)
    kept_out = [dict(zip(KEPT_NAMES, take(len(KEPT)))) for _ in range(2)]
    (output,) = take(1)
    kept = [{name: ref.at[b] for name, ref in zip(KEPT_NAMES, refs)} for b in range(2)]
    take(len(KEPT))
    attn_w, up_w, down_w, small, small_in, key_bias, in_bias, up_bias = take(8)
    send, recv, other, load, store = take(5)
    size = full[0].shape[1] // PARTS
    rows = inputs.shape[0]
    me = lax.rem(lax.axis_index("dp"), PARTS)
    z = lax.axis_index("mp")
    flying = []
    waiting = []

    def part(mask):
        return piece_rows(flip(me, mask), size)

    def place(i, chunks, mask, half=None):
        b, kind = divmod(i, 3)
        index = flip(me, mask)
        start, count = index * size, size
        if kind == 0:
            start = lax.rem(index, 2) * size
        if half is not None:
            start, count = start + half * (size // 2), size // 2
        where = pl.ds(pl.multiple_of(start, count), count)
        if kind == 0:
            return attn_w.at[b, lax.div(index, 2), chunks, where]
        return (up_w if kind == 1 else down_w).at[b, chunks, where]

    def slab(i, mask, half=None):
        return place(i, pl.ds(1, 3), mask, half)

    def along_z(i):
        b, kind = divmod(i, 3)

        def copies(source, rows_of):
            return [
                remote(
                    source.at[rows_of],
                    place(i, r, 0),
                    send.at[i, r - 1],
                    recv.at[i, r - 1],
                    {"mp": r},
                )
                for r in (1, 2, 3)
            ]

        if kind:
            return launch(copies(local[b][1 + kind], part(0)))
        project_in, project_out = local[b][:2]
        inner = project_in.shape[0] // size

        @pl.when(me < inner)
        def _():
            for copy in copies(project_in, part(0)):
                copy.start()

        @pl.when(me >= inner)
        def _():
            for copy in copies(project_out, piece_rows(lax.max(me - inner, 0), size)):
                copy.start()

        started = copies(project_out, pl.ds(0, size))
        flying.extend(started)
        return started

    def along_dp(i, slot, mask, bit, half=None):
        there = slab(i, mask, half)
        return remote(there, there, send.at[i, slot], recv.at[i, slot], {"dp": bit})

    def launch(copies):
        for copy in copies:
            copy.start()
        flying.extend(copies)
        return copies

    def landed(copies):
        for copy in copies:
            copy.wait_recv()

    state = [None] * COUNT

    at = [0] * COUNT
    plan = iter(FORWARD_PLAN)

    def slot():
        for i in next(plan):
            stage(i, at[i])
            at[i] += 1

    def stage(i, s):
        if s == 0:
            state[i] = along_z(i)
        elif s == 1:
            landed(state[i])
            state[i] = launch([along_dp(i, 3, 0, 2), along_dp(i, 4, 0, 4)])
            launch([along_dp(i, 7, 0, 1)])
        elif s == 2:
            landed(state[i])
            state[i] = launch([along_dp(i, 5, 2, 4, 0), along_dp(i, 6, 4, 2, 1)])
            launch([along_dp(i, 8, 2, 1), along_dp(i, 9, 4, 1)])
        elif s == 3:
            landed(state[i])
            launch([along_dp(i, 10, 6, 1)])

    def complete(i):
        for slot, mask in ((7, 0), (8, 2), (9, 4), (10, 6)):
            along_dp(i, slot, mask, 1).wait_recv()
        b, kind = divmod(i, 3)
        finish(owned[b][:4] if kind == 0 else owned[b][3 + kind : 4 + kind])
        save_full(i)

    def load_own():
        for b in range(2):
            project_in, project_out, up, down = local[b]
            copies = [
                pltpu.make_async_copy(
                    project_in.at[pl.ds(kind * 192, 192)], attn_w.at[b, kind, 0], load.at[b, kind]
                )
                for kind in range(3)
            ]
            copies += [
                pltpu.make_async_copy(project_out, attn_w.at[b, 3, 0], load.at[b, 3]),
                pltpu.make_async_copy(up, up_w.at[b, 0], load.at[b, 4]),
                pltpu.make_async_copy(down, down_w.at[b, 0], load.at[b, 5]),
            ]
            for copy in copies:
                copy.start()
            owned.append(copies)

    def save_full(i):
        b, kind = divmod(i, 3)
        if kind == 0:
            copies = [
                pltpu.make_async_copy(
                    attn_w.at[b, n, pl.ds(1, 3)],
                    full[i].at[:, pl.ds(n * 192, 192)],
                    load.at[b, 6 + n],
                )
                for n in range(4)
            ]
        else:
            source = up_w if kind == 1 else down_w
            copies = [
                pltpu.make_async_copy(source.at[b, pl.ds(1, 3)], full[i], load.at[b, 9 + kind])
            ]
        for copy in copies:
            copy.start()
        waiting.extend(copies)

    owned = []

    def finish(copies):
        for copy in copies:
            copy.wait()

    def save(b, *names):
        for name in names:
            copy = pltpu.make_async_copy(
                kept[b][name], kept_out[b][name], store.at[b, KEPT_NAMES.index(name)]
            )
            copy.start()
            waiting.append(copy)

    def exchange(b):
        copy = remote(
            kept[b]["normed"].at[pl.ds(0, rows)],
            kept[b]["normed"].at[pl.ds(rows, rows)],
            other.at[0, 3 + b],
            other.at[1, 3 + b],
            {"mp": 1},
        )
        return launch([copy])

    load_own()
    enter(lax.axis_size("dp"))
    slot()
    slot()
    for b in range(2):
        small[:, b] = jnp.zeros((4, 8, 768), F32)
        project_bias, hidden_bias = params[b][4:]
        for r in range(4):
            small[r, b, 0:1, :] = hidden_bias[...].reshape(1, 768)
            small[r, b, 1:3, r * 192 : (r + 1) * 192] = project_bias[...]
    bias_in = launch(
        [
            remote(small.at[r], small_in.at[r - 1], other.at[0, r - 1], other.at[1, r - 1], {"mp": r})
            for r in (1, 2, 3)
        ]
    )

    def widen(part_rows):
        kept[0]["resid"][part_rows, :] = inputs[part_rows, :].astype(F32)

    blocks(10, 32, widen)
    position = lax.broadcasted_iota(jnp.int32, (1, 2 * rows), 1)
    shifted = position + lax.rem(z, 2) * jnp.where(position < rows, rows, -rows)
    key_bias[...] = jnp.where(shifted < lengths[lax.div(z, 2)], 0.0, -1e30).astype(F32)

    def first_norm(b):
        gains, shifts = params[b][:2]
        k = kept[b]
        slot()
        norm_rows(k["resid"], gains[0:1, :], shifts[0:1, :], k["normed"].at[pl.ds(0, rows)])
        save(b, "resid")

    first_norm(0)
    for b in range(2):
        k = kept[b]
        gains, shifts, out_bias, scales = params[b][:4]
        base = 3 * b
        slot()
        swapped = exchange(b)
        slot()
        complete(base)
        if b == 0:
            landed(bias_in)
            for c in range(2):
                in_bias[c] = small[0, c] + small_in[0, c] + small_in[1, c] + small_in[2, c]
                up_bias[c, 0:1] = small[0, c, 0:1]
                for r in (1, 2, 3):
                    up_bias[c, r : r + 1] = small_in[r - 1, c, 0:1]
        project_bias = in_bias.at[b]
        slot()
        landed(swapped)
        slot()
        project_rows(
            k["normed"].at[pl.ds(0, rows)],
            attn_w.at[b, 0],
            project_bias.at[pl.ds(1, 1)],
            k["query"],
        )
        slot()
        project_rows(k["normed"], attn_w.at[b, 1], None, k["key"])
        slot()
        project_rows(k["normed"], attn_w.at[b, 2], project_bias.at[pl.ds(2, 1)], k["value"])
        save(b, "normed", "query", "key", "value")
        pair_args = (k["query"], k["key"], k["value"], key_bias, k["mixed"], k["log_total"])
        for pair in (0, 2, 4):
            slot()
            attend_pairs(pair, pair + 2, *pair_args)
        save(b, "log_total", "mixed")
        slot()
        attend_out(
            k["mixed"],
            attn_w.at[b, 3],
            out_bias.at[pl.ds(0, 1)],
            scales.at[pl.ds(0, 1)],
            k["resid"],
            k["attn"],
            k["middle"],
        )
        slot()
        norm_rows(k["middle"], gains[1:2, :], shifts[1:2, :], k["normed2"])
        save(b, "attn", "middle", "normed2")
        slot()
        complete(base + 1)
        for r in range(4):
            slot()
            mlp_up(r, k["normed2"], up_w.at[b], up_bias.at[b], k["pre"], k["hidden"])
        save(b, "pre", "hidden")
        slot()
        complete(base + 2)
        slot()
        mlp_down(k["hidden"], down_w.at[b], out_bias.at[pl.ds(1, 1)], k["mlp"])
        save(b, "mlp")
        slot()

        def result(part_rows):
            value = k["middle"][part_rows, :] + scales[1:2, :] * k["mlp"][part_rows, :]
            if b == 0:
                kept[1]["resid"][part_rows, :] = value
            else:
                output[part_rows, :] = value.astype(BF)

        blocks(10, 32, result)
        if b == 0:
            first_norm(1)
    slot()
    for copy in flying:
        copy.wait_send()
    finish(waiting)


def forward_all(locals_, inputs, lengths, params):
    anywhere = pl.BlockSpec(memory_space=pl.ANY)
    vmem = pl.BlockSpec(memory_space=pltpu.VMEM)
    smem = pl.BlockSpec(memory_space=pltpu.SMEM)
    matrix = locals_[2].shape
    kept_shapes = [jax.ShapeDtypeStruct(shape, kind) for _, shape, kind in KEPT]
    got = pl.pallas_call(
        forward_kernel,
        out_shape=[jax.ShapeDtypeStruct((3,) + matrix, BF)] * COUNT
        + kept_shapes * 2
        + [jax.ShapeDtypeStruct(inputs.shape, BF)],
        in_specs=[anywhere] * 8 + [vmem, smem] + [vmem] * 12,
        out_specs=[anywhere] * (COUNT + 2 * len(KEPT)) + [vmem],
        scratch_shapes=[pltpu.VMEM((2,) + shape, kind) for _, shape, kind in KEPT]
        + [
            pltpu.VMEM((2, 4, 4, 192, 768), BF),
            pltpu.VMEM((2, 4) + matrix, BF),
            pltpu.VMEM((2, 4) + matrix, BF),
            pltpu.VMEM((4, 2, 8, 768), F32),
            pltpu.VMEM((3, 2, 8, 768), F32),
            pltpu.VMEM((1, 2 * inputs.shape[0]), F32),
            pltpu.VMEM((2, 8, 768), F32),
            pltpu.VMEM((2, 8, 768), F32),
            pltpu.SemaphoreType.DMA((COUNT, 11)),
            pltpu.SemaphoreType.DMA((COUNT, 11)),
            pltpu.SemaphoreType.DMA((2, 5)),
            pltpu.SemaphoreType.DMA((2, 12)),
            pltpu.SemaphoreType.DMA((2, len(KEPT))),
        ],
        compiler_params=pltpu.CompilerParams(
            collective_id=0, has_side_effects=True, vmem_limit_bytes=63 * 1024 * 1024
        ),
    )(*locals_, inputs, lengths, *params)
    full = got[:COUNT]
    kept = [
        dict(zip(KEPT_NAMES, got[COUNT + b * len(KEPT) : COUNT + (b + 1) * len(KEPT)]))
        for b in range(2)
    ]
    return full, kept, got[-1]


RING = 3


def backward_kernel(dp_size, *refs):
    refs = list(refs)

    def take(count):
        got = refs[:count]
        del refs[:count]
        return got

    local = [take(4), take(4)]
    full = take(COUNT)
    kept = [dict(zip(KEPT_NAMES, take(len(KEPT)))) for _ in range(2)]
    cotangent, lengths = take(2)
    params = [take(2), take(2)]
    (whole, more_in, sums_out, grad_out) = take(4)
    (grad_w, core_in, first_in, second_in, more_stage, z_in, piece) = take(7)
    (near_in, far_in, turn_in, last_in) = take(4)
    (up_w, down_w, attn_w) = take(3)
    (grad, buf_p, buf_q, branch, normed2, hidden, pre) = take(7)
    (grad_pre, slope, query, key, value, normed, mixed) = take(7)
    (grad_mixed, grad_query, grad_key, grad_value, log_total) = take(5)
    (away, away_in, sums, sums_in, hidden_sum, key_bias) = take(6)
    (send, recv, load, store, free, other) = take(6)
    rows = grad.shape[0]
    size = piece.shape[1]
    me = lax.rem(lax.axis_index("dp"), PARTS)
    z = lax.axis_index("mp")
    more = [PARTS << e for e in range((dp_size // PARTS).bit_length() - 1)]
    thirds = () if more else THIRDS

    def part(mask):
        return piece_rows(flip(me, mask), size)

    slots = {}
    pending = {}

    def fetch(name, source, target):
        slot = slots.setdefault(name, len(slots))
        copy = pltpu.make_async_copy(source, target, load.at[slot])
        copy.start()
        pending[name] = copy

    def need(*names):
        for name in names:
            pending.pop(name).wait()

    def fetch_kept(b, name, target):
        fetch(name, kept[b][name], target)

    def chunk(i, r):
        return local[i // 3][1 + i % 3] if r == 0 else full[i].at[r - 1]

    def fetch_mlp(b, r):
        fetch(("pre", r % 2), kept[b]["pre"].at[r], pre.at[r % 2])
        fetch(("up", r % 2), chunk(3 * b + 1, r), up_w.at[r % 2])
        fetch(("down", r % 2), chunk(3 * b + 2, r), down_w.at[r % 2])

    def fetch_attn(b):
        for kind in range(4):
            for r in range(4):
                fetch(
                    ("attn", kind, r),
                    attn_chunk(local, full, 3 * b, r, kind),
                    attn_w.at[kind, pl.ds(r * 192, 192)],
                )

    def need_attn(*kinds):
        for kind in kinds:
            need(*[("attn", kind, r) for r in range(4)])

    flying = []
    state = [None] * (COUNT + 2)
    sent = [[] for _ in range(COUNT)]
    at = [0] * (COUNT + 2)

    def launch(copies):
        for copy in copies:
            copy.start()
        return copies

    def landed(copies):
        for copy in copies:
            copy.wait_recv()

    def added(left, right):
        left[...] = left[...] + right[...]

    def add_slabs(target, source):
        @pl.loop(0, 4)
        def _(r):
            added(target.at[r], source.at[r])

    half = [pl.ds(0, size // 2), pl.ds(size // 2, size // 2)]
    third = size // 3
    cut = [pl.ds(n * third, third) for n in range(3)]
    joint = pl.ds(0, 2 * third)

    def add_own(j, high, low, n=None):
        first, count = (0, size) if n is None else (n * third, third)
        start = flip(me, 4 * high + 2 * low) * size + first
        own = pl.ds(pl.multiple_of(start, count), count)

        @pl.loop(0, 4)
        def _(r):
            added(
                core_in.at[j % RING, high, low, r, pl.ds(first, count)], grad_w.at[j % 2, r, own]
            )

    def each_slot(body):
        for high in range(2):
            for low in range(2):
                body(high, low)

    owns = []

    def credit(stage, j, bits):
        if j < COUNT:
            pl.semaphore_signal(
                free.at[stage, j], inc=1, device_id=device_at(bits), device_id_type=MESH
            )

    def spend(stage, j):
        if j >= RING:
            pl.semaphore_wait(free.at[stage, j], 1)

    def across(j):
        spend(0, j)
        state[j] = launch(
            [
                remote(
                    grad_w.at[j % 2, :, part(1 | 4 * high | 2 * low)],
                    core_in.at[j % RING, high, low],
                    send.at[j, 2 * high + low],
                    recv.at[j, 2 * high + low],
                    {"dp": 1},
                )
                for high in range(2)
                for low in range(2)
            ]
        )
        sent[j] = list(state[j])

    def reuse(j):
        if j >= 2:
            for copy in sent[j - 2]:
                copy.wait_send()

    def spread(j, slot, mask, bit, half=None):
        if half is None:
            place = whole.at[j, part(mask)]
        else:
            start = flip(me, mask) * size + half * (size // 2)
            place = whole.at[j, pl.ds(pl.multiple_of(start, size // 2), size // 2)]
        source = piece.at[j] if mask == 0 else place
        return remote(source, place, send.at[j, slot], recv.at[j, slot], {"dp": bit})

    def advance(*matrices):
        for j in matrices:
            (stage if j < COUNT else sum_stage)(j, at[j])
            at[j] += 1

    def send_out(j, slot, source, target, bits):
        copies = launch([remote(source, target, send.at[j, slot], recv.at[j, slot], bits)])
        flying.extend((j, copy) for copy in copies)
        return copies[0]

    def stage(j, s):
        core = core_in.at[j % RING]
        if j in thirds and s < 5:
            third_stage(j, s, core)
        elif s == 0:
            landed(state[j])
            add_own(j, 1, 1)
            add_own(j, 0, 1)
            state[j] = [
                send_out(j, 4, core.at[:, 1, :, half[0]], first_in.at[j, 0], {"dp": 2})
            ]
            add_own(j, 1, 0)
            state[j].append(
                send_out(j, 5, core.at[1, :, :, half[1]], first_in.at[j, 1], {"dp": 4})
            )
            add_own(j, 0, 0)
        elif s == 1:
            got = state[j]
            state[j] = []
            for h, bit in enumerate((4, 2)):
                landed(got[h : h + 1])
                away_part = core.at[1, 0, :, half[0]] if h == 0 else core.at[0, 1, :, half[1]]
                add_slabs(away_part, first_in.at[j, h, 1])
                state[j].append(
                    send_out(j, 6 + h, away_part, second_in.at[j, h], {"dp": bit})
                )
            for h in range(2):
                add_slabs(core.at[0, 0, :, half[h]], first_in.at[j, h, 0])
        elif s == 2:
            landed(state[j])
            for h in range(2):
                add_slabs(core.at[0, 0, :, half[h]], second_in.at[j, h])
            mine = core.at[0, 0]
            for e, bit in enumerate(more):
                copy = remote(
                    mine, more_in.at[j, e], send.at[j, 24 + e], recv.at[j, 24 + e], {"dp": bit}
                )
                copy.start()
                copy.wait()
                back = pltpu.make_async_copy(more_in.at[j, e], more_stage, load.at[LOADS - 1])
                back.start()
                back.wait()
                add_slabs(mine, more_stage)
            state[j] = [
                send_out(j, 7 + r, mine.at[r], z_in.at[j, r - 1], {"mp": r}) for r in (1, 2, 3)
            ]
        elif s == 3:
            landed(state[j])
            total = core[0, 0, 0].astype(F32)
            for r in range(3):
                total = total + z_in[j, r].astype(F32)
            piece[j] = total.astype(BF)
            give_piece(j)
        elif s == 5:
            landed(state[j])
            state[j] = launch([spread(j, 13, 2, 4, 0), spread(j, 14, 4, 2, 1)])
            core_copies = launch([spread(j, 16, 2, 1), spread(j, 17, 4, 1)])
            flying.extend((j, copy) for copy in state[j] + core_copies)
        elif s == 6:
            landed(state[j])
            core_copies = launch([spread(j, 18, 6, 1)])
            flying.extend((j, copy) for copy in core_copies)
            state[j] = [spread(j, 15 + n, mask, 1) for n, mask in enumerate((0, 2, 4, 6))]
        elif s == 7:
            landed(state[j])

    def give_piece(j):
        state[j] = launch([spread(j, 11, 0, 2), spread(j, 12, 0, 4)])
        core_copy = launch([spread(j, 15, 0, 1)])
        own = pltpu.make_async_copy(piece.at[j], whole.at[j, part(0)], store.at[j])
        own.start()
        owns.append(own)
        if j + RING < COUNT:
            for owner, copy in flying:
                if owner == j:
                    copy.wait_send()
            flying[:] = [(owner, copy) for owner, copy in flying if owner != j]
            credit(0, j + RING, {"dp": 1})
        flying.extend((j, copy) for copy in state[j] + core_copy)

    def third_stage(j, s, core):
        n_third = thirds.index(j)
        near, far, turn, last = (
            ref.at[n_third] for ref in (near_in, far_in, turn_in, last_in)
        )
        if s == 0:
            landed(state[j])
            add_own(j, 0, 1, 0)
            add_own(j, 1, 1, 0)
            state[j] = [
                send_out(
                    j, 4, core.at[:, 1, :, cut[0]], first_in.at[j, 0, :, :, pl.ds(0, third)], {"dp": 2}
                )
            ]
            add_own(j, 1, 0, 1)
            add_own(j, 1, 1, 1)
            state[j].append(
                send_out(
                    j, 5, core.at[1, :, :, cut[1]], first_in.at[j, 1, :, :, pl.ds(0, third)], {"dp": 4}
                )
            )
            each_slot(lambda high, low: add_own(j, high, low, 2))
            state[j] += [
                send_out(j, 19 + n, core.at[:, :, 1 + 2 * n, cut[2]], near.at[n], {"mp": 1})
                for n in range(2)
            ]
            add_own(j, 0, 0, 0)
            add_own(j, 1, 0, 0)
            add_own(j, 0, 0, 1)
            add_own(j, 0, 1, 1)
        elif s == 1:
            got = state[j]
            state[j] = []
            for h, bit in enumerate((4, 2)):
                landed(got[h : h + 1])
                away_part = core.at[1, 0, :, cut[0]] if h == 0 else core.at[0, 1, :, cut[1]]
                add_slabs(away_part, first_in.at[j, h, 1, :, pl.ds(0, third)])
                state[j].append(
                    send_out(
                        j, 6 + h, away_part, second_in.at[j, h, :, pl.ds(0, third)], {"dp": bit}
                    )
                )
            landed(got[2:])
            for n in (1, 0):
                each_slot(
                    lambda high, low: added(
                        core.at[high, low, 2 * n, cut[2]], near.at[n, high, low]
                    )
                )
                if n:
                    state[j].append(
                        send_out(j, 21, core.at[:, :, 2, cut[2]], far, {"mp": 2})
                    )
            for h in range(2):
                add_slabs(core.at[0, 0, :, cut[h]], first_in.at[j, h, 0, :, pl.ds(0, third)])
        elif s == 2:
            landed(state[j][2:])
            each_slot(
                lambda high, low: added(core.at[high, low, 0, cut[2]], far.at[high, low])
            )
            turned = send_out(j, 22, core.at[:, 1, 0, cut[2]], turn, {"dp": 2})
            landed(state[j][:2])
            for h in range(2):
                add_slabs(core.at[0, 0, :, cut[h]], second_in.at[j, h, :, pl.ds(0, third)])
            mine = core.at[0, 0, :, joint]
            state[j] = [turned] + [
                send_out(j, 7 + r, mine.at[r], z_in.at[j, r - 1, joint], {"mp": r})
                for r in (1, 2, 3)
            ]
        elif s == 3:
            landed(state[j][:1])
            added(core.at[1, 0, 0, cut[2]], turn.at[1])
            final = send_out(j, 23, core.at[1, 0, 0, cut[2]], last, {"dp": 4})
            added(core.at[0, 0, 0, cut[2]], turn.at[0])
            landed(state[j][1:])
            total = core[0, 0, 0, joint, :].astype(F32)
            for r in range(3):
                total = total + z_in[j, r, joint, :].astype(F32)
            piece[j, joint, :] = total.astype(BF)
            state[j] = [final]
        else:
            landed(state[j])
            mine = core.at[0, 0, 0, cut[2]]
            added(mine, last)
            piece[j, cut[2], :] = mine[...]
            give_piece(j)

    def sum_send(b, step, bits):
        place = 2 * EXCHANGE + (SUM_STEPS + len(more)) * b + step
        copy = remote(
            sums.at[pl.ds(16 * b, 16)],
            sums_in.at[b, step],
            other.at[0, place],
            other.at[1, place],
            bits,
        )
        copy.start()
        return copy

    def sum_stage(j, s):
        b = 7 - j
        mine = sums.at[pl.ds(16 * b, 16)]
        if s:
            for copy in state[j]:
                copy.wait()
        if s == 0:
            state[j] = [sum_send(b, r - 1, {"mp": r}) for r in (1, 2, 3)]
        elif s == 1:
            mine[...] = (mine[...] + sums_in[b, 0]) + (sums_in[b, 1] + sums_in[b, 2])
            state[j] = [sum_send(b, 3, {"dp": 1})]
        elif s == 2:
            mine[...] += sums_in[b, 3]
            for e, bit in enumerate(more):
                sum_send(b, SUM_STEPS + e, {"dp": bit}).wait()
                mine[...] += sums_in[b, SUM_STEPS + e]
            state[j] = [sum_send(b, 3 + n, {"dp": 2 * n}) for n in (1, 2, 3)]
        elif s == 3:
            mine[...] = (mine[...] + sums_in[b, 4]) + (sums_in[b, 5] + sums_in[b, 6])

    def start_block(b):
        fetch_kept(b, "mlp", buf_p)
        fetch_kept(b, "hidden", hidden)
        fetch_mlp(b, 0)
        fetch_mlp(b, 1)
        fetch_kept(b, "normed2", normed2)

    def start_attn(b):
        fetch_kept(b, "mixed", mixed)
        fetch_kept(b, "query", query)
        fetch_kept(b, "key", key)
        fetch_kept(b, "value", value)
        fetch_kept(b, "log_total", log_total)

    def sum_of(b, row):
        return sums.at[pl.ds(16 * b + row, 1)]

    def head_sums(b, lane, source, count):
        hidden_sum[...] = jnp.zeros_like(hidden_sum)

        def body(chunk_rows):
            hidden_sum[...] += column_sum(source[chunk_rows, :].astype(F32))

        blocks(count // 160, 160, body)
        for r in range(4):
            row = pl.ds(16 * b + 12 + flip(z, r), 1)
            sums[row, lane : lane + 192] = hidden_sum[:, r * 192 : (r + 1) * 192]

    start_block(1)
    fetch_kept(1, "middle", buf_q)
    start_attn(1)
    fetch_kept(1, "normed", normed)
    fetch_attn(1)
    enter(dp_size)
    sums[...] = jnp.zeros_like(sums)
    position = lax.broadcasted_iota(jnp.int32, (2 * rows, 1), 0)
    shifted = position + lax.rem(z, 2) * jnp.where(position < rows, rows, -rows)
    key_bias[...] = jnp.where(shifted < lengths[lax.div(z, 2)], 0.0, -1e30).astype(F32)

    plan = iter(PLAN)

    def slot():
        advance(*next(plan))

    slot()

    def widen(chunk_rows):
        grad[chunk_rows, :] = cotangent[chunk_rows, :].astype(F32)

    blocks(rows // 32, 32, widen)

    for b in (1, 0):
        gains, scales = params[b]
        base = 3 if b == 0 else 0
        slot()
        need("mlp")
        branch_grad(grad, buf_p, scales[1:2, :], branch, sum_of(b, 7), sum_of(b, 5))
        fetch_kept(b, "attn", buf_p)
        need("hidden")
        slot()
        reuse(base)
        for r in range(4):
            if r % 2 == 0:
                slot()
            outer(hidden.at[r], branch, grad_w.at[base % 2, r])
        slot()
        across(base)
        if b == 1:
            fetch_kept(0, "hidden", hidden)
        need("normed2")
        slot()
        reuse(base + 1)
        for r in range(4):
            slot()
            need(("pre", r % 2), ("down", r % 2), ("up", r % 2))
            hidden_grad(branch, down_w.at[r % 2], pre.at[r % 2], grad_pre, hidden_sum)
            sums[pl.ds(16 * b + 8 + flip(z, r), 1), :] = hidden_sum[...]
            outer(normed2, grad_pre, grad_w.at[(base + 1) % 2, r])

            part_sum = dot(grad_pre[...], up_w[r % 2], (1, 1))
            if r == 0:
                slope[...] = part_sum
            else:
                slope[...] += part_sum
            if r < 2:
                fetch_mlp(b, r + 2)
            elif b == 1:
                fetch_mlp(0, r - 2)
        slot()
        across(base + 1)
        if b == 1:
            fetch_kept(0, "normed2", normed2)
        slot()
        need("middle", "attn")
        sum_of(b, 6)[...] = jnp.zeros((1, 768), F32)
        sum_of(b, 4)[...] = jnp.zeros((1, 768), F32)

        def after(chunk_rows, value_rows, b=b, scales=scales):
            sums[16 * b + 6 : 16 * b + 7, :] += column_sum(value_rows * buf_p[chunk_rows, :])
            low = (scales[0:1, :] * value_rows).astype(BF)
            branch[chunk_rows, :] = low
            sums[16 * b + 4 : 16 * b + 5, :] += column_sum(low.astype(F32))

        norm_back(buf_q, slope, gains[1:2, :], grad, sum_of(b, 1), sum_of(b, 3), after)
        fetch_kept(b, "resid", buf_q)
        if b == 1:
            fetch_kept(0, "mlp", buf_p)
        slot()
        need("mixed")
        need_attn(0, 1, 2, 3)
        project_rows(branch, attn_w.at[3], None, grad_mixed)
        need("query", "key", "value", "log_total")
        attn_args = (
            query,
            key,
            value,
            key_bias,
            log_total,
            grad_mixed,
            grad_query,
            grad_key,
            grad_value,
        )
        for pair in (0, 2, 4):
            slot()
            attend_pairs_back(pair, pair + 2, *attn_args)
        slot()

        if b == 0:
            for owner, copy in flying:
                if owner < 0:
                    copy.wait_send()
            flying[:] = [(owner, copy) for owner, copy in flying if owner >= 0]
        away[...] = (
            dot(grad_key[rows:, :], attn_w[1]) + dot(grad_value[rows:, :], attn_w[2])
        ).astype(BF)
        slot()
        given = launch(
            [
                remote(
                    away.at[pl.ds(n * rows // EXCHANGE, rows // EXCHANGE)],
                    away_in.at[b, pl.ds(n * rows // EXCHANGE, rows // EXCHANGE)],
                    other.at[0, b * EXCHANGE + n],
                    other.at[1, b * EXCHANGE + n],
                    {"mp": 1},
                )
                for n in range(EXCHANGE)
            ]
        )
        flying.extend((-1, copy) for copy in given)
        slot()
        reuse(base + 2)
        target = grad_w.at[(base + 2) % 2]
        need("normed")
        for kind, left, right in (
            (0, grad_query, normed.at[pl.ds(0, rows)]),
            (1, grad_key, normed),
            (2, grad_value, normed),
            (3, mixed, branch),
        ):
            if kind % 2 == 0:
                slot()
            for h in range(2):
                value_h = dot(left[:, h * 384 : (h + 1) * 384], right[...], (0, 0)).astype(BF)
                for r in range(2):
                    target[2 * h + r, kind * 192 : (kind + 1) * 192, :] = value_h[
                        r * 192 : (r + 1) * 192
                    ]
        slot()
        across(base + 2)
        slot()
        head_sums(b, 0, grad_query, rows)
        head_sums(b, 256, grad_value, 2 * rows)
        slot()

        slope[...] = (
            dot(grad_query[...], attn_w[0])
            + dot(grad_key[0:rows, :], attn_w[1])
            + dot(grad_value[0:rows, :], attn_w[2])
        )
        if b == 1:
            start_attn(0)
            fetch_kept(0, "normed", normed)
            fetch_attn(0)
        slot()
        landed(given)
        slot()

        def join(chunk_rows):
            slope[chunk_rows, :] += away_in[b, chunk_rows, :].astype(F32)

        blocks(rows // 32, 32, join)
        need("resid")
        if b == 1:
            norm_back(buf_q, slope, gains[0:1, :], grad, sum_of(b, 0), sum_of(b, 2))
            fetch_kept(0, "middle", buf_q)
        else:

            def final(chunk_rows, value_rows):
                grad_out[chunk_rows, :] = value_rows.astype(BF)

            norm_back(buf_q, slope, gains[0:1, :], grad, sum_of(b, 0), sum_of(b, 2), final)

        slot()
    slot()
    sums_out[...] = sums[...]
    for own in owns:
        own.wait()
    for _, copy in flying:
        copy.wait_send()
    for j in (COUNT - 2, COUNT - 1):
        for copy in sent[j]:
            copy.wait_send()


LOADS = 40
EXCHANGE = 1
THIRDS = (0, 2, 4)
SUM_STEPS = 7
PLAN = (
    (),
    (),
    (),
    (),
    (),
    (),
    (),
    (),
    (),
    (0,),
    (),
    (),
    (),
    (),
    (),
    (0,),
    (1,),
    (),
    (),
    (),
    (),
    (),
    (),
    (0,),
    (2,),
    (1, 0),
    (),
    (),
    (6,),
    (0,),
    (),
    (1,),
    (2,),
    (6,),
    (0, 3),
    (),
    (6,),
    (),
    (1, 1),
    (0,),
    (6,),
    (3, 2),
    (4,),
    (1,),
    (2,),
    (),
    (),
    (),
    (),
    (2, 1),
    (0, 3, 4),
    (5, 1, 2),
    (3, 2, 2, 4, 5),
    (),
    (),
    (7, 3, 5, 7, 3, 4, 3, 7, 4, 3, 4, 5, 7, 4, 4, 5, 5, 5, 5),
)


def backward_all(locals_, full, kept, cotangent, lengths, params):
    dp_size = lax.axis_size("dp")
    anywhere = pl.BlockSpec(memory_space=pl.ANY)
    vmem = pl.BlockSpec(memory_space=pltpu.VMEM)
    smem = pl.BlockSpec(memory_space=pltpu.SMEM)
    matrix = locals_[2].shape
    size = matrix[0] // PARTS
    rows = cotangent.shape[0]
    more = (dp_size // PARTS).bit_length() - 1
    more_shape = (COUNT, more, 4, size, 768) if more else (16, 128)
    stage_shape = (4, size, 768) if more else (16, 128)
    cut_count, cut_rows = (1, 16) if more else (len(THIRDS), size // 3)
    shape = jax.ShapeDtypeStruct
    steps = SUM_STEPS + more
    flat_kept = [kept[b][name] for b in range(2) for name in KEPT_NAMES]
    scratch = [
        ((2, 4) + matrix, BF),
        ((RING, 2, 2, 4, size, 768), BF),
        ((COUNT, 2, 2, 4, size // 2, 768), BF),
        ((COUNT, 2, 4, size // 2, 768), BF),
        (stage_shape, BF),
        ((COUNT, 3, size, 768), BF),
        ((COUNT, size, 768), BF),
        ((cut_count, 2, 2, 2, cut_rows, 768), BF),
        ((cut_count, 2, 2, cut_rows, 768), BF),
        ((cut_count, 2, cut_rows, 768), BF),
        ((cut_count, cut_rows, 768), BF),
        ((2,) + matrix, BF),
        ((2,) + matrix, BF),
        ((4,) + matrix, BF),
        ((rows, 768), F32),
        ((rows, 768), F32),
        ((rows, 768), F32),
        ((rows, 768), BF),
        ((rows, 768), BF),
        ((4, rows, 768), BF),
        ((2, rows, 768), F32),
        ((rows, 768), BF),
        ((rows, 768), F32),
        ((rows, 768), BF),
        ((2 * rows, 768), BF),
        ((2 * rows, 768), BF),
        ((2 * rows, 768), BF),
        ((rows, 768), BF),
        ((rows, 768), BF),
        ((rows, 768), BF),
        ((2 * rows, 768), BF),
        ((2 * rows, 768), BF),
        ((6, 8, 2 * rows), F32),
        ((rows, 768), BF),
        ((2, rows, 768), BF),
        ((32, 768), F32),
        ((2, steps, 16, 768), F32),
        ((1, 768), F32),
        ((2 * rows, 1), F32),
    ]
    got = pl.pallas_call(
        functools.partial(backward_kernel, dp_size),
        out_shape=[
            shape((COUNT,) + matrix, BF),
            shape(more_shape, BF),
            shape((32, 768), F32),
            shape((rows, 768), BF),
        ],
        in_specs=[anywhere] * (8 + COUNT + 2 * len(KEPT)) + [vmem, smem] + [vmem] * 4,
        out_specs=[anywhere] * 2 + [vmem] * 2,
        scratch_shapes=[pltpu.VMEM(dims, kind) for dims, kind in scratch]
        + [
            pltpu.SemaphoreType.DMA((COUNT, 24 + 2 * more)),
            pltpu.SemaphoreType.DMA((COUNT, 24 + 2 * more)),
            pltpu.SemaphoreType.DMA((LOADS,)),
            pltpu.SemaphoreType.DMA((COUNT,)),
            pltpu.SemaphoreType.REGULAR((1, COUNT)),
            pltpu.SemaphoreType.DMA((2, 2 * EXCHANGE + 2 * steps)),
        ],
        compiler_params=pltpu.CompilerParams(
            collective_id=1, has_side_effects=True, vmem_limit_bytes=63 * 1024 * 1024
        ),
    )(*locals_, *full, *flat_kept, cotangent, lengths, *params)
    return got[0], got[2], got[3]


def finish_kernel(whole, sums, *refs):
    passed, outs, refs = refs[:2], refs[2:24], refs[24:]
    low, high, load, store = refs
    z = lax.axis_index("mp")
    loads = [
        pltpu.make_async_copy(whole.at[j], low.at[j], load.at[j]) for j in range(COUNT)
    ]
    for copy in loads:
        copy.start()
    for source, target in zip(passed, outs[:2]):
        target[...] = source[...]
    stores = []

    def keep(source, target):
        copy = pltpu.make_async_copy(source, target, store.at[len(stores)])
        copy.start()
        stores.append(copy)

    for b in range(2):
        project_in, project_out, up, down = outs[2 + 10 * b : 6 + 10 * b]
        gains, shifts, out_bias, scales, up_bias, project_bias = outs[6 + 10 * b : 12 + 10 * b]
        base = 16 * b
        for row, ref in zip((0, 2, 4, 6), (gains, shifts, out_bias, scales)):
            ref[...] = sums[base + row : base + row + 2, :]
        up_bias[...] = sums[pl.ds(base + 8 + z, 1), :].reshape(768)
        mine = sums[pl.ds(base + 12 + z, 1), :]
        project_bias[0:1, :] = mine[:, 0:192]
        project_bias[1:2, :] = mine[:, 256:448]
    for j in range(COUNT):
        b = 1 if j < 3 else 0
        project_in, project_out, up, down = outs[2 + 10 * b : 6 + 10 * b]
        loads[j].wait()

        def widen(chunk_rows):
            high[j, chunk_rows, :] = low[j, chunk_rows, :].astype(F32)

        blocks(8, 96, widen)
        if j % 3 == 0:
            keep(high.at[j], down)
        elif j % 3 == 1:
            keep(high.at[j], up)
        else:
            keep(high.at[j, pl.ds(0, 576)], project_in)
            keep(high.at[j, pl.ds(576, 192)], project_out)
    for copy in stores:
        copy.wait()


def finish_all(whole, sums, output, grad_input):
    anywhere = pl.BlockSpec(memory_space=pl.ANY)
    vmem = pl.BlockSpec(memory_space=pltpu.VMEM)
    shape = jax.ShapeDtypeStruct
    matrix = whole.shape[1:]
    big = [shape((576, 768), F32), shape((192, 768), F32), shape(matrix, F32), shape(matrix, F32)]
    little = [shape((2, 768), F32)] * 4 + [shape((768,), F32), shape((2, 192), F32)]
    return pl.pallas_call(
        finish_kernel,
        out_shape=[shape(output.shape, BF)] * 2 + (big + little) * 2,
        in_specs=[anywhere] + [vmem] * 3,
        out_specs=[vmem] * 2 + ([anywhere] * 4 + [vmem] * 6) * 2,
        scratch_shapes=[
            pltpu.VMEM((COUNT,) + matrix, BF),
            pltpu.VMEM((COUNT,) + matrix, F32),
            pltpu.SemaphoreType.DMA((COUNT,)),
            pltpu.SemaphoreType.DMA((COUNT + 2,)),
        ],
        compiler_params=pltpu.CompilerParams(vmem_limit_bytes=60 * 1024 * 1024),
    )(whole, sums, output, grad_input)


def local_block(weights):
    p_in, p_out, up, down = weights[2], weights[4], weights[7], weights[9]
    return [p_in.swapaxes(1, 2).reshape(-1, p_in.shape[1]), p_out, up, down]


def arrange(grads):
    project_in, project_out, up, down = grads[:4]
    gains, shifts, out_bias, scales, up_bias, project_bias = grads[4:]
    return (
        gains,
        shifts,
        project_in.reshape(3, 192, 768).swapaxes(1, 2),
        project_bias,
        project_out,
        out_bias,
        scales,
        up,
        up_bias,
        down,
    )


def body(inputs, lengths, cotangent, *params):
    blocks_ = params[:10], params[10:]
    locals_ = local_block(blocks_[0]) + local_block(blocks_[1])
    forward_params = [weights[p] for weights in blocks_ for p in (0, 1, 5, 6, 3, 8)]
    full, kept, output = forward_all(locals_, inputs, lengths, forward_params)
    backward_params = [weights[p] for weights in blocks_ for p in (0, 6)]
    whole, sums, grad_input = backward_all(
        locals_, full, kept, cotangent, lengths, backward_params
    )
    outs = finish_all(whole, sums, output, grad_input)
    return tuple(outs[:2]) + arrange(outs[2:12]) + arrange(outs[12:22])


def solution(mesh):
    rows = P(("dp", "mp"), None)
    weights = (
        P(),
        P(),
        P(None, None, "mp"),
        P(None, "mp"),
        P("mp", None),
        P(),
        P(),
        P(None, "mp"),
        P("mp"),
        P("mp", None),
    )
    in_specs = (rows, P("dp"), rows) + weights + weights
    out_specs = (rows, rows) + weights + weights
    return jax.shard_map(body, mesh=mesh, in_specs=in_specs, out_specs=out_specs, check_vma=False)
```

```python
import functools

import jax
import jax.numpy as jnp
from jax import lax
from jax.experimental import pallas as pl
from jax.experimental.pallas import tpu as pltpu
from jax.sharding import PartitionSpec as P

HEAD_DIM = 64
SLOT = 640
PARTS = 8
BF = jnp.bfloat16
F32 = jnp.float32

epsilon = 1e-06

MESH = pl.DeviceIdType.MESH
COUNT = 6


def flip(index, bits):
    bit = 1
    while bit <= bits:
        if bits & bit:
            index = index + bit - 2 * bit * lax.rem(lax.div(index, bit), 2)
        bit *= 2
    return index


def partners(dp_size):
    bits = [{"dp": 6}]
    bit = 1
    while bit < dp_size:
        bits.append({"dp": bit})
        bit *= 2
    return bits + [{"mp": r} for r in (1, 2, 3)]


def device_at(bits):
    return {axis: flip(lax.axis_index(axis), bit) for axis, bit in bits.items()}


def enter(dp_size):
    barrier = pltpu.get_barrier_semaphore()
    for bits in partners(dp_size):
        pl.semaphore_signal(barrier, inc=1, device_id=device_at(bits), device_id_type=MESH)
    pl.semaphore_wait(barrier, len(partners(dp_size)))


def remote(source, target, send, recv, bits):
    return pltpu.make_async_remote_copy(
        src_ref=source,
        dst_ref=target,
        send_sem=send,
        recv_sem=recv,
        device_id=device_at(bits),
        device_id_type=MESH,
    )


def piece_rows(index, size):
    return pl.ds(pl.multiple_of(index * size, size), size)


def dot(left_side, right_side, contract=(1, 0)):
    return lax.dot_general(
        left_side,
        right_side,
        (((contract[0],), (contract[1],)), ((), ())),
        preferred_element_type=F32,
    )


def blocks(count, size, body):
    @pl.loop(0, count)
    def _(i):
        body(pl.ds(pl.multiple_of(i * size, size), size))


def norm_parts(values):
    center = values - jnp.mean(values, axis=-1, keepdims=True)
    spread = jnp.mean(center * center, axis=-1, keepdims=True)
    inverse = lax.rsqrt(spread + epsilon)
    return center * inverse, inverse


def norm_rows(source, gain, shift, target):
    unit, _ = norm_parts(source[...])
    target[...] = (unit * gain + shift).astype(BF)


def project_rows(source, weight, bias, target):
    value = dot(source[...], weight[...].reshape(768, 768), (1, 1))
    if bias is not None:
        value = value + bias[...]
    target[...] = value.astype(BF)


def low_lanes(shape):
    return lax.broadcasted_iota(jnp.int32, shape, 1) < HEAD_DIM


def two_heads(pair, low):
    nothing = jnp.zeros_like(pair)
    return jnp.concatenate([jnp.where(low, pair, nothing), jnp.where(low, nothing, pair)])


def attend_pairs(first, last, query, key, value, key_bias, mixed, log_total):
    rows = query.shape[0]

    @pl.loop(first, last)
    def _(p):
        lanes = pl.ds(pl.multiple_of(p * 128, 128), 128)
        low = low_lanes((rows, 128))
        both = two_heads(query[:, lanes], low)
        scores = dot(both, key[:, lanes], (1, 1)) * HEAD_DIM ** (-0.5) + key_bias[...]
        peak = jnp.max(scores, axis=1, keepdims=True)
        exponent = jnp.exp(scores - peak)
        total = jnp.sum(exponent, axis=1, keepdims=True)
        probs = (exponent * (1.0 / total)).astype(BF)
        result = dot(probs, value[:, lanes])
        logs = jnp.broadcast_to(peak + jnp.log(total), (2 * rows, 128))
        log_total[p, :, :] = logs.T[0:8, :]
        mixed[:, lanes] = jnp.where(low, result[0:rows], result[rows:]).astype(BF)


def attend_out(mixed, weight, bias, scale, resid, attn, middle):
    value = dot(mixed[...], weight[...].reshape(768, 768)) + bias[...]
    attn[...] = value
    middle[...] = resid[...] + scale[...] * value


def gelu_exact(values):
    return 0.5 * values * (1.0 + lax.erf(values * (0.5**0.5)))


def mlp_up(r, normed, up, up_bias, pre, hidden):
    value = dot(normed[...], up[r]) + up_bias[r : r + 1, :]
    pre[r] = value
    hidden[r] = gelu_exact(value).astype(BF)


def mlp_down(hidden, down, bias, mlp):
    value = dot(hidden[0], down[0])
    for r in (1, 2, 3):
        value = value + dot(hidden[r], down[r])
    mlp[...] = value + bias[...]


def attend_pairs_back(
    first, last, query, key, value, key_bias, log_total, grad, grad_query, grad_key, grad_value
):
    rows = query.shape[0]
    scale = HEAD_DIM ** (-0.5)

    @pl.loop(first, last)
    def _(p):
        lanes = pl.ds(pl.multiple_of(p * 128, 128), 128)
        low = low_lanes((rows, 128))
        both = two_heads(query[:, lanes], low)
        both_grad = two_heads(grad[:, lanes], low)
        key_pair = key[:, lanes]
        scores = dot(key_pair, both, (1, 1)) * scale + key_bias[...]
        probs = jnp.exp(scores - log_total[p, 0:1, :])
        grad_value[:, lanes] = dot(probs.astype(BF), both_grad).astype(BF)
        grad_probs = dot(value[:, lanes], both_grad, (1, 1))
        inner = jnp.sum(probs * grad_probs, axis=0, keepdims=True)
        grad_scores = (probs * (grad_probs - inner)).astype(BF)
        grad_key[:, lanes] = (dot(grad_scores, both) * scale).astype(BF)
        result = dot(grad_scores, key_pair, (0, 0)) * scale
        grad_query[:, lanes] = jnp.where(low, result[0:rows], result[rows:]).astype(BF)


def gelu_slope(values):
    bell = jnp.exp(-0.5 * values * values) * 0.3989422804014327
    return 0.5 * (1.0 + lax.erf(values * (0.5**0.5))) + values * bell


def column_sum(values):
    return jnp.sum(values, axis=0, keepdims=True)


def branch_grad(grad, mlp, scale, branch, scale_sum, bias_sum):
    scale_sum[...] = jnp.zeros_like(scale_sum)
    bias_sum[...] = jnp.zeros_like(bias_sum)

    def body(rows):
        value = grad[rows, :]
        scale_sum[...] += column_sum(value * mlp[rows, :])
        low = (scale * value).astype(BF)
        branch[rows, :] = low
        bias_sum[...] += column_sum(low.astype(F32))

    blocks(grad.shape[0] // 32, 32, body)


def norm_back(source, slope, gain, grad, gain_sum, shift_sum, after=None):
    gain_sum[...] = jnp.zeros_like(gain_sum)
    shift_sum[...] = jnp.zeros_like(shift_sum)

    def body(rows):
        unit, inverse = norm_parts(source[rows, :])
        value = slope[rows, :]
        gain_sum[...] += column_sum(value * unit)
        shift_sum[...] += column_sum(value)
        scaled = value * gain
        value = (
            scaled
            - jnp.mean(scaled, axis=-1, keepdims=True)
            - unit * jnp.mean(scaled * unit, axis=-1, keepdims=True)
        )
        value = grad[rows, :] + inverse * value
        grad[rows, :] = value
        if after is not None:
            after(rows, value)

    blocks(source.shape[0] // 160, 160, body)


def outer(left_side, right_side, target):
    target[...] = dot(left_side[...], right_side[...], (0, 0)).astype(BF)


def hidden_grad(branch, down, pre, grad_pre, bias_sum):
    value = dot(branch[...], down[...], (1, 1)) * gelu_slope(pre[...])
    low = value.astype(BF)
    grad_pre[...] = low
    bias_sum[...] = column_sum(low.astype(F32))


KEPT = (
    ("resid", (320, 768), F32),
    ("normed", (640, 768), BF),
    ("query", (320, 768), BF),
    ("key", (640, 768), BF),
    ("value", (640, 768), BF),
    ("log_total", (6, 8, 640), F32),
    ("mixed", (320, 768), BF),
    ("attn", (320, 768), F32),
    ("middle", (320, 768), F32),
    ("normed2", (320, 768), BF),
    ("pre", (4, 320, 768), F32),
    ("hidden", (4, 320, 768), BF),
    ("mlp", (320, 768), F32),
)
KEPT_NAMES = [name for name, _, _ in KEPT]


FORWARD_PLAN = (
    (),
    (0,),
    (),
    (),
    (0, 1, 0, 2, 0, 1),
    (),
    (3, 2),
    (),
    (4,),
    (),
    (1, 2),
    (3,),
    (),
    (1,),
    (),
    (5,),
    (),
    (),
    (2,),
    (4,),
    (),
    (),
    (),
    (),
    (3, 5, 3),
    (),
    (),
    (),
    (),
    (4,),
    (5,),
    (),
    (4,),
    (),
    (),
    (),
    (),
    (5,),
    (),
    (),
    (),
    (),
    (),
)


def attn_chunk(local, full, i, r, kind):
    if r:
        return full[i].at[r - 1, pl.ds(kind * 192, 192)]
    project_in, project_out = local[i // 3][:2]
    return project_in.at[pl.ds(kind * 192, 192)] if kind < 3 else project_out


def forward_kernel(*refs):
    refs = list(refs)

    def take(count):
        got = refs[:count]
        del refs[:count]
        return got

    local = [take(4), take(4)]
    inputs, lengths = take(2)
    params = [take(6), take(6)]
    full = take(COUNT)
    kept_out = [dict(zip(KEPT_NAMES, take(len(KEPT)))) for _ in range(2)]
    (output,) = take(1)
    kept = [{name: ref.at[b] for name, ref in zip(KEPT_NAMES, refs)} for b in range(2)]
    take(len(KEPT))
    attn_w, up_w, down_w, small, small_in, key_bias, in_bias, up_bias = take(8)
    send, recv, other, load, store = take(5)
    size = full[0].shape[1] // PARTS
    rows = inputs.shape[0]
    me = lax.rem(lax.axis_index("dp"), PARTS)
    z = lax.axis_index("mp")
    flying = []
    waiting = []

    def part(mask):
        return piece_rows(flip(me, mask), size)

    def place(i, chunks, mask, half=None):
        b, kind = divmod(i, 3)
        index = flip(me, mask)
        start, count = index * size, size
        if kind == 0:
            start = lax.rem(index, 2) * size
        if half is not None:
            start, count = start + half * (size // 2), size // 2
        where = pl.ds(pl.multiple_of(start, count), count)
        if kind == 0:
            return attn_w.at[b, lax.div(index, 2), chunks, where]
        return (up_w if kind == 1 else down_w).at[b, chunks, where]

    def slab(i, mask, half=None):
        return place(i, pl.ds(1, 3), mask, half)

    def along_z(i):
        b, kind = divmod(i, 3)

        def copies(source, rows_of):
            return [
                remote(
                    source.at[rows_of],
                    place(i, r, 0),
                    send.at[i, r - 1],
                    recv.at[i, r - 1],
                    {"mp": r},
                )
                for r in (1, 2, 3)
            ]

        if kind:
            return launch(copies(local[b][1 + kind], part(0)))
        project_in, project_out = local[b][:2]
        inner = project_in.shape[0] // size

        @pl.when(me < inner)
        def _():
            for copy in copies(project_in, part(0)):
                copy.start()

        @pl.when(me >= inner)
        def _():
            for copy in copies(project_out, piece_rows(lax.max(me - inner, 0), size)):
                copy.start()

        started = copies(project_out, pl.ds(0, size))
        flying.extend(started)
        return started

    def along_dp(i, slot, mask, bit, half=None):
        there = slab(i, mask, half)
        return remote(there, there, send.at[i, slot], recv.at[i, slot], {"dp": bit})

    def launch(copies):
        for copy in copies:
            copy.start()
        flying.extend(copies)
        return copies

    def landed(copies):
        for copy in copies:
            copy.wait_recv()

    state = [None] * COUNT

    at = [0] * COUNT
    bias_in = []
    plan = iter(FORWARD_PLAN)

    def slot():
        for i in next(plan):
            stage(i, at[i])
            at[i] += 1

    def stage(i, s):
        if s == 0:
            state[i] = along_z(i)
        elif s == 1:
            landed(state[i])
            state[i] = launch([along_dp(i, 3, 0, 2), along_dp(i, 4, 0, 4)])
            launch([along_dp(i, 7, 0, 1)])
            if i == 0:
                bias_in.extend(
                    launch(
                        [
                            remote(
                                small.at[r],
                                small_in.at[r - 1],
                                other.at[0, r - 1],
                                other.at[1, r - 1],
                                {"mp": r},
                            )
                            for r in (1, 2, 3)
                        ]
                    )
                )
        elif s == 2:
            landed(state[i])
            state[i] = launch([along_dp(i, 5, 2, 4, 0), along_dp(i, 6, 4, 2, 1)])
            launch([along_dp(i, 8, 2, 1), along_dp(i, 9, 4, 1)])
        elif s == 3:
            landed(state[i])
            launch([along_dp(i, 10, 6, 1)])

    def complete(i):
        for slot, mask in ((7, 0), (8, 2), (9, 4), (10, 6)):
            along_dp(i, slot, mask, 1).wait_recv()
        b, kind = divmod(i, 3)
        finish(owned[b][:4] if kind == 0 else owned[b][3 + kind : 4 + kind])
        save_full(i)

    def load_own():
        for b in range(2):
            project_in, project_out, up, down = local[b]
            copies = [
                pltpu.make_async_copy(
                    project_in.at[pl.ds(kind * 192, 192)], attn_w.at[b, kind, 0], load.at[b, kind]
                )
                for kind in range(3)
            ]
            copies += [
                pltpu.make_async_copy(project_out, attn_w.at[b, 3, 0], load.at[b, 3]),
                pltpu.make_async_copy(up, up_w.at[b, 0], load.at[b, 4]),
                pltpu.make_async_copy(down, down_w.at[b, 0], load.at[b, 5]),
            ]
            for copy in copies:
                copy.start()
            owned.append(copies)

    def save_full(i):
        b, kind = divmod(i, 3)
        if kind == 0:
            copies = [
                pltpu.make_async_copy(
                    attn_w.at[b, n, pl.ds(1, 3)],
                    full[i].at[:, pl.ds(n * 192, 192)],
                    load.at[b, 6 + n],
                )
                for n in range(4)
            ]
        else:
            source = up_w if kind == 1 else down_w
            copies = [
                pltpu.make_async_copy(source.at[b, pl.ds(1, 3)], full[i], load.at[b, 9 + kind])
            ]
        for copy in copies:
            copy.start()
        waiting.extend(copies)

    owned = []

    def finish(copies):
        for copy in copies:
            copy.wait()

    def save(b, *names):
        for name in names:
            copy = pltpu.make_async_copy(
                kept[b][name], kept_out[b][name], store.at[b, KEPT_NAMES.index(name)]
            )
            copy.start()
            waiting.append(copy)

    def exchange(b):
        copy = remote(
            kept[b]["normed"].at[pl.ds(0, rows)],
            kept[b]["normed"].at[pl.ds(rows, rows)],
            other.at[0, 3 + b],
            other.at[1, 3 + b],
            {"mp": 1},
        )
        return launch([copy])

    load_own()
    small[...] = jnp.zeros_like(small)
    for b in range(2):
        project_bias, hidden_bias = params[b][4:]
        for r in range(4):
            small[r, 3 * b : 3 * b + 1, :] = hidden_bias[...].reshape(1, 768)
            small[r, 3 * b + 1 : 3 * b + 3, r * 192 : (r + 1) * 192] = project_bias[...]
    enter(lax.axis_size("dp"))
    slot()
    slot()

    def widen(part_rows):
        kept[0]["resid"][part_rows, :] = inputs[part_rows, :].astype(F32)

    blocks(10, 32, widen)
    position = lax.broadcasted_iota(jnp.int32, (1, 2 * rows), 1)
    shifted = position + lax.rem(z, 2) * jnp.where(position < rows, rows, -rows)
    key_bias[...] = jnp.where(shifted < lengths[lax.div(z, 2)], 0.0, -1e30).astype(F32)

    def first_norm(b):
        gains, shifts = params[b][:2]
        k = kept[b]
        slot()
        norm_rows(k["resid"], gains[0:1, :], shifts[0:1, :], k["normed"].at[pl.ds(0, rows)])
        save(b, "resid")

    first_norm(0)
    for b in range(2):
        k = kept[b]
        gains, shifts, out_bias, scales = params[b][:4]
        base = 3 * b
        slot()
        swapped = exchange(b)
        slot()
        complete(base)
        if b == 0:
            landed(bias_in)
            joined = small[0] + small_in[0] + small_in[1] + small_in[2]
            for c in range(2):
                in_bias[c, 1:3] = joined[3 * c + 1 : 3 * c + 3]
                up_bias[c, 0:1] = small[0, 3 * c : 3 * c + 1]
                for r in (1, 2, 3):
                    up_bias[c, r : r + 1] = small_in[r - 1, 3 * c : 3 * c + 1]
        project_bias = in_bias.at[b]
        slot()
        landed(swapped)
        slot()
        project_rows(
            k["normed"].at[pl.ds(0, rows)],
            attn_w.at[b, 0],
            project_bias.at[pl.ds(1, 1)],
            k["query"],
        )
        slot()
        project_rows(k["normed"], attn_w.at[b, 1], None, k["key"])
        slot()
        project_rows(k["normed"], attn_w.at[b, 2], project_bias.at[pl.ds(2, 1)], k["value"])
        save(b, "normed", "query", "key", "value")
        pair_args = (k["query"], k["key"], k["value"], key_bias, k["mixed"], k["log_total"])
        for pair in (0, 2, 4):
            slot()
            attend_pairs(pair, pair + 2, *pair_args)
        save(b, "log_total", "mixed")
        slot()
        attend_out(
            k["mixed"],
            attn_w.at[b, 3],
            out_bias.at[pl.ds(0, 1)],
            scales.at[pl.ds(0, 1)],
            k["resid"],
            k["attn"],
            k["middle"],
        )
        slot()
        norm_rows(k["middle"], gains[1:2, :], shifts[1:2, :], k["normed2"])
        save(b, "attn", "middle", "normed2")
        slot()
        complete(base + 1)
        for r in range(4):
            slot()
            mlp_up(r, k["normed2"], up_w.at[b], up_bias.at[b], k["pre"], k["hidden"])
        save(b, "pre", "hidden")
        slot()
        complete(base + 2)
        slot()
        mlp_down(k["hidden"], down_w.at[b], out_bias.at[pl.ds(1, 1)], k["mlp"])
        save(b, "mlp")
        slot()

        def result(part_rows):
            value = k["middle"][part_rows, :] + scales[1:2, :] * k["mlp"][part_rows, :]
            if b == 0:
                kept[1]["resid"][part_rows, :] = value
            else:
                output[part_rows, :] = value.astype(BF)

        blocks(10, 32, result)
        if b == 0:
            first_norm(1)
    slot()
    for copy in flying:
        copy.wait_send()
    finish(waiting)


def forward_all(locals_, inputs, lengths, params):
    anywhere = pl.BlockSpec(memory_space=pl.ANY)
    vmem = pl.BlockSpec(memory_space=pltpu.VMEM)
    smem = pl.BlockSpec(memory_space=pltpu.SMEM)
    matrix = locals_[2].shape
    kept_shapes = [jax.ShapeDtypeStruct(shape, kind) for _, shape, kind in KEPT]
    got = pl.pallas_call(
        forward_kernel,
        out_shape=[jax.ShapeDtypeStruct((3,) + matrix, BF)] * COUNT
        + kept_shapes * 2
        + [jax.ShapeDtypeStruct(inputs.shape, BF)],
        in_specs=[anywhere] * 8 + [vmem, smem] + [vmem] * 12,
        out_specs=[anywhere] * (COUNT + 2 * len(KEPT)) + [vmem],
        scratch_shapes=[pltpu.VMEM((2,) + shape, kind) for _, shape, kind in KEPT]
        + [
            pltpu.VMEM((2, 4, 4, 192, 768), BF),
            pltpu.VMEM((2, 4) + matrix, BF),
            pltpu.VMEM((2, 4) + matrix, BF),
            pltpu.VMEM((4, 8, 768), F32),
            pltpu.VMEM((3, 8, 768), F32),
            pltpu.VMEM((1, 2 * inputs.shape[0]), F32),
            pltpu.VMEM((2, 8, 768), F32),
            pltpu.VMEM((2, 8, 768), F32),
            pltpu.SemaphoreType.DMA((COUNT, 11)),
            pltpu.SemaphoreType.DMA((COUNT, 11)),
            pltpu.SemaphoreType.DMA((2, 5)),
            pltpu.SemaphoreType.DMA((2, 12)),
            pltpu.SemaphoreType.DMA((2, len(KEPT))),
        ],
        compiler_params=pltpu.CompilerParams(
            collective_id=0, has_side_effects=True, vmem_limit_bytes=63 * 1024 * 1024
        ),
    )(*locals_, inputs, lengths, *params)
    full = got[:COUNT]
    kept = [
        dict(zip(KEPT_NAMES, got[COUNT + b * len(KEPT) : COUNT + (b + 1) * len(KEPT)]))
        for b in range(2)
    ]
    return full, kept, got[-1]


RING = 3


def backward_kernel(dp_size, *refs):
    refs = list(refs)

    def take(count):
        got = refs[:count]
        del refs[:count]
        return got

    local = [take(4), take(4)]
    full = take(COUNT)
    kept = [dict(zip(KEPT_NAMES, take(len(KEPT)))) for _ in range(2)]
    cotangent, lengths = take(2)
    params = [take(2), take(2)]
    (whole, more_in, sums_out, grad_out) = take(4)
    (grad_w, core_in, first_in, second_in, more_stage, z_in, piece) = take(7)
    (near_in, far_in, turn_in, last_in) = take(4)
    (up_w, down_w, attn_w) = take(3)
    (grad, buf_p, buf_q, branch, normed2, hidden, pre) = take(7)
    (grad_pre, slope, query, key, value, normed, mixed) = take(7)
    (grad_mixed, grad_query, grad_key, grad_value, log_total) = take(5)
    (away, away_in, sums, sums_in, hidden_sum, key_bias) = take(6)
    (send, recv, load, store, free, other) = take(6)
    rows = grad.shape[0]
    size = piece.shape[1]
    me = lax.rem(lax.axis_index("dp"), PARTS)
    z = lax.axis_index("mp")
    more = [PARTS << e for e in range((dp_size // PARTS).bit_length() - 1)]
    thirds = () if more else THIRDS

    def part(mask):
        return piece_rows(flip(me, mask), size)

    slots = {}
    pending = {}

    def fetch(name, source, target):
        slot = slots.setdefault(name, len(slots))
        copy = pltpu.make_async_copy(source, target, load.at[slot])
        copy.start()
        pending[name] = copy

    def need(*names):
        for name in names:
            pending.pop(name).wait()

    def fetch_kept(b, name, target):
        fetch(name, kept[b][name], target)

    def chunk(i, r):
        return local[i // 3][1 + i % 3] if r == 0 else full[i].at[r - 1]

    def fetch_mlp(b, r):
        fetch(("pre", r % 2), kept[b]["pre"].at[r], pre.at[r % 2])
        fetch(("up", r % 2), chunk(3 * b + 1, r), up_w.at[r % 2])
        fetch(("down", r % 2), chunk(3 * b + 2, r), down_w.at[r % 2])

    def fetch_attn(b):
        for kind in range(4):
            for r in range(4):
                fetch(
                    ("attn", kind, r),
                    attn_chunk(local, full, 3 * b, r, kind),
                    attn_w.at[kind, pl.ds(r * 192, 192)],
                )

    def need_attn(*kinds):
        for kind in kinds:
            need(*[("attn", kind, r) for r in range(4)])

    flying = []
    state = [None] * (COUNT + 2)
    sent = [[] for _ in range(COUNT)]
    at = [0] * (COUNT + 2)

    def launch(copies):
        for copy in copies:
            copy.start()
        return copies

    def landed(copies):
        for copy in copies:
            copy.wait_recv()

    def added(left, right):
        left[...] = left[...] + right[...]

    def add_slabs(target, source):
        @pl.loop(0, 4)
        def _(r):
            added(target.at[r], source.at[r])

    half = [pl.ds(0, size // 2), pl.ds(size // 2, size // 2)]
    third = size // 3
    cut = [pl.ds(n * third, third) for n in range(3)]
    joint = pl.ds(0, 2 * third)

    def add_own(j, high, low, n=None):
        first, count = (0, size) if n is None else (n * third, third)
        start = flip(me, 4 * high + 2 * low) * size + first
        own = pl.ds(pl.multiple_of(start, count), count)

        @pl.loop(0, 4)
        def _(r):
            added(
                core_in.at[j % RING, high, low, r, pl.ds(first, count)], grad_w.at[j % 2, r, own]
            )

    def each_slot(body):
        for high in range(2):
            for low in range(2):
                body(high, low)

    owns = []

    def credit(stage, j, bits):
        if j < COUNT:
            pl.semaphore_signal(
                free.at[stage, j], inc=1, device_id=device_at(bits), device_id_type=MESH
            )

    def spend(stage, j):
        if j >= RING:
            pl.semaphore_wait(free.at[stage, j], 1)

    def across(j):
        spend(0, j)
        state[j] = launch(
            [
                remote(
                    grad_w.at[j % 2, :, part(1 | 4 * high | 2 * low)],
                    core_in.at[j % RING, high, low],
                    send.at[j, 2 * high + low],
                    recv.at[j, 2 * high + low],
                    {"dp": 1},
                )
                for high in range(2)
                for low in range(2)
            ]
        )
        sent[j] = list(state[j])

    def reuse(j):
        if j >= 2:
            for copy in sent[j - 2]:
                copy.wait_send()

    def spread(j, slot, mask, bit, half=None):
        if half is None:
            place = whole.at[j, part(mask)]
        else:
            start = flip(me, mask) * size + half * (size // 2)
            place = whole.at[j, pl.ds(pl.multiple_of(start, size // 2), size // 2)]
        source = piece.at[j] if mask == 0 else place
        return remote(source, place, send.at[j, slot], recv.at[j, slot], {"dp": bit})

    def advance(*matrices):
        for j in matrices:
            (stage if j < COUNT else sum_stage)(j, at[j])
            at[j] += 1

    def send_out(j, slot, source, target, bits):
        copies = launch([remote(source, target, send.at[j, slot], recv.at[j, slot], bits)])
        flying.extend((j, copy) for copy in copies)
        return copies[0]

    def stage(j, s):
        core = core_in.at[j % RING]
        if j in thirds and s < 5:
            third_stage(j, s, core)
        elif s == 0:
            landed(state[j])
            add_own(j, 1, 1)
            add_own(j, 0, 1)
            state[j] = [
                send_out(j, 4, core.at[:, 1, :, half[0]], first_in.at[j, 0], {"dp": 2})
            ]
            add_own(j, 1, 0)
            state[j].append(
                send_out(j, 5, core.at[1, :, :, half[1]], first_in.at[j, 1], {"dp": 4})
            )
            add_own(j, 0, 0)
        elif s == 1:
            got = state[j]
            state[j] = []
            for h, bit in enumerate((4, 2)):
                landed(got[h : h + 1])
                away_part = core.at[1, 0, :, half[0]] if h == 0 else core.at[0, 1, :, half[1]]
                add_slabs(away_part, first_in.at[j, h, 1])
                state[j].append(
                    send_out(j, 6 + h, away_part, second_in.at[j, h], {"dp": bit})
                )
            for h in range(2):
                add_slabs(core.at[0, 0, :, half[h]], first_in.at[j, h, 0])
        elif s == 2:
            landed(state[j])
            for h in range(2):
                add_slabs(core.at[0, 0, :, half[h]], second_in.at[j, h])
            mine = core.at[0, 0]
            for e, bit in enumerate(more):
                copy = remote(
                    mine, more_in.at[j, e], send.at[j, 24 + e], recv.at[j, 24 + e], {"dp": bit}
                )
                copy.start()
                copy.wait()
                back = pltpu.make_async_copy(more_in.at[j, e], more_stage, load.at[LOADS - 1])
                back.start()
                back.wait()
                add_slabs(mine, more_stage)
            state[j] = [
                send_out(j, 7 + r, mine.at[r], z_in.at[j, r - 1], {"mp": r}) for r in (1, 2, 3)
            ]
        elif s == 3:
            landed(state[j])
            total = core[0, 0, 0].astype(F32)
            for r in range(3):
                total = total + z_in[j, r].astype(F32)
            piece[j] = total.astype(BF)
            give_piece(j)
        elif s == 5:
            landed(state[j])
            state[j] = launch([spread(j, 13, 2, 4, 0), spread(j, 14, 4, 2, 1)])
            core_copies = launch([spread(j, 16, 2, 1), spread(j, 17, 4, 1)])
            flying.extend((j, copy) for copy in state[j] + core_copies)
        elif s == 6:
            landed(state[j])
            core_copies = launch([spread(j, 18, 6, 1)])
            flying.extend((j, copy) for copy in core_copies)
            state[j] = [spread(j, 15 + n, mask, 1) for n, mask in enumerate((0, 2, 4, 6))]
        elif s == 7:
            landed(state[j])

    def give_piece(j):
        state[j] = launch([spread(j, 11, 0, 2), spread(j, 12, 0, 4)])
        core_copy = launch([spread(j, 15, 0, 1)])
        own = pltpu.make_async_copy(piece.at[j], whole.at[j, part(0)], store.at[j])
        own.start()
        owns.append(own)
        if j + RING < COUNT:
            for owner, copy in flying:
                if owner == j:
                    copy.wait_send()
            flying[:] = [(owner, copy) for owner, copy in flying if owner != j]
            credit(0, j + RING, {"dp": 1})
        flying.extend((j, copy) for copy in state[j] + core_copy)

    def third_stage(j, s, core):
        n_third = thirds.index(j)
        near, far, turn, last = (
            ref.at[n_third] for ref in (near_in, far_in, turn_in, last_in)
        )
        if s == 0:
            landed(state[j])
            add_own(j, 0, 1, 0)
            add_own(j, 1, 1, 0)
            state[j] = [
                send_out(
                    j, 4, core.at[:, 1, :, cut[0]], first_in.at[j, 0, :, :, pl.ds(0, third)], {"dp": 2}
                )
            ]
            add_own(j, 1, 0, 1)
            add_own(j, 1, 1, 1)
            state[j].append(
                send_out(
                    j, 5, core.at[1, :, :, cut[1]], first_in.at[j, 1, :, :, pl.ds(0, third)], {"dp": 4}
                )
            )
            each_slot(lambda high, low: add_own(j, high, low, 2))
            state[j] += [
                send_out(j, 19 + n, core.at[:, :, 1 + 2 * n, cut[2]], near.at[n], {"mp": 1})
                for n in range(2)
            ]
            add_own(j, 0, 0, 0)
            add_own(j, 1, 0, 0)
            add_own(j, 0, 0, 1)
            add_own(j, 0, 1, 1)
        elif s == 1:
            got = state[j]
            state[j] = []
            for h, bit in enumerate((4, 2)):
                landed(got[h : h + 1])
                away_part = core.at[1, 0, :, cut[0]] if h == 0 else core.at[0, 1, :, cut[1]]
                add_slabs(away_part, first_in.at[j, h, 1, :, pl.ds(0, third)])
                state[j].append(
                    send_out(
                        j, 6 + h, away_part, second_in.at[j, h, :, pl.ds(0, third)], {"dp": bit}
                    )
                )
            landed(got[2:])
            for n in (1, 0):
                each_slot(
                    lambda high, low: added(
                        core.at[high, low, 2 * n, cut[2]], near.at[n, high, low]
                    )
                )
                if n:
                    state[j].append(
                        send_out(j, 21, core.at[:, :, 2, cut[2]], far, {"mp": 2})
                    )
            for h in range(2):
                add_slabs(core.at[0, 0, :, cut[h]], first_in.at[j, h, 0, :, pl.ds(0, third)])
        elif s == 2:
            landed(state[j][2:])
            each_slot(
                lambda high, low: added(core.at[high, low, 0, cut[2]], far.at[high, low])
            )
            turned = send_out(j, 22, core.at[:, 1, 0, cut[2]], turn, {"dp": 2})
            landed(state[j][:2])
            for h in range(2):
                add_slabs(core.at[0, 0, :, cut[h]], second_in.at[j, h, :, pl.ds(0, third)])
            mine = core.at[0, 0, :, joint]
            state[j] = [turned] + [
                send_out(j, 7 + r, mine.at[r], z_in.at[j, r - 1, joint], {"mp": r})
                for r in (1, 2, 3)
            ]
        elif s == 3:
            landed(state[j][:1])
            added(core.at[1, 0, 0, cut[2]], turn.at[1])
            final = send_out(j, 23, core.at[1, 0, 0, cut[2]], last, {"dp": 4})
            added(core.at[0, 0, 0, cut[2]], turn.at[0])
            landed(state[j][1:])
            total = core[0, 0, 0, joint, :].astype(F32)
            for r in range(3):
                total = total + z_in[j, r, joint, :].astype(F32)
            piece[j, joint, :] = total.astype(BF)
            state[j] = [final]
        else:
            landed(state[j])
            mine = core.at[0, 0, 0, cut[2]]
            added(mine, last)
            piece[j, cut[2], :] = mine[...]
            give_piece(j)

    def sum_send(b, step, bits):
        place = 2 * EXCHANGE + (SUM_STEPS + len(more)) * b + step
        copy = remote(
            sums.at[pl.ds(16 * b, 16)],
            sums_in.at[b, step],
            other.at[0, place],
            other.at[1, place],
            bits,
        )
        copy.start()
        return copy

    def sum_stage(j, s):
        b = 7 - j
        mine = sums.at[pl.ds(16 * b, 16)]
        if s:
            for copy in state[j]:
                copy.wait()
        if s == 0:
            state[j] = [sum_send(b, r - 1, {"mp": r}) for r in (1, 2, 3)]
        elif s == 1:
            mine[...] = (mine[...] + sums_in[b, 0]) + (sums_in[b, 1] + sums_in[b, 2])
            state[j] = [sum_send(b, 3, {"dp": 1})]
        elif s == 2:
            mine[...] += sums_in[b, 3]
            for e, bit in enumerate(more):
                sum_send(b, SUM_STEPS + e, {"dp": bit}).wait()
                mine[...] += sums_in[b, SUM_STEPS + e]
            state[j] = [sum_send(b, 3 + n, {"dp": 2 * n}) for n in (1, 2, 3)]
        elif s == 3:
            mine[...] = (mine[...] + sums_in[b, 4]) + (sums_in[b, 5] + sums_in[b, 6])

    def start_block(b):
        fetch_kept(b, "mlp", buf_p)
        fetch_kept(b, "hidden", hidden)
        fetch_mlp(b, 0)
        fetch_mlp(b, 1)
        fetch_kept(b, "normed2", normed2)

    def start_attn(b):
        fetch_kept(b, "mixed", mixed)
        fetch_kept(b, "query", query)
        fetch_kept(b, "key", key)
        fetch_kept(b, "value", value)
        fetch_kept(b, "log_total", log_total)

    def sum_of(b, row):
        return sums.at[pl.ds(16 * b + row, 1)]

    def head_sums(b, lane, source, count):
        hidden_sum[...] = jnp.zeros_like(hidden_sum)

        def body(chunk_rows):
            hidden_sum[...] += column_sum(source[chunk_rows, :].astype(F32))

        blocks(count // 160, 160, body)
        for r in range(4):
            row = pl.ds(16 * b + 12 + flip(z, r), 1)
            sums[row, lane : lane + 192] = hidden_sum[:, r * 192 : (r + 1) * 192]

    start_block(1)
    fetch_kept(1, "middle", buf_q)
    start_attn(1)
    fetch_kept(1, "normed", normed)
    fetch_attn(1)
    enter(dp_size)
    sums[...] = jnp.zeros_like(sums)
    position = lax.broadcasted_iota(jnp.int32, (2 * rows, 1), 0)
    shifted = position + lax.rem(z, 2) * jnp.where(position < rows, rows, -rows)
    key_bias[...] = jnp.where(shifted < lengths[lax.div(z, 2)], 0.0, -1e30).astype(F32)

    plan = iter(PLAN)

    def slot():
        advance(*next(plan))

    slot()

    def widen(chunk_rows):
        grad[chunk_rows, :] = cotangent[chunk_rows, :].astype(F32)

    blocks(rows // 32, 32, widen)

    for b in (1, 0):
        gains, scales = params[b]
        base = 3 if b == 0 else 0
        slot()
        need("mlp")
        branch_grad(grad, buf_p, scales[1:2, :], branch, sum_of(b, 7), sum_of(b, 5))
        fetch_kept(b, "attn", buf_p)
        need("hidden")
        slot()
        reuse(base)
        for r in range(4):
            if r % 2 == 0:
                slot()
            outer(hidden.at[r], branch, grad_w.at[base % 2, r])
        slot()
        across(base)
        if b == 1:
            fetch_kept(0, "hidden", hidden)
        need("normed2")
        slot()
        reuse(base + 1)
        for r in range(4):
            slot()
            need(("pre", r % 2), ("down", r % 2), ("up", r % 2))
            hidden_grad(branch, down_w.at[r % 2], pre.at[r % 2], grad_pre, hidden_sum)
            sums[pl.ds(16 * b + 8 + flip(z, r), 1), :] = hidden_sum[...]
            outer(normed2, grad_pre, grad_w.at[(base + 1) % 2, r])

            part_sum = dot(grad_pre[...], up_w[r % 2], (1, 1))
            if r == 0:
                slope[...] = part_sum
            else:
                slope[...] += part_sum
            if r < 2:
                fetch_mlp(b, r + 2)
            elif b == 1:
                fetch_mlp(0, r - 2)
        slot()
        across(base + 1)
        if b == 1:
            fetch_kept(0, "normed2", normed2)
        slot()
        need("middle", "attn")
        sum_of(b, 6)[...] = jnp.zeros((1, 768), F32)
        sum_of(b, 4)[...] = jnp.zeros((1, 768), F32)

        def after(chunk_rows, value_rows, b=b, scales=scales):
            sums[16 * b + 6 : 16 * b + 7, :] += column_sum(value_rows * buf_p[chunk_rows, :])
            low = (scales[0:1, :] * value_rows).astype(BF)
            branch[chunk_rows, :] = low
            sums[16 * b + 4 : 16 * b + 5, :] += column_sum(low.astype(F32))

        norm_back(buf_q, slope, gains[1:2, :], grad, sum_of(b, 1), sum_of(b, 3), after)
        fetch_kept(b, "resid", buf_q)
        if b == 1:
            fetch_kept(0, "mlp", buf_p)
        slot()
        need("mixed")
        need_attn(0, 1, 2, 3)
        project_rows(branch, attn_w.at[3], None, grad_mixed)
        need("query", "key", "value", "log_total")
        attn_args = (
            query,
            key,
            value,
            key_bias,
            log_total,
            grad_mixed,
            grad_query,
            grad_key,
            grad_value,
        )
        for pair in (0, 2, 4):
            slot()
            attend_pairs_back(pair, pair + 2, *attn_args)
        slot()

        if b == 0:
            for owner, copy in flying:
                if owner < 0:
                    copy.wait_send()
            flying[:] = [(owner, copy) for owner, copy in flying if owner >= 0]
        away[...] = (
            dot(grad_key[rows:, :], attn_w[1]) + dot(grad_value[rows:, :], attn_w[2])
        ).astype(BF)
        slot()
        given = launch(
            [
                remote(
                    away.at[pl.ds(n * rows // EXCHANGE, rows // EXCHANGE)],
                    away_in.at[b, pl.ds(n * rows // EXCHANGE, rows // EXCHANGE)],
                    other.at[0, b * EXCHANGE + n],
                    other.at[1, b * EXCHANGE + n],
                    {"mp": 1},
                )
                for n in range(EXCHANGE)
            ]
        )
        flying.extend((-1, copy) for copy in given)
        slot()
        reuse(base + 2)
        target = grad_w.at[(base + 2) % 2]
        need("normed")
        for kind, left, right in (
            (0, grad_query, normed.at[pl.ds(0, rows)]),
            (1, grad_key, normed),
            (2, grad_value, normed),
            (3, mixed, branch),
        ):
            if kind % 2 == 0:
                slot()
            for h in range(2):
                value_h = dot(left[:, h * 384 : (h + 1) * 384], right[...], (0, 0)).astype(BF)
                for r in range(2):
                    target[2 * h + r, kind * 192 : (kind + 1) * 192, :] = value_h[
                        r * 192 : (r + 1) * 192
                    ]
        slot()
        across(base + 2)
        slot()
        head_sums(b, 0, grad_query, rows)
        head_sums(b, 256, grad_value, 2 * rows)
        slot()

        slope[...] = (
            dot(grad_query[...], attn_w[0])
            + dot(grad_key[0:rows, :], attn_w[1])
            + dot(grad_value[0:rows, :], attn_w[2])
        )
        if b == 1:
            start_attn(0)
            fetch_kept(0, "normed", normed)
            fetch_attn(0)
        slot()
        landed(given)
        slot()

        def join(chunk_rows):
            slope[chunk_rows, :] += away_in[b, chunk_rows, :].astype(F32)

        blocks(rows // 32, 32, join)
        need("resid")
        if b == 1:
            norm_back(buf_q, slope, gains[0:1, :], grad, sum_of(b, 0), sum_of(b, 2))
            fetch_kept(0, "middle", buf_q)
        else:

            def final(chunk_rows, value_rows):
                grad_out[chunk_rows, :] = value_rows.astype(BF)

            norm_back(buf_q, slope, gains[0:1, :], grad, sum_of(b, 0), sum_of(b, 2), final)

        slot()
    slot()
    sums_out[...] = sums[...]
    for own in owns:
        own.wait()
    for _, copy in flying:
        copy.wait_send()
    for j in (COUNT - 2, COUNT - 1):
        for copy in sent[j]:
            copy.wait_send()


LOADS = 40
EXCHANGE = 1
THIRDS = (0, 2, 4)
SUM_STEPS = 7
PLAN = (
    (),
    (),
    (),
    (),
    (),
    (),
    (),
    (),
    (),
    (0,),
    (),
    (),
    (),
    (),
    (),
    (1, 0),
    (),
    (),
    (),
    (),
    (),
    (),
    (0,),
    (1, 0, 2),
    (),
    (),
    (),
    (),
    (6,),
    (),
    (0,),
    (),
    (1,),
    (3,),
    (),
    (6,),
    (2, 1),
    (),
    (1,),
    (),
    (6, 2, 0),
    (),
    (4,),
    (),
    (3, 0),
    (),
    (),
    (),
    (2, 4),
    (2, 1),
    (3, 5, 4),
    (5, 5, 4),
    (3,),
    (4, 2),
    (0, 3, 6, 3, 1),
    (4, 2, 7, 5, 3, 5, 4, 5, 1, 7, 2, 7, 4, 5, 7, 5, 3),
)


def backward_all(locals_, full, kept, cotangent, lengths, params):
    dp_size = lax.axis_size("dp")
    anywhere = pl.BlockSpec(memory_space=pl.ANY)
    vmem = pl.BlockSpec(memory_space=pltpu.VMEM)
    smem = pl.BlockSpec(memory_space=pltpu.SMEM)
    matrix = locals_[2].shape
    size = matrix[0] // PARTS
    rows = cotangent.shape[0]
    more = (dp_size // PARTS).bit_length() - 1
    more_shape = (COUNT, more, 4, size, 768) if more else (16, 128)
    stage_shape = (4, size, 768) if more else (16, 128)
    cut_count, cut_rows = (1, 16) if more else (len(THIRDS), size // 3)
    shape = jax.ShapeDtypeStruct
    steps = SUM_STEPS + more
    flat_kept = [kept[b][name] for b in range(2) for name in KEPT_NAMES]
    scratch = [
        ((2, 4) + matrix, BF),
        ((RING, 2, 2, 4, size, 768), BF),
        ((COUNT, 2, 2, 4, size // 2, 768), BF),
        ((COUNT, 2, 4, size // 2, 768), BF),
        (stage_shape, BF),
        ((COUNT, 3, size, 768), BF),
        ((COUNT, size, 768), BF),
        ((cut_count, 2, 2, 2, cut_rows, 768), BF),
        ((cut_count, 2, 2, cut_rows, 768), BF),
        ((cut_count, 2, cut_rows, 768), BF),
        ((cut_count, cut_rows, 768), BF),
        ((2,) + matrix, BF),
        ((2,) + matrix, BF),
        ((4,) + matrix, BF),
        ((rows, 768), F32),
        ((rows, 768), F32),
        ((rows, 768), F32),
        ((rows, 768), BF),
        ((rows, 768), BF),
        ((4, rows, 768), BF),
        ((2, rows, 768), F32),
        ((rows, 768), BF),
        ((rows, 768), F32),
        ((rows, 768), BF),
        ((2 * rows, 768), BF),
        ((2 * rows, 768), BF),
        ((2 * rows, 768), BF),
        ((rows, 768), BF),
        ((rows, 768), BF),
        ((rows, 768), BF),
        ((2 * rows, 768), BF),
        ((2 * rows, 768), BF),
        ((6, 8, 2 * rows), F32),
        ((rows, 768), BF),
        ((2, rows, 768), BF),
        ((32, 768), F32),
        ((2, steps, 16, 768), F32),
        ((1, 768), F32),
        ((2 * rows, 1), F32),
    ]
    got = pl.pallas_call(
        functools.partial(backward_kernel, dp_size),
        out_shape=[
            shape((COUNT,) + matrix, BF),
            shape(more_shape, BF),
            shape((32, 768), F32),
            shape((rows, 768), BF),
        ],
        in_specs=[anywhere] * (8 + COUNT + 2 * len(KEPT)) + [vmem, smem] + [vmem] * 4,
        out_specs=[anywhere] * 2 + [vmem] * 2,
        scratch_shapes=[pltpu.VMEM(dims, kind) for dims, kind in scratch]
        + [
            pltpu.SemaphoreType.DMA((COUNT, 24 + 2 * more)),
            pltpu.SemaphoreType.DMA((COUNT, 24 + 2 * more)),
            pltpu.SemaphoreType.DMA((LOADS,)),
            pltpu.SemaphoreType.DMA((COUNT,)),
            pltpu.SemaphoreType.REGULAR((1, COUNT)),
            pltpu.SemaphoreType.DMA((2, 2 * EXCHANGE + 2 * steps)),
        ],
        compiler_params=pltpu.CompilerParams(
            collective_id=1, has_side_effects=True, vmem_limit_bytes=63 * 1024 * 1024
        ),
    )(*locals_, *full, *flat_kept, cotangent, lengths, *params)
    return got[0], got[2], got[3]


def finish_kernel(whole, sums, *refs):
    passed, outs, refs = refs[:2], refs[2:24], refs[24:]
    low, high, load, store = refs
    z = lax.axis_index("mp")
    loads = [
        pltpu.make_async_copy(whole.at[j], low.at[j], load.at[j]) for j in range(COUNT)
    ]
    for copy in loads:
        copy.start()
    for source, target in zip(passed, outs[:2]):
        target[...] = source[...]
    stores = []

    def keep(source, target):
        copy = pltpu.make_async_copy(source, target, store.at[len(stores)])
        copy.start()
        stores.append(copy)

    for b in range(2):
        project_in, project_out, up, down = outs[2 + 10 * b : 6 + 10 * b]
        gains, shifts, out_bias, scales, up_bias, project_bias = outs[6 + 10 * b : 12 + 10 * b]
        base = 16 * b
        for row, ref in zip((0, 2, 4, 6), (gains, shifts, out_bias, scales)):
            ref[...] = sums[base + row : base + row + 2, :]
        up_bias[...] = sums[pl.ds(base + 8 + z, 1), :].reshape(768)
        mine = sums[pl.ds(base + 12 + z, 1), :]
        project_bias[0:1, :] = mine[:, 0:192]
        project_bias[1:2, :] = mine[:, 256:448]
    for j in range(COUNT):
        b = 1 if j < 3 else 0
        project_in, project_out, up, down = outs[2 + 10 * b : 6 + 10 * b]
        loads[j].wait()

        def widen(chunk_rows):
            high[j, chunk_rows, :] = low[j, chunk_rows, :].astype(F32)

        blocks(8, 96, widen)
        if j % 3 == 0:
            keep(high.at[j], down)
        elif j % 3 == 1:
            keep(high.at[j], up)
        else:
            keep(high.at[j, pl.ds(0, 576)], project_in)
            keep(high.at[j, pl.ds(576, 192)], project_out)
    for copy in stores:
        copy.wait()


def finish_all(whole, sums, output, grad_input):
    anywhere = pl.BlockSpec(memory_space=pl.ANY)
    vmem = pl.BlockSpec(memory_space=pltpu.VMEM)
    shape = jax.ShapeDtypeStruct
    matrix = whole.shape[1:]
    big = [shape((576, 768), F32), shape((192, 768), F32), shape(matrix, F32), shape(matrix, F32)]
    little = [shape((2, 768), F32)] * 4 + [shape((768,), F32), shape((2, 192), F32)]
    return pl.pallas_call(
        finish_kernel,
        out_shape=[shape(output.shape, BF)] * 2 + (big + little) * 2,
        in_specs=[anywhere] + [vmem] * 3,
        out_specs=[vmem] * 2 + ([anywhere] * 4 + [vmem] * 6) * 2,
        scratch_shapes=[
            pltpu.VMEM((COUNT,) + matrix, BF),
            pltpu.VMEM((COUNT,) + matrix, F32),
            pltpu.SemaphoreType.DMA((COUNT,)),
            pltpu.SemaphoreType.DMA((COUNT + 2,)),
        ],
        compiler_params=pltpu.CompilerParams(vmem_limit_bytes=60 * 1024 * 1024),
    )(whole, sums, output, grad_input)


def local_block(weights):
    p_in, p_out, up, down = weights[2], weights[4], weights[7], weights[9]
    return [p_in.swapaxes(1, 2).reshape(-1, p_in.shape[1]), p_out, up, down]


def arrange(grads):
    project_in, project_out, up, down = grads[:4]
    gains, shifts, out_bias, scales, up_bias, project_bias = grads[4:]
    return (
        gains,
        shifts,
        project_in.reshape(3, 192, 768).swapaxes(1, 2),
        project_bias,
        project_out,
        out_bias,
        scales,
        up,
        up_bias,
        down,
    )


def body(inputs, lengths, cotangent, *params):
    blocks_ = params[:10], params[10:]
    locals_ = local_block(blocks_[0]) + local_block(blocks_[1])
    forward_params = [weights[p] for weights in blocks_ for p in (0, 1, 5, 6, 3, 8)]
    full, kept, output = forward_all(locals_, inputs, lengths, forward_params)
    backward_params = [weights[p] for weights in blocks_ for p in (0, 6)]
    whole, sums, grad_input = backward_all(
        locals_, full, kept, cotangent, lengths, backward_params
    )
    outs = finish_all(whole, sums, output, grad_input)
    return tuple(outs[:2]) + arrange(outs[2:12]) + arrange(outs[12:22])


def solution(mesh):
    rows = P(("dp", "mp"), None)
    weights = (
        P(),
        P(),
        P(None, None, "mp"),
        P(None, "mp"),
        P("mp", None),
        P(),
        P(),
        P(None, "mp"),
        P("mp"),
        P("mp", None),
    )
    in_specs = (rows, P("dp"), rows) + weights + weights
    out_specs = (rows, rows) + weights + weights
    return jax.shard_map(body, mesh=mesh, in_specs=in_specs, out_specs=out_specs, check_vma=False)
```
